32 devices in a mesh: crop: 4 (over y, x), slab: 8 (over z, core).
Axes of the slice: x: 2, y: 2, z: 4, core: 2. Of those that a mesh axis runs over, the one named last changes fastest.
Arguments:
- patches: bfloat16 [8, 8, 64, 16384], P('crop', 'slab'), may hold values from -6 to 6
- modality: int32 [8], P('crop'), may hold values from 0 to 1
- skip_feats: bfloat16 [8, 16, 16, 16, 128], P('crop', 'slab'), may hold values from -7.5 to 7.5
- cotangent: bfloat16 [8, 16, 16, 16, 128], P('crop', 'slab'), may hold values from -7.5 to 7.5
- embedding: float32 [20480, 768], P('slab', 'crop'), may hold values from -0.0625 to 0.0625
- attention_in: float32 [768, 2304], P('slab', 'crop'), may hold values from -0.3125 to 0.3125
- attention_out: float32 [768, 768], P('slab', 'crop'), may hold values from -0.625 to 0.625
- expand_up: float32 [768, 3072], P('slab', 'crop'), may hold values from -0.21875 to 0.21875
- expand_down: float32 [3072, 768], P('slab', 'crop'), may hold values from -0.109375 to 0.109375
- upsample: float32 [768, 1024], P('slab', 'crop'), may hold values from -0.3247595 to 0.3247595
- convolve_one: float32 [6912, 128], P('slab', 'crop'), may hold values from -0.078125 to 0.078125
- convolve_two: float32 [3456, 128], P('slab', 'crop'), may hold values from -0.109375 to 0.109375
- positions: float32 [512, 768], P('slab', 'crop'), may hold values from -0.48 to 0.48
- vectors: float32 [9216], P(('crop', 'slab')), may hold values from -1.5 to 1.5
- embedding_mean: float32 [20480, 768], P('slab', 'crop'), may hold values from -0.00012207031 to 0.00012207031
- attention_in_mean: float32 [768, 2304], P('slab', 'crop'), may hold values from -0.00012207031 to 0.00012207031
- attention_out_mean: float32 [768, 768], P('slab', 'crop'), may hold values from -0.00012207031 to 0.00012207031
- expand_up_mean: float32 [768, 3072], P('slab', 'crop'), may hold values from -0.00012207031 to 0.00012207031
- expand_down_mean: float32 [3072, 768], P('slab', 'crop'), may hold values from -0.00012207031 to 0.00012207031
- upsample_mean: float32 [768, 1024], P('slab', 'crop'), may hold values from -0.00012207031 to 0.00012207031
- convolve_one_mean: float32 [6912, 128], P('slab', 'crop'), may hold values from -0.00012207031 to 0.00012207031
- convolve_two_mean: float32 [3456, 128], P('slab', 'crop'), may hold values from -0.00012207031 to 0.00012207031
- positions_mean: float32 [512, 768], P('slab', 'crop'), may hold values from -7.6293945e-06 to 7.6293945e-06
- vectors_mean: float32 [9216], P(('crop', 'slab')), may hold values from -0.00061035156 to 0.00061035156
- embedding_square: float32 [20480, 768], P('slab', 'crop'), may hold values from 2.0772044e-09 to 8.293021e-09
- attention_in_square: float32 [768, 2304], P('slab', 'crop'), may hold values from 2.0772044e-09 to 8.293021e-09
- attention_out_square: float32 [768, 768], P('slab', 'crop'), may hold values from 2.0772044e-09 to 8.293021e-09
- expand_up_square: float32 [768, 3072], P('slab', 'crop'), may hold values from 2.0772044e-09 to 8.293021e-09
- expand_down_square: float32 [3072, 768], P('slab', 'crop'), may hold values from 2.0772044e-09 to 8.293021e-09
- upsample_square: float32 [768, 1024], P('slab', 'crop'), may hold values from 2.0772044e-09 to 8.293021e-09
- convolve_one_square: float32 [6912, 128], P('slab', 'crop'), may hold values from 2.0772044e-09 to 8.293021e-09
- convolve_two_square: float32 [3456, 128], P('slab', 'crop'), may hold values from 2.0772044e-09 to 8.293021e-09
- positions_square: float32 [512, 768], P('slab', 'crop'), may hold values from 6.864573e-12 to 2.7381162e-11
- vectors_square: float32 [9216], P(('crop', 'slab')), may hold values from 5.2127564e-08 to 2.0772043e-07
Outputs:
- block_output: bfloat16 [8, 16, 16, 16, 128], P('crop', 'slab')
- patch_grad: bfloat16 [8, 8, 64, 16384], P('crop', 'slab')
- skip_grad: bfloat16 [8, 16, 16, 16, 128], P('crop', 'slab')
- grad_norm: float32 [], replicated
- embedding_new: float32 [20480, 768], P('slab', 'crop')
- attention_in_new: float32 [768, 2304], P('slab', 'crop')
- attention_out_new: float32 [768, 768], P('slab', 'crop')
- expand_up_new: float32 [768, 3072], P('slab', 'crop')
- expand_down_new: float32 [3072, 768], P('slab', 'crop')
- upsample_new: float32 [768, 1024], P('slab', 'crop')
- convolve_one_new: float32 [6912, 128], P('slab', 'crop')
- convolve_two_new: float32 [3456, 128], P('slab', 'crop')
- positions_new: float32 [512, 768], P('slab', 'crop')
- vectors_new: float32 [9216], P(('crop', 'slab'))
- embedding_mean_new: float32 [20480, 768], P('slab', 'crop')
- attention_in_mean_new: float32 [768, 2304], P('slab', 'crop')
- attention_out_mean_new: float32 [768, 768], P('slab', 'crop')
- expand_up_mean_new: float32 [768, 3072], P('slab', 'crop')
- expand_down_mean_new: float32 [3072, 768], P('slab', 'crop')
- upsample_mean_new: float32 [768, 1024], P('slab', 'crop')
- convolve_one_mean_new: float32 [6912, 128], P('slab', 'crop')
- convolve_two_mean_new: float32 [3456, 128], P('slab', 'crop')
- positions_mean_new: float32 [512, 768], P('slab', 'crop')
- vectors_mean_new: float32 [9216], P(('crop', 'slab'))
- embedding_square_new: float32 [20480, 768], P('slab', 'crop')
- attention_in_square_new: float32 [768, 2304], P('slab', 'crop')
- attention_out_square_new: float32 [768, 768], P('slab', 'crop')
- expand_up_square_new: float32 [768, 3072], P('slab', 'crop')
- expand_down_square_new: float32 [3072, 768], P('slab', 'crop')
- upsample_square_new: float32 [768, 1024], P('slab', 'crop')
- convolve_one_square_new: float32 [6912, 128], P('slab', 'crop')
- convolve_two_square_new: float32 [3456, 128], P('slab', 'crop')
- positions_square_new: float32 [512, 768], P('slab', 'crop')
- vectors_square_new: float32 [9216], P(('crop', 'slab'))
The draws below stay inside these ranges and needn't reach their ends.
All inputs are finite; a program needn't handle non-finite values.
Results may differ from the reference program's by a relative error of at most 0.022.
Values may be sent and summed in bfloat16 or wider, within the bound.
No kernel may reach another device: no remote copies, remote signals or barrier semaphores. Data moves between devices by JAX's collectives and lax.ppermute only.
A program may use at most 320 MiB of HBM per device.

```python
import math
import jax
import jax.numpy as jnp
from jax import lax

D = 768
HEADS = 12
HDIM = 64
FF = 3072
PATCH = 4096
CHANS = 4
DEC = 128
SIDE = 8
STEP = 10
PLANE = 64
CROPS = 8
DEPTH = 8
LENGTH = 512
NPARAMS = 25322496


def draw_vectors(key, part):
    row_index = jnp.arange(12 * D) // D
    gain_draw = jax.random.uniform(key, (12 * D,), jnp.float32, 0.6, 1.4)
    shift_draw = jnp.clip(0.3 * jax.random.normal(jax.random.fold_in(key, 1), (12 * D,), jnp.float32), -1.5, 1.5)
    is_gain = (row_index == 0) | (row_index == 2)
    return jnp.where(is_gain, gain_draw, shift_draw)


def depth_ramp(levels, start, finish):
    fraction = jnp.arange(levels, dtype=jnp.float32) / max(levels - 1, 1)
    return start * (finish / start) ** fraction


def ramped_volume(noise, ramp, offset_key):
    offset = jax.random.uniform(offset_key, (CROPS, 1, 1, 1, DEC), jnp.float32, -1.0, 1.0)
    return noise + offset * ramp[None, :, None, None, None]


def draw_skip_feats(key, part):
    inner_key = jax.random.fold_in(key, 23)
    shape = (CROPS, 2 * DEPTH, 2 * SIDE, 2 * SIDE, DEC)
    noise = jnp.clip(jax.random.normal(inner_key, shape, jnp.float32), -6.0, 6.0)
    ramp = depth_ramp(2 * DEPTH, 0.5, 1.5)
    return ramped_volume(noise, ramp, jax.random.fold_in(inner_key, 5)).astype(jnp.bfloat16)


def draw_cotangent(key, part):
    inner_key = jax.random.fold_in(key, 11)
    shape = (CROPS, 2 * DEPTH, 2 * SIDE, 2 * SIDE, DEC)
    noise = jnp.clip(jax.random.normal(inner_key, shape, jnp.float32), -6.0, 6.0)
    ramp = depth_ramp(2 * DEPTH, 0.5, 1.5)
    return ramped_volume(noise, ramp, jax.random.fold_in(inner_key, 5)).astype(jnp.bfloat16)


def draw_upsample(key, part):
    inner_key = jax.random.fold_in(key, 37)
    shape = (D, 8 * DEC)
    fraction = jnp.arange(D, dtype=jnp.float32) / (D - 1) - 0.5
    noise = jnp.clip(jax.random.normal(inner_key, shape, jnp.float32), -4.0, 4.0)
    row_scale = 3.0 ** fraction
    return noise * row_scale[:, None] * D ** (-0.5)


def plant(values, own_key, smallest, high):
    extent = values.shape
    index_at = [jax.random.randint(jax.random.fold_in(own_key, axis), (), 0, extent[axis]) for axis in range(len(extent))]
    values = values.at[tuple(index_at)].set(smallest)
    longest = extent.index(max(extent))
    index_at[longest] = (index_at[longest] + 1) % extent[longest]
    return values.at[tuple(index_at)].set(high)


def block_levels(key, shape, split, low, high):
    level, own = 1.0, jax.random.fold_in(key, 6)
    for axis_at, shards_of in split:
        steps = jnp.exp(jax.random.uniform(jax.random.fold_in(own, axis_at), (shards_of,), jnp.float32, low / len(split), high / len(split)))
        level = level * jnp.repeat(steps, shape[axis_at] // shards_of).reshape([-1 if axis == axis_at else 1 for axis in range(len(shape))])
    return level


def bell_draw(rng, dims, scale, reach, split=(), held_as=jnp.bfloat16):
    level = block_levels(rng, dims, split, -0.22, 0.18) if split else 1.0
    array = jax.random.normal(rng, dims, jnp.float32) * scale * level
    return jnp.minimum(jnp.maximum(array, -reach), reach).astype(held_as)


def setup_inputs(seed: int = 0) -> dict:
    seeds = jax.random.split(jax.random.key(seed), 35)
    return {
        "patches": bell_draw(seeds[0], (CROPS, DEPTH, PLANE, CHANS * PATCH), 1.0, 6.0, ((0, 4), (1, 8))),
        "modality": plant(jax.random.randint(seeds[1], (CROPS,), 0, 2), jax.random.fold_in(seeds[1], 1), 0, 1).astype(jnp.int32),
        "skip_feats": draw_skip_feats(jax.random.fold_in(seeds[34], 71), 0),
        "cotangent": draw_cotangent(jax.random.fold_in(seeds[34], 71), 0),
        "embedding": bell_draw(seeds[4], ((CHANS + 1) * PATCH, D), (2 * PATCH) ** -0.5, 0.0625, ((0, 8), (1, 4)), jnp.float32),
        "attention_in": bell_draw(seeds[5], (D, 3 * D), (D // 2) ** -0.5, 0.3125, ((0, 8), (1, 4)), jnp.float32),
        "attention_out": bell_draw(seeds[6], (D, D), (D // 8) ** -0.5, 0.625, ((0, 8), (1, 4)), jnp.float32),
        "expand_up": bell_draw(seeds[7], (D, FF), D ** -0.5, 0.21875, ((0, 8), (1, 4)), jnp.float32),
        "expand_down": bell_draw(seeds[8], (FF, D), FF ** -0.5, 0.109375, ((0, 8), (1, 4)), jnp.float32),
        "upsample": draw_upsample(jax.random.fold_in(seeds[34], 71), 0),
        "convolve_one": bell_draw(seeds[10], (54 * DEC, DEC), (54 * DEC) ** -0.5, 0.078125, ((0, 8), (1, 4)), jnp.float32),
        "convolve_two": bell_draw(seeds[11], (27 * DEC, DEC), (27 * DEC) ** -0.5, 0.109375, ((0, 8), (1, 4)), jnp.float32),
        "positions": bell_draw(seeds[12], (LENGTH, D), 0.08, 0.48, ((0, 8), (1, 4)), jnp.float32),
        "vectors": draw_vectors(jax.random.fold_in(seeds[34], 71), 0),
        "embedding_mean": bell_draw(seeds[14], ((CHANS + 1) * PATCH, D), (0.111 * NPARAMS ** -0.5), 0.00012207031, ((0, 8), (1, 4)), jnp.float32),
        "attention_in_mean": bell_draw(seeds[15], (D, 3 * D), (0.111 * NPARAMS ** -0.5), 0.00012207031, ((0, 8), (1, 4)), jnp.float32),
        "attention_out_mean": bell_draw(seeds[16], (D, D), (0.111 * NPARAMS ** -0.5), 0.00012207031, ((0, 8), (1, 4)), jnp.float32),
        "expand_up_mean": bell_draw(seeds[17], (D, FF), (0.111 * NPARAMS ** -0.5), 0.00012207031, ((0, 8), (1, 4)), jnp.float32),
        "expand_down_mean": bell_draw(seeds[18], (FF, D), (0.111 * NPARAMS ** -0.5), 0.00012207031, ((0, 8), (1, 4)), jnp.float32),
        "upsample_mean": bell_draw(seeds[19], (D, 8 * DEC), (0.111 * NPARAMS ** -0.5), 0.00012207031, ((0, 8), (1, 4)), jnp.float32),
        "convolve_one_mean": bell_draw(seeds[20], (54 * DEC, DEC), (0.111 * NPARAMS ** -0.5), 0.00012207031, ((0, 8), (1, 4)), jnp.float32),
        "convolve_two_mean": bell_draw(seeds[21], (27 * DEC, DEC), (0.111 * NPARAMS ** -0.5), 0.00012207031, ((0, 8), (1, 4)), jnp.float32),
        "positions_mean": bell_draw(seeds[22], (LENGTH, D), (0.144 * (NPARAMS * LENGTH) ** -0.5), 7.62939453125e-06, ((0, 8), (1, 4)), jnp.float32),
        "vectors_mean": bell_draw(seeds[23], (12 * D,), (0.555 * NPARAMS ** -0.5), 0.00061035156, ((0, 32),), jnp.float32),
        "embedding_square": jnp.clip(jnp.exp(math.log(8.293021380723076e-09) - 1.3843914 * jax.random.uniform(seeds[24], ((CHANS + 1) * PATCH, D), jnp.float32) ** block_levels(seeds[24], ((CHANS + 1) * PATCH, D), ((0, 8), (1, 4)), -0.2, 0.2)), 2.0772044084793606e-09, 8.293021380723076e-09),
        "attention_in_square": jnp.clip(jnp.exp(math.log(8.293021380723076e-09) - 1.3843914 * jax.random.uniform(seeds[25], (D, 3 * D), jnp.float32) ** block_levels(seeds[25], (D, 3 * D), ((0, 8), (1, 4)), -0.2, 0.2)), 2.0772044084793606e-09, 8.293021380723076e-09),
        "attention_out_square": jnp.clip(jnp.exp(math.log(8.293021380723076e-09) - 1.3843914 * jax.random.uniform(seeds[26], (D, D), jnp.float32) ** block_levels(seeds[26], (D, D), ((0, 8), (1, 4)), -0.2, 0.2)), 2.0772044084793606e-09, 8.293021380723076e-09),
        "expand_up_square": jnp.clip(jnp.exp(math.log(8.293021380723076e-09) - 1.3843914 * jax.random.uniform(seeds[27], (D, FF), jnp.float32) ** block_levels(seeds[27], (D, FF), ((0, 8), (1, 4)), -0.2, 0.2)), 2.0772044084793606e-09, 8.293021380723076e-09),
        "expand_down_square": jnp.clip(jnp.exp(math.log(8.293021380723076e-09) - 1.3843914 * jax.random.uniform(seeds[28], (FF, D), jnp.float32) ** block_levels(seeds[28], (FF, D), ((0, 8), (1, 4)), -0.2, 0.2)), 2.0772044084793606e-09, 8.293021380723076e-09),
        "upsample_square": jnp.clip(jnp.exp(math.log(8.293021380723076e-09) - 1.3843914 * jax.random.uniform(seeds[29], (D, 8 * DEC), jnp.float32) ** block_levels(seeds[29], (D, 8 * DEC), ((0, 8), (1, 4)), -0.2, 0.2)), 2.0772044084793606e-09, 8.293021380723076e-09),
        "convolve_one_square": jnp.clip(jnp.exp(math.log(8.293021380723076e-09) - 1.3843914 * jax.random.uniform(seeds[30], (54 * DEC, DEC), jnp.float32) ** block_levels(seeds[30], (54 * DEC, DEC), ((0, 8), (1, 4)), -0.2, 0.2)), 2.0772044084793606e-09, 8.293021380723076e-09),
        "convolve_two_square": jnp.clip(jnp.exp(math.log(8.293021380723076e-09) - 1.3843914 * jax.random.uniform(seeds[31], (27 * DEC, DEC), jnp.float32) ** block_levels(seeds[31], (27 * DEC, DEC), ((0, 8), (1, 4)), -0.2, 0.2)), 2.0772044084793606e-09, 8.293021380723076e-09),
        "positions_square": jnp.clip(jnp.exp(math.log(2.738116157419146e-11) - 1.3834814 * jax.random.uniform(seeds[32], (LENGTH, D), jnp.float32) ** block_levels(seeds[32], (LENGTH, D), ((0, 8), (1, 4)), -0.2, 0.2)), 6.864573146025954e-12, 2.738116157419146e-11),
        "vectors_square": jnp.clip(jnp.exp(math.log(2.0772043285433028e-07) - 1.3824992 * jax.random.uniform(seeds[33], (12 * D,), jnp.float32) ** block_levels(seeds[33], (12 * D,), ((0, 32),), -0.2, 0.2)), 5.2127564487136624e-08, 2.0772043285433028e-07),
    }


@jax.custom_vjp
def low(v):
    return lax.optimization_barrier(v.astype(jnp.bfloat16)).astype(jnp.float32)

@jax.custom_vjp
def low_back(v):
    return v

def low_keep(v):
    return (low(v), None)

def low_pass(kept, grad):
    return (grad,)

def back_keep(v):
    return (v, None)

def back_low(kept, grad):
    return (low(grad),)
low.defvjp(low_keep, low_pass)
low_back.defvjp(back_keep, back_low)
HIGH = lax.Precision.HIGHEST
BETA_ONE = 0.9
BETA_TWO = 0.95
RATE = 0.07
DECAY = 0.05
VECTOR_RATE = 0.4
VECTOR_DECAY = 0.0
EPSILON = 1e-08
CLIP = 1.0

def matmul(left, right):
    return jnp.dot(left, right, precision=HIGH)

def layer_norm(values, gain, shift):
    center = values - lax.optimization_barrier(jnp.mean(values, -1, keepdims=True))
    spread = lax.optimization_barrier(jnp.mean(center * center, -1, keepdims=True))
    return center * lax.rsqrt(spread + 1e-06) * gain + shift

def instance_norm(values):
    center = values - lax.optimization_barrier(jnp.mean(values, (0, 1, 2), keepdims=True))
    spread = lax.optimization_barrier(jnp.mean(center * center, (0, 1, 2), keepdims=True))
    return center * lax.rsqrt(spread + 1e-05)

def gelu_exact(values):
    return jax.nn.gelu(values, approximate=False)

def convolve(volume, kernel):
    inputs = volume.shape[-1]
    taps = kernel.reshape(3, 3, 3, inputs, kernel.shape[-1])
    return lax.conv_general_dilated(volume[None], taps, (1, 1, 1), 'SAME', dimension_numbers=('NDHWC', 'DHWIO', 'NDHWC'), precision=HIGH)[0]

def attend(query, keys, values):
    length = query.shape[0]
    block_rows = math.gcd(length, 512)
    blocks = query.reshape(length // block_rows, block_rows, HEADS, HDIM)

    def one_block(block):
        scores = low_back(jnp.einsum('qhd,khd->hqk', block, keys, precision=HIGH) * HDIM ** (-0.5))
        weights = low(jax.nn.softmax(scores, axis=-1))
        return jnp.einsum('hqk,khd->qhd', weights, values, precision=HIGH)
    return lax.map(jax.checkpoint(one_block), blocks).reshape(length, HEADS * HDIM)

def forward(params, pixels, skip_volume, modal_kind):
    embed_w, triple_w, output_w, up_w, down_w, lift_w, first_w, second_w, posit_w, vector_w = [low(entry) for entry in params]
    vector_rows = vector_w.reshape(12, D)
    ct_term = low_back(matmul(pixels[:, :PATCH], embed_w[:PATCH])) + vector_rows[6]
    mri_term = low_back(matmul(pixels, embed_w[PATCH:])) + vector_rows[7]
    hidden = jnp.where(modal_kind == 1, mri_term, ct_term) + posit_w
    normed = low(layer_norm(hidden, vector_rows[0], vector_rows[1]))
    triple = low(low_back(matmul(normed, triple_w)))
    query = triple[:, :D].reshape(-1, HEADS, HDIM)
    keys = triple[:, D:2 * D].reshape(-1, HEADS, HDIM)
    values = triple[:, 2 * D:].reshape(-1, HEADS, HDIM)
    mixed = low(low_back(attend(query, keys, values)))
    hidden = hidden + low_back(matmul(mixed, output_w)) + vector_rows[4]
    normed = low(layer_norm(hidden, vector_rows[2], vector_rows[3]))
    inner = low_back(matmul(normed, up_w)) + vector_rows[8:].reshape(FF)
    activated = low(gelu_exact(inner))
    hidden = hidden + low_back(matmul(activated, down_w)) + vector_rows[5]
    lifted = low_back(matmul(low(hidden), lift_w))
    volume = lifted.reshape(DEPTH, SIDE, SIDE, 2, 2, 2, DEC).transpose(0, 3, 1, 4, 2, 5, 6).reshape(2 * DEPTH, 2 * SIDE, 2 * SIDE, DEC)
    joined = jnp.concatenate([low(volume), skip_volume], -1)
    first_act = low(gelu_exact(instance_norm(low_back(convolve(joined, first_w)))))
    second = instance_norm(low_back(convolve(first_act, second_w)))
    return gelu_exact(second + volume)

def adam_update(weight, gradient, mean_old, square_old, factor, step_rate, step_decay):
    clipped = gradient * factor
    mean_new = BETA_ONE * mean_old + (1.0 - BETA_ONE) * clipped
    square_new = BETA_TWO * square_old + (1.0 - BETA_TWO) * clipped * clipped
    direction = mean_new / (1.0 - BETA_ONE ** STEP) / (jnp.sqrt(square_new / (1.0 - BETA_TWO ** STEP)) + EPSILON)
    return (weight - step_rate * (direction + step_decay * weight), mean_new, square_new)

def reference(patches, modality, skip_feats, cotangent, embedding, attention_in, attention_out, expand_up, expand_down, upsample, convolve_one, convolve_two, positions, vectors, embedding_mean, attention_in_mean, attention_out_mean, expand_up_mean, expand_down_mean, upsample_mean, convolve_one_mean, convolve_two_mean, positions_mean, vectors_mean, embedding_square, attention_in_square, attention_out_square, expand_up_square, expand_down_square, upsample_square, convolve_one_square, convolve_two_square, positions_square, vectors_square):
    params = (embedding, attention_in, attention_out, expand_up, expand_down, upsample, convolve_one, convolve_two, positions, vectors)
    means_in = (embedding_mean, attention_in_mean, attention_out_mean, expand_up_mean, expand_down_mean, upsample_mean, convolve_one_mean, convolve_two_mean, positions_mean, vectors_mean)
    squares_in = (embedding_square, attention_in_square, attention_out_square, expand_up_square, expand_down_square, upsample_square, convolve_one_square, convolve_two_square, positions_square, vectors_square)
    step_rates = (RATE,) * 9 + (VECTOR_RATE,)
    step_decays = (DECAY,) * 9 + (VECTOR_DECAY,)

    def one_crop(running, crop_index):
        pixels = patches[crop_index].reshape(LENGTH, CHANS * PATCH).astype(jnp.float32)
        skip_volume = skip_feats[crop_index].astype(jnp.float32)
        modal_kind = modality[crop_index]

        def local(weights, pixel_rows, skip_rows):
            return forward(weights, pixel_rows, skip_rows, modal_kind)
        output, pull = jax.vjp(local, params, pixels, skip_volume)
        grads, pixel_grad, skip_back = pull(cotangent[crop_index].astype(jnp.float32))
        running = jax.tree.map(jnp.add, running, grads)
        return (running, (output.astype(jnp.bfloat16), pixel_grad.reshape(DEPTH, PLANE, CHANS * PATCH).astype(jnp.bfloat16), skip_back.astype(jnp.bfloat16)))
    zeros = tuple((jnp.zeros(entry.shape, jnp.float32) for entry in params))
    totals, (outputs, patch_grads, skip_grads) = lax.scan(one_crop, zeros, jnp.arange(CROPS))
    squared = jnp.float32(0.0)
    for gradient in totals:
        squared = squared + jnp.sum(gradient * gradient)
    grad_norm = jnp.sqrt(squared)
    factor = jnp.minimum(1.0, CLIP / grad_norm)
    news, means, squares = ([], [], [])
    for weight, gradient, mean_old, square_old, step_rate, step_decay in zip(params, totals, means_in, squares_in, step_rates, step_decays):
        weight_new, mean_new, square_new = adam_update(weight, gradient, mean_old, square_old, factor, step_rate, step_decay)
        news.append(weight_new)
        means.append(mean_new)
        squares.append(square_new)
    return (outputs, patch_grads, skip_grads, grad_norm, news[0], news[1], news[2], news[3], news[4], news[5], news[6], news[7], news[8], news[9], means[0], means[1], means[2], means[3], means[4], means[5], means[6], means[7], means[8], means[9], squares[0], squares[1], squares[2], squares[3], squares[4], squares[5], squares[6], squares[7], squares[8], squares[9])
```

```python
import math

import jax
import jax.numpy as jnp
from jax import lax
from jax.sharding import Mesh
from jax.sharding import PartitionSpec as P

D = 768
HEADS = 12
HDIM = 64
FF = 3072
PATCH = 4096
CHANS = 4
DEC = 128
SIDE = 8
STEP = 10


BETA_ONE = 0.9
BETA_TWO = 0.95
RATE = 0.07
DECAY = 0.05
VECTOR_RATE = 0.4
VECTOR_DECAY = 0.0
EPSILON = 1e-08
CLIP = 1.0
CONTRACT_ROWS = (((0,), (0,)), ((), ()))
CONTRACT_COLS = (((1,), (1,)), ((), ()))


def layer_norm(values, gain, shift):
    center = values - jnp.mean(values, -1, keepdims=True)
    spread = jnp.mean(center * center, -1, keepdims=True)
    return center * lax.rsqrt(spread + 1e-06) * gain + shift


def gelu_exact(values):
    return jax.nn.gelu(values, approximate=False)


def gelu_slope(values):
    return (
        0.5 * (1.0 + lax.erf(values * 0.7071067811865476))
        + values * jnp.exp(-0.5 * values * values) * 0.3989422804014327
    )


def matmul(left, right):
    return jnp.dot(left, right, preferred_element_type=jnp.float32)


def matmul_left_t(left, right):
    return lax.dot_general(left, right, CONTRACT_ROWS, preferred_element_type=jnp.float32)


def matmul_right_t(left, right):
    return lax.dot_general(left, right, CONTRACT_COLS, preferred_element_type=jnp.float32)


SLAB = ("z", "core")
SWAP = [(0, 1), (1, 0)]


def flip_pairs(count, step):
    return [(i, i ^ step) for i in range(count)]


def slab_sum(values):
    values = values + lax.ppermute(values, "core", SWAP)
    count, step = lax.axis_size("z"), 1
    while step < count:
        values = values + lax.ppermute(values, "z", flip_pairs(count, step))
        step *= 2
    return values


def crop_sum(values):
    count, step = lax.axis_size("crop"), 1
    while step < count:
        values = values + lax.ppermute(values, "crop", flip_pairs(count, step))
        step *= 2
    return values


def crop_swap(pieces):
    return lax.all_to_all(pieces, "crop", 0, 0, tiled=True)


def crop_stack(block):
    count = lax.axis_size("crop")
    own = lax.axis_index("crop")
    if count != 4:
        return lax.all_gather(block, "crop", axis=0)
    half = block.shape[0] // 2
    upper, lower = block[:half], block[half:]
    upper_x = lax.ppermute(upper, "crop", flip_pairs(4, 1))
    lower_y = lax.ppermute(lower, "crop", flip_pairs(4, 2))
    upper_y = lax.ppermute(jnp.stack([upper, upper_x]), "crop", flip_pairs(4, 2))
    lower_x = lax.ppermute(jnp.stack([lower, lower_y]), "crop", flip_pairs(4, 1))
    upper_parts = [upper, upper_x, upper_y[0], upper_y[1]]
    lower_parts = [lower, lower_x[0], lower_y, lower_x[1]]
    whole = jnp.zeros((4,) + block.shape, block.dtype)
    zeros = (0,) * (block.ndim - 1)
    for shift in range(4):
        place = own ^ shift
        whole = lax.dynamic_update_slice(whole, upper_parts[shift][None], (place, 0) + zeros)
        whole = lax.dynamic_update_slice(whole, lower_parts[shift][None], (place, half) + zeros)
    return whole


def gather_pack(pack):
    own = crop_stack(lax.all_gather(pack, "z", axis=0))
    other = lax.ppermute(own, "core", SWAP)
    first = lax.axis_index("core") == 0
    return (jnp.where(first, own, other), jnp.where(first, other, own))


def pick(pair, start, rows, chunks):
    both = jnp.stack([part[:, :, start : start + rows * chunks] for part in pair])
    _, crops, layers, _, width = both.shape
    shaped = both.reshape(2, crops, layers, chunks, rows, width)
    return shaped.transpose(2, 0, 1, 4, 3, 5).reshape(-1, chunks * width)


def to_pack(full, chunks):
    crops, layers = lax.axis_size("crop"), lax.axis_size("z")
    width = full.shape[1] // chunks
    shaped = full.reshape(layers, 2, crops, -1, chunks, width)
    return shaped.transpose(0, 1, 2, 4, 3, 5).reshape(layers, 2, crops, -1, width)


def halve(block, axis, index, dim):
    keep = lax.dynamic_index_in_dim(block, index, dim, keepdims=False)
    send = lax.dynamic_index_in_dim(block, 1 - index, dim, keepdims=False)
    got = lax.ppermute(send, axis[0], axis[1])
    return (keep.astype(jnp.float32) + got.astype(jnp.float32)).astype(jnp.bfloat16)


def scatter_pack(pack):
    core = lax.axis_index("core")
    crops = lax.axis_size("crop")
    pack = halve(pack, ("core", SWAP), core, 1)
    if crops != 4:
        pack = lax.psum_scatter(pack, "crop", scatter_dimension=1, tiled=False)
    else:
        own = lax.axis_index("crop")
        side_y, side_x = own // 2, own % 2
        along_y, along_x = ("crop", flip_pairs(4, 2)), ("crop", flip_pairs(4, 1))
        layers, _, rows, width = pack.shape
        half = rows // 2
        upper = pack[:, :, :half].reshape(layers, 2, 2, half, width)
        lower = pack[:, :, half:].reshape(layers, 2, 2, rows - half, width)
        upper = halve(halve(upper, along_y, side_y, 1), along_x, side_x, 1)
        lower = halve(halve(lower, along_x, side_x, 2), along_y, side_y, 1)
        pack = jnp.concatenate([upper, lower], 1)
    return lax.psum_scatter(pack, "z", scatter_dimension=0, tiled=False)


def with_rims(volume):
    layers, cores = lax.axis_size("z"), lax.axis_size("core")
    count = layers * cores
    forward = [(i, i + 1) for i in range(count - 1)]
    backward = [(target, source) for source, target in forward]
    low = lax.ppermute(volume[:, -1:], SLAB, forward)
    high = lax.ppermute(volume[:, :1], SLAB, backward)
    rimmed = jnp.concatenate([low, volume, high], axis=1)
    return jnp.pad(rimmed, ((0, 0), (0, 0), (1, 1), (1, 1), (0, 0)))


def columns(volume):
    padded = with_rims(volume)
    crop_count, layers, breadth = (volume.shape[0], volume.shape[1], volume.shape[2])
    pieces = [
        padded[
            :,
            shift_z : shift_z + layers,
            shift_y : shift_y + breadth,
            shift_x : shift_x + breadth,
            :,
        ]
        for shift_z in range(3)
        for shift_y in range(3)
        for shift_x in range(3)
    ]
    return jnp.concatenate(pieces, -1).reshape(crop_count * layers * breadth * breadth, -1)


def back_conv(grad_out, kernel, inputs):
    outputs = kernel.shape[1]
    flipped = (
        kernel.reshape(27, inputs, outputs)[::-1].transpose(0, 2, 1).reshape(27 * outputs, inputs)
    )
    return matmul(columns(grad_out), flipped).reshape(grad_out.shape[:-1] + (inputs,))


def slab_totals(first, second):
    both = jnp.stack([jnp.sum(first, (1, 2, 3)), jnp.sum(second, (1, 2, 3))])
    return slab_sum(both)


def norm_forward(values, voxel_count):
    totals = slab_totals(values, values * values)
    average = totals[0] / voxel_count
    inverse = lax.rsqrt(totals[1] / voxel_count - average * average + 1e-05)
    return ((values - average[:, None, None, None, :]) * inverse[:, None, None, None, :], inverse)


def norm_backward(grad, normed, inverse, voxel_count):
    totals = slab_totals(grad, grad * normed)
    first_mean = totals[0][:, None, None, None, :] / voxel_count
    second_mean = totals[1][:, None, None, None, :] / voxel_count
    return inverse[:, None, None, None, :] * (grad - first_mean - normed * second_mean)


def heads_out(block, parts):
    crop_count, tokens = block.shape[0], block.shape[1]
    slab_count = lax.axis_size(SLAB)
    shaped = block.reshape(crop_count, tokens, parts, HEADS, HDIM).transpose(0, 3, 1, 2, 4)
    shaped = shaped.reshape(crop_count * HEADS, tokens, parts * HDIM)
    spare = -shaped.shape[0] % slab_count
    shaped = jnp.pad(shaped, ((0, spare), (0, 0), (0, 0)))
    return lax.all_to_all(shaped, SLAB, 0, 1, tiled=True)


def heads_back(block, crop_count, parts):
    shaped = lax.all_to_all(block, SLAB, 1, 0, tiled=True)[: crop_count * HEADS]
    tokens = shaped.shape[1]
    shaped = shaped.reshape(crop_count, HEADS, tokens, parts, HDIM).transpose(0, 2, 3, 1, 4)
    return shaped.reshape(crop_count * tokens, parts * D)


def to_volume(lifted, crop_count):
    layers = lifted.shape[0] // (crop_count * SIDE * SIDE)
    shaped = lifted.reshape(crop_count, layers, SIDE, SIDE, 2, 2, 2, DEC)
    return shaped.transpose(0, 1, 4, 2, 5, 3, 6, 7).reshape(
        crop_count, 2 * layers, 2 * SIDE, 2 * SIDE, DEC
    )


def to_tokens(volume):
    crop_count, layers = (volume.shape[0], volume.shape[1] // 2)
    shaped = volume.reshape(crop_count, layers, 2, SIDE, 2, SIDE, 2, DEC)
    return shaped.transpose(0, 1, 3, 5, 2, 4, 6, 7).reshape(
        crop_count * layers * SIDE * SIDE, 8 * DEC
    )


def adam_update(weight, gradient, mean_old, square_old, factor, step_rate, step_decay):
    clipped = gradient * factor
    mean_new = BETA_ONE * mean_old + (1.0 - BETA_ONE) * clipped
    square_new = BETA_TWO * square_old + (1.0 - BETA_TWO) * clipped * clipped
    direction = (
        mean_new
        / (1.0 - BETA_ONE**STEP)
        / (jnp.sqrt(square_new / (1.0 - BETA_TWO**STEP)) + EPSILON)
    )
    return (weight - step_rate * (direction + step_decay * weight), mean_new, square_new)


def local(
    patches,
    modality,
    skip_feats,
    cotangent,
    embedding,
    attention_in,
    attention_out,
    expand_up,
    expand_down,
    upsample,
    convolve_one,
    convolve_two,
    positions,
    vectors,
    embedding_mean,
    attention_in_mean,
    attention_out_mean,
    expand_up_mean,
    expand_down_mean,
    upsample_mean,
    convolve_one_mean,
    convolve_two_mean,
    positions_mean,
    vectors_mean,
    embedding_square,
    attention_in_square,
    attention_out_square,
    expand_up_square,
    expand_down_square,
    upsample_square,
    convolve_one_square,
    convolve_two_square,
    positions_square,
    vectors_square,
):
    shards = (
        embedding,
        attention_in,
        attention_out,
        expand_up,
        expand_down,
        upsample,
        convolve_one,
        convolve_two,
        positions,
        vectors,
    )
    means_in = (
        embedding_mean,
        attention_in_mean,
        attention_out_mean,
        expand_up_mean,
        expand_down_mean,
        upsample_mean,
        convolve_one_mean,
        convolve_two_mean,
        positions_mean,
        vectors_mean,
    )
    squares_in = (
        embedding_square,
        attention_in_square,
        attention_out_square,
        expand_up_square,
        expand_down_square,
        upsample_square,
        convolve_one_square,
        convolve_two_square,
        positions_square,
        vectors_square,
    )
    step_rates = (RATE,) * 9 + (VECTOR_RATE,)
    step_decays = (DECAY,) * 9 + (VECTOR_DECAY,)
    crops = lax.axis_size("crop")
    layers = lax.axis_size("z")
    slab_count = 2 * layers
    crop_batch = patches.shape[0]
    local_tokens = patches.shape[1] * patches.shape[2]
    rows_in = crop_batch * local_tokens
    voxel_count = skip_feats.shape[1] * skip_feats.shape[2] * skip_feats.shape[3] * slab_count
    score_scale = HDIM ** (-0.5)
    unit = D // crops

    lows = [entry.astype(jnp.bfloat16) for entry in shards]
    embed_rows = embedding.shape[0]
    share = embed_rows // crops
    block = math.gcd(share, PATCH)
    groups = share // block
    row_count = attention_in.shape[0] // crops
    down_count = expand_down.shape[0] // crops
    wide = jnp.concatenate(
        [
            lows[0].reshape(groups, crops, block, unit).transpose(1, 0, 2, 3).reshape(crops, share, unit),
            lows[1].reshape(crops, row_count, 3, unit).transpose(0, 2, 1, 3).reshape(crops, -1, unit),
            lows[2].reshape(crops, row_count, unit),
            lows[3].reshape(crops, row_count, 4, unit).transpose(0, 2, 1, 3).reshape(crops, -1, unit),
            lows[4].reshape(crops, down_count, unit),
            jnp.broadcast_to(lows[8][None], (crops,) + lows[8].shape),
        ],
        1,
    )
    first_count = -(-convolve_one.shape[0] // crops)
    second_count = -(-convolve_two.shape[0] // crops)
    narrow = jnp.concatenate(
        [
            jnp.pad(lows[6], ((0, crops * first_count - lows[6].shape[0]), (0, 0))).reshape(
                crops, first_count, -1
            ),
            jnp.pad(lows[7], ((0, crops * second_count - lows[7].shape[0]), (0, 0))).reshape(
                crops, second_count, -1
            ),
        ],
        1,
    )
    wide = crop_swap(wide)
    lift_rows = crop_swap(lows[5].reshape(crops, row_count, -1))
    narrow = crop_swap(narrow)
    marks = []
    edge = 0
    for size in (share, 3 * row_count, row_count, 4 * row_count, down_count, lows[8].shape[0]):
        marks.append(wide[:, edge : edge + size])
        edge += size
    embed_part = marks[0].transpose(1, 0, 2).reshape(share, D)
    triple_part = marks[1].reshape(3, crops, row_count, unit).transpose(0, 2, 1, 3).reshape(-1, D)
    output_part = marks[2].transpose(1, 0, 2).reshape(row_count, D)
    up_part = marks[3].reshape(4, crops, row_count, unit).transpose(0, 2, 1, 3).reshape(-1, D)
    down_part = marks[4].transpose(1, 0, 2).reshape(down_count, D)
    position_rows = marks[5].transpose(1, 0, 2).reshape(-1, D).astype(jnp.float32)
    lift_part = (
        lift_rows.transpose(1, 0, 2).reshape(row_count, 8, DEC).transpose(1, 0, 2).reshape(-1, DEC)
    )
    narrow_part = narrow.transpose(1, 0, 2).reshape(-1, DEC)
    slim = jnp.concatenate([lift_part, narrow_part], 0)
    slim_rows = -(-slim.shape[0] // 48) * 8
    slim = jnp.pad(slim, ((0, 6 * slim_rows - slim.shape[0]), (0, 0)))
    slim = slim.reshape(6, slim_rows, DEC).transpose(1, 0, 2).reshape(slim_rows, D)
    vector_size = vectors.shape[0]
    vector_part = jnp.pad(lows[9][None], ((0, 7), (0, D - vector_size)))

    embed_full = lax.all_gather(embed_part, SLAB, axis=0, tiled=True)
    pair_one = gather_pack(jnp.concatenate([triple_part, output_part, vector_part], 0))
    pair_two = gather_pack(jnp.concatenate([up_part, down_part, slim], 0))
    triple_full = pick(pair_one, 0, row_count, 3)
    output_full = pick(pair_one, 3 * row_count, row_count, 1)
    vector_full = jnp.stack([part[:, :, 4 * row_count, :vector_size] for part in pair_one])
    vector_full = vector_full.transpose(1, 2, 0, 3).reshape(12 * D)
    up_full = pick(pair_two, 0, row_count, 4)
    down_full = pick(pair_two, 4 * row_count, down_count, 1)
    slim_start = 4 * row_count + down_count
    slim_pair = [
        part[:, :, slim_start:]
        .reshape(crops, layers, slim_rows, 6, DEC)
        .transpose(0, 1, 3, 2, 4)
        .reshape(crops, layers, 6 * slim_rows, DEC)
        for part in pair_two
    ]
    lift_full = pick(slim_pair, 0, row_count, 8)
    first_start = 8 * row_count
    second_start = first_start + first_count
    first_full = (
        pick(slim_pair, first_start, first_count, 1)
        .reshape(slab_count, -1, DEC)[:, : convolve_one.shape[0]]
        .reshape(-1, DEC)
    )
    second_full = (
        pick(slim_pair, second_start, second_count, 1)
        .reshape(slab_count, -1, DEC)[:, : convolve_two.shape[0]]
        .reshape(-1, DEC)
    )
    vector_rows = vector_full.astype(jnp.float32).reshape(12, D)

    pieces = (CHANS * PATCH) // (block * crops)
    ct_size = PATCH // crops
    pixels = patches.reshape(rows_in, pieces, crops, block).transpose(2, 0, 1, 3)
    pixels = crop_swap(pixels.reshape(crops * rows_in, pieces * block))
    kinds_own = jnp.broadcast_to(modality.astype(jnp.float32)[:, None], (crop_batch, 128))
    kinds_all = jnp.concatenate([kinds_own[None]] * crops, 0)
    kinds_all = crop_swap(kinds_all).reshape(crops * crop_batch, 128)[:, :1]
    is_mri = (
        jnp.broadcast_to(kinds_all[:, :, None] > 0.5, (crops * crop_batch, local_tokens, 1))
        .reshape(-1, 1)
    )
    none = jnp.zeros((), jnp.bfloat16)
    pixel_rows = jnp.concatenate(
        [jnp.where(is_mri, none, pixels[:, :ct_size]), jnp.where(is_mri, pixels, none)], 1
    )
    partial = matmul(pixel_rows, embed_full).astype(jnp.bfloat16)
    partial = crop_swap(partial.reshape(crops, rows_in, D)).astype(jnp.float32)
    product = jnp.sum(partial, 0)
    own_mri = jnp.broadcast_to(
        (modality == 1)[:, None, None], (crop_batch, local_tokens, 1)
    ).reshape(-1, 1)
    embedded = (
        product
        + jnp.where(own_mri, vector_rows[7], vector_rows[6])
        + jnp.concatenate([position_rows] * crop_batch, 0)
    )
    normed_one, pull_one = jax.vjp(layer_norm, embedded, vector_rows[0], vector_rows[1])
    normed_one = normed_one.astype(jnp.bfloat16)
    triple = matmul(normed_one, triple_full).astype(jnp.bfloat16)
    triple = heads_out(triple.reshape(crop_batch, local_tokens, 3 * D), 3)
    query, keys, values = triple[..., :HDIM], triple[..., HDIM : 2 * HDIM], triple[..., 2 * HDIM :]
    scores = (
        jnp.einsum("pqd,pkd->pqk", query, keys, preferred_element_type=jnp.float32) * score_scale
    )
    probs = jax.nn.softmax(scores, axis=-1)
    probs_low = probs.astype(jnp.bfloat16)
    mixed = jnp.einsum("pqk,pkd->pqd", probs_low, values, preferred_element_type=jnp.float32)
    mixed = heads_back(mixed.astype(jnp.bfloat16), crop_batch, 1)
    hidden_one = embedded + matmul(mixed, output_full) + vector_rows[4]
    normed_two, pull_two = jax.vjp(layer_norm, hidden_one, vector_rows[2], vector_rows[3])
    normed_two = normed_two.astype(jnp.bfloat16)
    inner = matmul(normed_two, up_full) + vector_rows[8:].reshape(FF)
    activated = gelu_exact(inner).astype(jnp.bfloat16)
    hidden_two = hidden_one + matmul(activated, down_full) + vector_rows[5]
    hidden_low = hidden_two.astype(jnp.bfloat16)
    volume = to_volume(matmul(hidden_low, lift_full), crop_batch)
    joined = jnp.concatenate([volume.astype(jnp.bfloat16), skip_feats], -1)
    cols_one = columns(joined)
    conv_one = matmul(cols_one, first_full).reshape(volume.shape)
    normed_a, inverse_a = norm_forward(conv_one, voxel_count)
    first_act = gelu_exact(normed_a).astype(jnp.bfloat16)
    cols_two = columns(first_act)
    conv_two = matmul(cols_two, second_full).reshape(volume.shape)
    normed_b, inverse_b = norm_forward(conv_two, voxel_count)
    before = normed_b + volume
    block_output = gelu_exact(before).astype(jnp.bfloat16)

    grad_before = cotangent.astype(jnp.float32) * gelu_slope(before)
    grad_conv_two = norm_backward(grad_before, normed_b, inverse_b, voxel_count).astype(
        jnp.bfloat16
    )
    weight_second = matmul_left_t(cols_two, grad_conv_two.reshape(-1, DEC))
    grad_first = back_conv(grad_conv_two, second_full, DEC) * gelu_slope(normed_a)
    grad_conv_one = norm_backward(grad_first, normed_a, inverse_a, voxel_count).astype(
        jnp.bfloat16
    )
    weight_first = matmul_left_t(cols_one, grad_conv_one.reshape(-1, DEC))
    grad_joined = back_conv(grad_conv_one, first_full, 2 * DEC)
    skip_grad = grad_joined[..., DEC:].astype(jnp.bfloat16)
    grad_lifted = to_tokens(grad_before + grad_joined[..., :DEC]).astype(jnp.bfloat16)
    weight_lift = matmul_left_t(hidden_low, grad_lifted)
    grad_hidden = matmul_right_t(grad_lifted, lift_full)
    bias_down = jnp.sum(grad_hidden, 0)
    grad_branch = grad_hidden.astype(jnp.bfloat16)
    weight_down = matmul_left_t(activated, grad_branch)
    grad_inner = matmul_right_t(grad_branch, down_full) * gelu_slope(inner)
    bias_up = jnp.sum(grad_inner, 0)
    grad_inner_low = grad_inner.astype(jnp.bfloat16)
    weight_up = matmul_left_t(normed_two, grad_inner_low)

    def slab_pad(full, target):
        shaped = full.reshape(slab_count, -1, full.shape[1])
        return jnp.pad(shaped, ((0, 0), (0, target - shaped.shape[1]), (0, 0))).reshape(
            -1, full.shape[1]
        )

    slim_pack = jnp.concatenate(
        [
            to_pack(weight_lift.astype(jnp.bfloat16), 8),
            to_pack(slab_pad(weight_first.astype(jnp.bfloat16), crops * first_count), 1),
            to_pack(slab_pad(weight_second.astype(jnp.bfloat16), crops * second_count), 1),
        ],
        3,
    )
    slim_pack = jnp.pad(
        slim_pack, ((0, 0),) * 3 + ((0, 6 * slim_rows - slim_pack.shape[3]), (0, 0))
    )
    slim_pack = (
        slim_pack.reshape(layers, 2, crops, 6, slim_rows, DEC)
        .transpose(0, 1, 2, 4, 3, 5)
        .reshape(layers, 2, crops, slim_rows, D)
    )
    sum_two = scatter_pack(
        jnp.concatenate(
            [
                to_pack(weight_up.astype(jnp.bfloat16), 4),
                to_pack(weight_down.astype(jnp.bfloat16), 1),
                slim_pack,
            ],
            3,
        )
    )

    back_two = pull_two(matmul_right_t(grad_inner_low, up_full))
    grad_hidden = grad_hidden + back_two[0]
    bias_out = jnp.sum(grad_hidden, 0)
    grad_branch = grad_hidden.astype(jnp.bfloat16)
    weight_out = matmul_left_t(mixed, grad_branch)
    grad_mixed = matmul_right_t(grad_branch, output_full).astype(jnp.bfloat16)
    grad_mixed = heads_out(grad_mixed.reshape(crop_batch, local_tokens, D), 1)
    grad_probs = jnp.einsum(
        "pqd,pkd->pqk", grad_mixed, values, preferred_element_type=jnp.float32
    )
    centre = jnp.sum(probs * grad_probs, -1, keepdims=True)
    grad_scores = (probs * (grad_probs - centre)).astype(jnp.bfloat16)
    grad_query = (
        jnp.einsum("pqk,pkd->pqd", grad_scores, keys, preferred_element_type=jnp.float32)
        * score_scale
    )
    grad_keys = (
        jnp.einsum("pqk,pqd->pkd", grad_scores, query, preferred_element_type=jnp.float32)
        * score_scale
    )
    grad_values = jnp.einsum(
        "pqk,pqd->pkd", probs_low, grad_mixed, preferred_element_type=jnp.float32
    )
    grad_triple = jnp.concatenate([grad_query, grad_keys, grad_values], -1).astype(jnp.bfloat16)
    grad_triple = heads_back(grad_triple, crop_batch, 3)
    weight_triple = matmul_left_t(normed_one, grad_triple)
    back_one = pull_one(matmul_right_t(grad_triple, triple_full))
    grad_hidden = grad_hidden + back_one[0]
    grad_low = grad_hidden.astype(jnp.bfloat16)

    grad_rows = crop_stack(grad_low).reshape(crops * rows_in, D)
    weight_embed = matmul_left_t(pixel_rows, grad_rows).astype(jnp.bfloat16)
    embed_sum = lax.psum_scatter(weight_embed, SLAB, scatter_dimension=0, tiled=True)
    pixel_grad = matmul_right_t(grad_rows, embed_full)
    ct_grad = jnp.pad(pixel_grad[:, :ct_size], ((0, 0), (0, (CHANS - 1) * ct_size)))
    pixel_grad = jnp.where(is_mri, pixel_grad[:, ct_size:], ct_grad).astype(jnp.bfloat16)
    pixel_grad = crop_swap(pixel_grad).reshape(crops, rows_in, pieces, block)
    patch_grad = pixel_grad.transpose(1, 2, 0, 3).reshape(patches.shape)

    bias_ct = jnp.sum(jnp.where(own_mri, 0.0, grad_hidden), 0)
    bias_mri = jnp.sum(jnp.where(own_mri, grad_hidden, 0.0), 0)
    position_grad = jnp.sum(grad_hidden.reshape(crop_batch, local_tokens, D), 0)
    vector_grad = jnp.concatenate(
        [
            jnp.stack(
                [
                    back_one[1],
                    back_one[2],
                    back_two[1],
                    back_two[2],
                    bias_out,
                    bias_down,
                    bias_ct,
                    bias_mri,
                ]
            ),
            bias_up.reshape(4, D),
        ],
        0,
    ).astype(jnp.bfloat16)
    vector_pack = vector_grad.reshape(crops, layers, 2, 1, vector_size).transpose(1, 2, 0, 3, 4)
    vector_pack = jnp.pad(vector_pack, ((0, 0),) * 3 + ((0, 7), (0, D - vector_size)))
    sum_one = scatter_pack(
        jnp.concatenate(
            [
                to_pack(weight_triple.astype(jnp.bfloat16), 3),
                to_pack(weight_out.astype(jnp.bfloat16), 1),
                vector_pack,
            ],
            3,
        )
    )

    def by_units(rows, chunks):
        shaped = rows.reshape(chunks, -1, crops, unit).transpose(0, 2, 1, 3)
        return shaped.reshape(crops, -1, unit)

    def join_units(got, chunks):
        return (
            got.reshape(crops, chunks, -1, unit).transpose(0, 2, 1, 3).reshape(-1, chunks * unit)
        )

    embed_got = crop_swap(by_units(embed_sum, 1)).astype(jnp.float32)
    embed_grad = (
        embed_got.reshape(crops, groups, block, unit).transpose(1, 0, 2, 3).reshape(-1, unit)
    )
    wide_two = jnp.concatenate(
        [by_units(sum_two[: 4 * row_count], 4), by_units(sum_two[4 * row_count : slim_start], 1)], 1
    )
    wide_two = crop_swap(wide_two).astype(jnp.float32)
    up_grad = join_units(wide_two[:, : 4 * row_count], 4)
    down_grad = join_units(wide_two[:, 4 * row_count :], 1)
    slim_sum = (
        sum_two[slim_start:].reshape(slim_rows, 6, DEC).transpose(1, 0, 2).reshape(-1, DEC)
    )
    lift_sum = slim_sum[:first_start].reshape(8, row_count, DEC).transpose(1, 0, 2)
    lift_sum = lift_sum.reshape(row_count, crops, -1).transpose(1, 0, 2)
    lift_grad = crop_swap(lift_sum).astype(jnp.float32).reshape(upsample.shape)
    narrow_sum = slim_sum[first_start : second_start + second_count]
    narrow_sum = narrow_sum.reshape(-1, crops, DEC // crops).transpose(1, 0, 2)
    narrow_got = crop_swap(narrow_sum).astype(jnp.float32)
    first_grad = narrow_got[:, :first_count].reshape(-1, DEC // crops)[: convolve_one.shape[0]]
    second_grad = narrow_got[:, first_count:].reshape(-1, DEC // crops)[: convolve_two.shape[0]]
    wide_one = jnp.concatenate(
        [
            by_units(sum_one[: 3 * row_count], 3),
            by_units(sum_one[3 * row_count : 4 * row_count], 1),
            by_units(position_grad.astype(jnp.bfloat16), 1),
        ],
        1,
    )
    wide_one = crop_swap(wide_one).astype(jnp.float32)
    triple_grad = join_units(wide_one[:, : 3 * row_count], 3)
    output_grad = join_units(wide_one[:, 3 * row_count : 4 * row_count], 1)
    position_grad = jnp.sum(wide_one[:, 4 * row_count :], 0)
    vector_final = sum_one[4 * row_count, :vector_size].astype(jnp.float32)
    gradients = (
        embed_grad,
        triple_grad,
        output_grad,
        up_grad,
        down_grad,
        lift_grad,
        first_grad,
        second_grad,
        position_grad,
        vector_final,
    )
    local_sum = jnp.float32(0.0)
    for gradient in gradients:
        local_sum = local_sum + jnp.sum(gradient * gradient)
    grad_norm = jnp.sqrt(crop_sum(slab_sum(local_sum.reshape(1, 1))))[0, 0]
    factor = jnp.minimum(1.0, CLIP / grad_norm)
    news, means, squares = ([], [], [])
    for weight, gradient, mean_old, square_old, step_rate, step_decay in zip(
        shards, gradients, means_in, squares_in, step_rates, step_decays
    ):
        weight_new, mean_new, square_new = adam_update(
            weight, gradient, mean_old, square_old, factor, step_rate, step_decay
        )
        news.append(weight_new)
        means.append(mean_new)
        squares.append(square_new)
    return (
        block_output,
        patch_grad,
        skip_grad,
        grad_norm,
        news[0],
        news[1],
        news[2],
        news[3],
        news[4],
        news[5],
        news[6],
        news[7],
        news[8],
        news[9],
        means[0],
        means[1],
        means[2],
        means[3],
        means[4],
        means[5],
        means[6],
        means[7],
        means[8],
        means[9],
        squares[0],
        squares[1],
        squares[2],
        squares[3],
        squares[4],
        squares[5],
        squares[6],
        squares[7],
        squares[8],
        squares[9],
    )


def solution(mesh):
    crops, slabs = mesh.devices.shape
    mesh = Mesh(mesh.devices.reshape(crops, slabs // 2, 2), ("crop", "z", "core"))
    return jax.shard_map(
        local,
        mesh=mesh,
        in_specs=(
            P("crop", ("z", "core"), None, None),
            P("crop"),
            P("crop", ("z", "core"), None, None, None),
            P("crop", ("z", "core"), None, None, None),
            P(("z", "core"), "crop"),
            P(("z", "core"), "crop"),
            P(("z", "core"), "crop"),
            P(("z", "core"), "crop"),
            P(("z", "core"), "crop"),
            P(("z", "core"), "crop"),
            P(("z", "core"), "crop"),
            P(("z", "core"), "crop"),
            P(("z", "core"), "crop"),
            P(("crop", "z", "core")),
            P(("z", "core"), "crop"),
            P(("z", "core"), "crop"),
            P(("z", "core"), "crop"),
            P(("z", "core"), "crop"),
            P(("z", "core"), "crop"),
            P(("z", "core"), "crop"),
            P(("z", "core"), "crop"),
            P(("z", "core"), "crop"),
            P(("z", "core"), "crop"),
            P(("crop", "z", "core")),
            P(("z", "core"), "crop"),
            P(("z", "core"), "crop"),
            P(("z", "core"), "crop"),
            P(("z", "core"), "crop"),
            P(("z", "core"), "crop"),
            P(("z", "core"), "crop"),
            P(("z", "core"), "crop"),
            P(("z", "core"), "crop"),
            P(("z", "core"), "crop"),
            P(("crop", "z", "core")),
        ),
        out_specs=(
            P("crop", ("z", "core"), None, None, None),
            P("crop", ("z", "core"), None, None),
            P("crop", ("z", "core"), None, None, None),
            P(),
            P(("z", "core"), "crop"),
            P(("z", "core"), "crop"),
            P(("z", "core"), "crop"),
            P(("z", "core"), "crop"),
            P(("z", "core"), "crop"),
            P(("z", "core"), "crop"),
            P(("z", "core"), "crop"),
            P(("z", "core"), "crop"),
            P(("z", "core"), "crop"),
            P(("crop", "z", "core")),
            P(("z", "core"), "crop"),
            P(("z", "core"), "crop"),
            P(("z", "core"), "crop"),
            P(("z", "core"), "crop"),
            P(("z", "core"), "crop"),
            P(("z", "core"), "crop"),
            P(("z", "core"), "crop"),
            P(("z", "core"), "crop"),
            P(("z", "core"), "crop"),
            P(("crop", "z", "core")),
            P(("z", "core"), "crop"),
            P(("z", "core"), "crop"),
            P(("z", "core"), "crop"),
            P(("z", "core"), "crop"),
            P(("z", "core"), "crop"),
            P(("z", "core"), "crop"),
            P(("z", "core"), "crop"),
            P(("z", "core"), "crop"),
            P(("z", "core"), "crop"),
            P(("crop", "z", "core")),
        ),
        check_vma=False,
    )
```

```python
import math

import jax
import jax.numpy as jnp
from jax import lax
from jax.experimental import pallas as pl
from jax.experimental.pallas import tpu as pltpu
from jax.sharding import Mesh
from jax.sharding import PartitionSpec as P

D = 768
HEADS = 12
HDIM = 64
FF = 3072
PATCH = 4096
CHANS = 4
DEC = 128
SIDE = 8
STEP = 10


BETA_ONE = 0.9
BETA_TWO = 0.95
RATE = 0.07
DECAY = 0.05
VECTOR_RATE = 0.4
VECTOR_DECAY = 0.0
EPSILON = 1e-08
CLIP = 1.0
CONTRACT_ROWS = (((0,), (0,)), ((), ()))
CONTRACT_COLS = (((1,), (1,)), ((), ()))


def layer_norm(values, gain, shift):
    center = values - jnp.mean(values, -1, keepdims=True)
    spread = jnp.mean(center * center, -1, keepdims=True)
    return center * lax.rsqrt(spread + 1e-06) * gain + shift


def gelu_exact(values):
    return jax.nn.gelu(values, approximate=False)


def gelu_slope(values):
    return (
        0.5 * (1.0 + lax.erf(values * 0.7071067811865476))
        + values * jnp.exp(-0.5 * values * values) * 0.3989422804014327
    )


def matmul(left, right):
    return jnp.dot(left, right, preferred_element_type=jnp.float32)


def matmul_left_t(left, right):
    return lax.dot_general(left, right, CONTRACT_ROWS, preferred_element_type=jnp.float32)


def matmul_right_t(left, right):
    return lax.dot_general(left, right, CONTRACT_COLS, preferred_element_type=jnp.float32)


SLAB = ("z", "core")
SWAP = [(0, 1), (1, 0)]


def flip_pairs(count, step):
    return [(i, i ^ step) for i in range(count)]


def slab_sum(values):
    values = values + lax.ppermute(values, "core", SWAP)
    count, step = lax.axis_size("z"), 1
    while step < count:
        values = values + lax.ppermute(values, "z", flip_pairs(count, step))
        step *= 2
    return values


def crop_swap(pieces):
    return lax.all_to_all(pieces, "crop", 0, 0, tiled=True)


def flips(value, axis):
    count = lax.axis_size(axis)
    return [value] + [
        lax.ppermute(value, axis, flip_pairs(count, shift)) for shift in range(1, count)
    ]


def flips_of(pieces, axis):
    count = lax.axis_size(axis)
    return [pieces[0]] + [
        lax.ppermute(pieces[shift], axis, flip_pairs(count, shift)) for shift in range(1, count)
    ]


def total_of(pieces):
    total = pieces[0].astype(jnp.float32)
    for piece in pieces[1:]:
        total = total + piece.astype(jnp.float32)
    return total


def moves(plan, inputs, outputs):
    place = jnp.stack([lax.axis_index("crop"), lax.axis_index("core")]).astype(jnp.int32)

    def kernel(place_ref, *refs):
        crop, core = place_ref[0], place_ref[1]
        sources, targets = refs[: len(inputs)], refs[len(inputs) : -1]
        copies = [
            pltpu.make_async_copy(
                sources[source].at[from_index(crop, core)],
                targets[target].at[to_index(crop, core)],
                refs[-1].at[number],
            )
            for number, (source, from_index, target, to_index) in enumerate(plan)
        ]
        for copy in copies:
            copy.start()
        for copy in copies:
            copy.wait()

    size = sum(math.prod(shape) for shape in outputs)
    return pl.pallas_call(
        kernel,
        in_specs=[pl.BlockSpec(memory_space=pltpu.SMEM)]
        + [pl.BlockSpec(memory_space=pl.ANY)] * len(inputs),
        out_specs=[pl.BlockSpec(memory_space=pltpu.VMEM)] * len(outputs),
        out_shape=[jax.ShapeDtypeStruct(shape, jnp.bfloat16) for shape in outputs],
        scratch_shapes=[pltpu.SemaphoreType.DMA((len(plan),))],
        compiler_params=pltpu.CompilerParams(vmem_limit_bytes=4 * size + 2**22),
        cost_estimate=pl.CostEstimate(flops=0, transcendentals=0, bytes_accessed=4 * size),
    )(place, *inputs)


def chunk_at(spot, crop, core):
    kind, number, width = spot
    if kind == "row":
        return (slice(None), core, crop, number)
    return (slice(None), core, crop, slice(None), pl.ds(number * width, width))


def pack_at(number, lanes):
    if lanes is None:
        return (slice(None), number)
    return (slice(None), number, slice(None), pl.ds(lanes, DEC))


def gather_plan(spots):
    plan = []
    crops = lax.axis_size("crop")
    for side in range(2):
        for shift in range(crops):
            for number, lanes, target, spot in spots:
                plan.append(
                    (
                        side * crops + shift,
                        lambda crop, core, number=number, lanes=lanes: pack_at(number, lanes),
                        target,
                        lambda crop, core, side=side, shift=shift, spot=spot: chunk_at(
                            spot, crop ^ shift, core ^ side
                        ),
                    )
                )
    return plan


def core_swap(pieces):
    return [lax.ppermute(piece, "core", SWAP) for piece in pieces]


def scatter_plan(spots):
    plan = []
    for side in range(2):
        for shift in range(lax.axis_size("crop")):
            for number, lanes, source, spot in spots:
                plan.append(
                    (
                        source,
                        lambda crop, core, side=side, shift=shift, spot=spot: chunk_at(
                            spot, crop ^ shift, core ^ side
                        ),
                        side,
                        lambda crop, core, shift=shift, number=number, lanes=lanes: (shift,)
                        + pack_at(number, lanes),
                    )
                )
    return plan


def scatter_cores(weights, spots, chunks):
    crops, layers = lax.axis_size("crop"), lax.axis_size("z")
    shape = (crops, layers, chunks, weights[0].shape[3], D)
    return moves(scatter_plan(spots), weights, [shape, shape])


def core_sum(keep, send):
    got = lax.ppermute(send, "core", SWAP)
    return [
        (keep[shift].astype(jnp.float32) + got[shift].astype(jnp.float32)).astype(jnp.bfloat16)
        for shift in range(keep.shape[0])
    ]


def row_pad(rows, count):
    return jnp.pad(rows, ((0, count - rows.shape[0]), (0, 0)))


def slab_trim(full, piece, size):
    layers, cores, crops = full.shape[:3]
    rows = full.reshape(layers * cores, crops, -1, DEC)[:, :, :piece]
    return rows.reshape(layers * cores, -1, DEC)[:, :size].reshape(-1, DEC)


def slab_fill(full, piece, chunks, rows):
    layers, crops = lax.axis_size("z"), lax.axis_size("crop")
    shaped = full.reshape(2 * layers, -1, DEC)
    shaped = jnp.pad(shaped, ((0, 0), (0, crops * piece - shaped.shape[1]), (0, 0)))
    shaped = shaped.reshape(2 * layers, crops, piece, DEC)
    shaped = jnp.pad(shaped, ((0, 0), (0, 0), (0, chunks * rows - piece), (0, 0)))
    return shaped.reshape(layers, 2, crops, chunks, rows, DEC)


def to_units(rows, unit):
    crops, size = rows.shape[0], rows.shape[1] * rows.shape[2]
    flat = jnp.pad(rows.reshape(crops, size), ((0, 0), (0, -size % unit)))
    return flat.reshape(crops, -1, unit)


def from_units(units, rows, width):
    return units.reshape(units.shape[0], -1)[:, : rows * width].reshape(-1, rows, width)


def after(value, earlier):
    return lax.optimization_barrier((value, earlier))[0]


def z_scatter(pack):
    return lax.psum_scatter(pack, "z", scatter_dimension=0, tiled=False)


def neighbours(volume):
    count = lax.axis_size(SLAB)
    forward = [(i, i + 1) for i in range(count - 1)]
    backward = [(target, source) for source, target in forward]
    low = lax.ppermute(volume[:, -1:], SLAB, forward)
    high = lax.ppermute(volume[:, :1], SLAB, backward)
    return low, high


def with_planes(volume, rims):
    low, high = rims
    return jnp.concatenate([low.astype(volume.dtype), volume, high.astype(volume.dtype)], axis=1)


def inside(rimmed):
    place, last = lax.axis_index(SLAB), lax.axis_size(SLAB) - 1
    plane = lax.broadcasted_iota(jnp.int32, rimmed.shape, 1)
    outside = ((plane == 0) & (place == 0)) | (
        (plane == rimmed.shape[1] - 1) & (place == last)
    )
    return jnp.where(outside, jnp.zeros((), rimmed.dtype), rimmed)


def columns(rimmed):
    padded = jnp.pad(rimmed, ((0, 0), (0, 0), (1, 1), (1, 1), (0, 0)))
    crop_count, layers, breadth = (rimmed.shape[0], rimmed.shape[1] - 2, rimmed.shape[2])
    pieces = [
        padded[
            :,
            shift_z : shift_z + layers,
            shift_y : shift_y + breadth,
            shift_x : shift_x + breadth,
            :,
        ]
        for shift_z in range(3)
        for shift_y in range(3)
        for shift_x in range(3)
    ]
    return jnp.concatenate(pieces, -1).reshape(crop_count * layers * breadth * breadth, -1)


def back_conv(grad_rimmed, kernel, inputs):
    outputs = kernel.shape[1]
    flipped = (
        kernel.reshape(27, inputs, outputs)[::-1].transpose(0, 2, 1).reshape(27 * outputs, inputs)
    )
    crop_count, planes, breadth = grad_rimmed.shape[:3]
    return matmul(columns(grad_rimmed), flipped).reshape(
        crop_count, planes - 2, breadth, breadth, inputs
    )


def slab_totals(first, second):
    both = jnp.stack([jnp.sum(first, (1, 2, 3)), jnp.sum(second, (1, 2, 3))])
    return slab_sum(both)


def over_voxels(values):
    return values[:, None, None, None, :]


def norm_scales(values, voxel_count):
    totals = slab_totals(values, values * values)
    average = totals[0] / voxel_count
    inverse = lax.rsqrt(totals[1] / voxel_count - average * average + 1e-05)
    return over_voxels(average), over_voxels(inverse)


def norm_slopes(grad, normed, voxel_count):
    totals = slab_totals(grad, grad * normed)
    return over_voxels(totals[0] / voxel_count), over_voxels(totals[1] / voxel_count)


def heads_out(block, parts):
    crop_count, tokens = block.shape[0], block.shape[1]
    slab_count = lax.axis_size(SLAB)
    shaped = block.reshape(crop_count, tokens, parts, HEADS, HDIM).transpose(0, 3, 1, 2, 4)
    shaped = shaped.reshape(crop_count * HEADS, tokens, parts * HDIM)
    spare = -shaped.shape[0] % slab_count
    shaped = jnp.pad(shaped, ((0, spare), (0, 0), (0, 0)))
    return lax.all_to_all(shaped, SLAB, 0, 1, tiled=True)


def heads_back(block, crop_count, parts):
    shaped = lax.all_to_all(block, SLAB, 1, 0, tiled=True)[: crop_count * HEADS]
    tokens = shaped.shape[1]
    shaped = shaped.reshape(crop_count, HEADS, tokens, parts, HDIM).transpose(0, 2, 3, 1, 4)
    return shaped.reshape(crop_count * tokens, parts * D)


def to_volume(lifted, crop_count):
    layers = lifted.shape[0] // (crop_count * SIDE * SIDE)
    shaped = lifted.reshape(crop_count, layers, SIDE, SIDE, 2, 2, 2, DEC)
    return shaped.transpose(0, 1, 4, 2, 5, 3, 6, 7).reshape(
        crop_count, 2 * layers, 2 * SIDE, 2 * SIDE, DEC
    )


def to_tokens(volume):
    crop_count, layers = (volume.shape[0], volume.shape[1] // 2)
    shaped = volume.reshape(crop_count, layers, 2, SIDE, 2, SIDE, 2, DEC)
    return shaped.transpose(0, 1, 3, 5, 2, 4, 6, 7).reshape(
        crop_count * layers * SIDE * SIDE, 8 * DEC
    )


def adam_update(weight, gradient, mean_old, square_old, factor, step_rate, step_decay):
    clipped = gradient * factor
    mean_new = BETA_ONE * mean_old + (1.0 - BETA_ONE) * clipped
    square_new = BETA_TWO * square_old + (1.0 - BETA_TWO) * clipped * clipped
    direction = (
        mean_new
        / (1.0 - BETA_ONE**STEP)
        / (jnp.sqrt(square_new / (1.0 - BETA_TWO**STEP)) + EPSILON)
    )
    return (weight - step_rate * (direction + step_decay * weight), mean_new, square_new)


def local(
    patches,
    modality,
    skip_feats,
    cotangent,
    embedding,
    attention_in,
    attention_out,
    expand_up,
    expand_down,
    upsample,
    convolve_one,
    convolve_two,
    positions,
    vectors,
    embedding_mean,
    attention_in_mean,
    attention_out_mean,
    expand_up_mean,
    expand_down_mean,
    upsample_mean,
    convolve_one_mean,
    convolve_two_mean,
    positions_mean,
    vectors_mean,
    embedding_square,
    attention_in_square,
    attention_out_square,
    expand_up_square,
    expand_down_square,
    upsample_square,
    convolve_one_square,
    convolve_two_square,
    positions_square,
    vectors_square,
):
    shards = (
        embedding,
        attention_in,
        attention_out,
        expand_up,
        expand_down,
        upsample,
        convolve_one,
        convolve_two,
        positions,
        vectors,
    )
    means_in = (
        embedding_mean,
        attention_in_mean,
        attention_out_mean,
        expand_up_mean,
        expand_down_mean,
        upsample_mean,
        convolve_one_mean,
        convolve_two_mean,
        positions_mean,
        vectors_mean,
    )
    squares_in = (
        embedding_square,
        attention_in_square,
        attention_out_square,
        expand_up_square,
        expand_down_square,
        upsample_square,
        convolve_one_square,
        convolve_two_square,
        positions_square,
        vectors_square,
    )
    step_rates = (RATE,) * 9 + (VECTOR_RATE,)
    step_decays = (DECAY,) * 9 + (VECTOR_DECAY,)
    crops = lax.axis_size("crop")
    layers = lax.axis_size("z")
    slab_count = 2 * layers
    crop_batch = patches.shape[0]
    local_tokens = patches.shape[1] * patches.shape[2]
    rows_in = crop_batch * local_tokens
    voxel_count = skip_feats.shape[1] * skip_feats.shape[2] * skip_feats.shape[3] * slab_count
    score_scale = HDIM ** (-0.5)
    unit = D // crops

    lows = [entry.astype(jnp.bfloat16) for entry in shards]
    embed_rows = embedding.shape[0]
    share = embed_rows // crops
    block = math.gcd(share, PATCH)
    groups = share // block
    row_count = attention_in.shape[0] // crops
    down_count = expand_down.shape[0] // crops
    embed_wide = (
        lows[0].reshape(groups, crops, block, unit).transpose(1, 0, 2, 3).reshape(crops, share, unit)
    )
    first_count = -(-convolve_one.shape[0] // crops)
    second_count = -(-convolve_two.shape[0] // crops)
    narrow = jnp.concatenate(
        [
            jnp.pad(lows[6], ((0, crops * first_count - lows[6].shape[0]), (0, 0))).reshape(
                crops, first_count, -1
            ),
            jnp.pad(lows[7], ((0, crops * second_count - lows[7].shape[0]), (0, 0))).reshape(
                crops, second_count, -1
            ),
        ],
        1,
    )
    up_rows = expand_up.shape[0]
    class_size = FF // crops
    per_class = class_size // crops
    up_units = lows[3].reshape(up_rows, -1, crops, down_count).transpose(2, 0, 1, 3)
    up_units = to_units(up_units.reshape(crops, up_rows, per_class), unit)
    lift_units = to_units(lows[5].reshape(crops, row_count, -1), unit)
    narrow_units = to_units(narrow, unit)
    wide = jnp.concatenate(
        [
            lows[1].reshape(crops, row_count, 3, unit).transpose(0, 2, 1, 3).reshape(crops, -1, unit),
            lows[2].reshape(crops, row_count, unit),
            up_units,
            lows[4].reshape(crops, down_count, unit),
            jnp.broadcast_to(lows[8][None], (crops,) + lows[8].shape),
            lift_units,
            narrow_units,
        ],
        1,
    )
    pieces = (CHANS * PATCH) // (block * crops)
    ct_size = PATCH // crops
    own_crop = lax.axis_index("crop")
    own_mri = jnp.broadcast_to(
        (modality == 1)[:, None, None], (crop_batch, local_tokens, 1)
    ).reshape(-1, 1)
    marks = jnp.broadcast_to(own_mri.astype(jnp.float32), (rows_in, 128))
    is_mri = jnp.concatenate(flips(marks, "crop"), 0)[:, :1] > 0.5
    pixels = patches.reshape(rows_in, pieces, crops, block).transpose(2, 0, 1, 3)
    pixels = pixels.reshape(crops, rows_in, pieces * block)
    pixels = [
        lax.dynamic_index_in_dim(pixels, own_crop ^ shift, 0, keepdims=False)
        for shift in range(crops)
    ]
    pixel_parts = flips_of(pixels, "crop")
    wide = crop_swap(after(wide, is_mri))
    embed_part = crop_swap(after(embed_wide, (wide, pixels)))
    embed_part = embed_part.transpose(1, 0, 2).reshape(share, D)
    marks = []
    edge = 0
    for size in (3 * row_count, row_count, up_units.shape[1], down_count, lows[8].shape[0],
                 lift_units.shape[1], narrow_units.shape[1]):
        marks.append(wide[:, edge : edge + size])
        edge += size
    lift_rows = from_units(marks[5], row_count, 8 * DEC // crops)
    narrow = from_units(marks[6], first_count + second_count, DEC // crops)
    triple_part = marks[0].reshape(3, crops, row_count, unit).transpose(0, 2, 1, 3).reshape(-1, D)
    output_part = marks[1].transpose(1, 0, 2).reshape(row_count, D)
    up_part = from_units(marks[2], up_rows, per_class).transpose(1, 0, 2).reshape(-1, D)
    down_part = marks[3].transpose(1, 0, 2).reshape(down_count, D)
    position_rows = marks[4].transpose(1, 0, 2).reshape(-1, D).astype(jnp.float32)
    lift_part = (
        lift_rows.transpose(1, 0, 2).reshape(row_count, 8, DEC).transpose(1, 0, 2).reshape(-1, DEC)
    )
    narrow_part = narrow.transpose(1, 0, 2).reshape(-1, DEC)
    first_chunks, second_chunks = -(-first_count // row_count), -(-second_count // row_count)
    slim = jnp.concatenate(
        [
            lift_part,
            row_pad(narrow_part[:first_count], first_chunks * row_count),
            row_pad(narrow_part[first_count:], second_chunks * row_count),
        ],
        0,
    )
    slim_chunks = -(-(8 + first_chunks + second_chunks) // 6)
    slim = row_pad(slim, 6 * slim_chunks * row_count)
    slim = slim.reshape(slim_chunks, 6, row_count, DEC).transpose(0, 2, 1, 3).reshape(-1, D)
    vector_size = vectors.shape[0]
    vector_part = jnp.pad(lows[9][None], ((0, row_count - 1), (0, D - vector_size)))

    quarter = 6
    packs = jnp.concatenate([triple_part, output_part, vector_part, slim], 0)
    packs = lax.all_gather(packs.reshape(-1, row_count, D), "z", axis=0)
    packs = after(packs, pixel_parts)
    pack_one, pack_slim = packs[:, :5], packs[:, 5:]
    embed_full = lax.all_gather(embed_part, SLAB, axis=0, tiled=True)
    up_size = up_part.shape[0]
    ff_part = after(jnp.concatenate([up_part, down_part], 0), embed_full)
    ff_full = lax.all_gather(ff_part, SLAB, axis=0)
    up_full = ff_full[:, :up_size].reshape(D, class_size)
    down_full = ff_full[:, up_size:].reshape(class_size, D)
    one_spots = [
        (0, None, 0, ("lane", 0, D)),
        (1, None, 0, ("lane", 1, D)),
        (2, None, 0, ("lane", 2, D)),
        (3, None, 1, ("lane", 0, D)),
        (4, None, 2, ("lane", 0, D)),
    ]
    slim_list = [(0, ("lane", k, DEC)) for k in range(8)]
    slim_list += [(1, ("row", k, DEC)) for k in range(first_chunks)]
    slim_list += [(2, ("row", k, DEC)) for k in range(second_chunks)]
    slim_spots = [
        (number // quarter, number % quarter * DEC, target, spot)
        for number, (target, spot) in enumerate(slim_list)
    ]
    lead = (layers, 2, crops)
    none = jnp.zeros((), jnp.bfloat16)
    one_own = flips(pack_one, "crop")
    pixels = jnp.concatenate(after(pixel_parts, one_own), 0)
    pixel_rows = jnp.concatenate(
        [jnp.where(is_mri, none, pixels[:, :ct_size]), jnp.where(is_mri, pixels, none)], 1
    )
    partial = matmul(pixel_rows, embed_full).astype(jnp.bfloat16).reshape(crops, rows_in, D)
    product = total_of(flips_of(list(partial), "crop"))
    one_other = core_swap(after(one_own, partial))
    triple_full, output_full, vector_full = moves(
        gather_plan(one_spots),
        one_own + one_other,
        [lead + (row_count, 3 * D), lead + (row_count, D), lead + (row_count, D)],
    )
    triple_full = triple_full.reshape(D, 3 * D)
    output_full = output_full.reshape(D, D)
    vector_full = vector_full[:, :, :, 0, :vector_size].transpose(2, 0, 1, 3).reshape(12 * D)
    vector_rows = vector_full.astype(jnp.float32).reshape(12, D)
    embedded = (
        product
        + jnp.where(own_mri, vector_rows[7], vector_rows[6])
        + jnp.concatenate([position_rows] * crop_batch, 0)
    )
    normed_one, pull_one = jax.vjp(layer_norm, embedded, vector_rows[0], vector_rows[1])
    normed_one = normed_one.astype(jnp.bfloat16)
    triple = matmul(normed_one, triple_full).astype(jnp.bfloat16)
    triple = heads_out(triple.reshape(crop_batch, local_tokens, 3 * D), 3)
    query, keys, values = triple[..., :HDIM], triple[..., HDIM : 2 * HDIM], triple[..., 2 * HDIM :]
    scores = (
        jnp.einsum("pqd,pkd->pqk", query, keys, preferred_element_type=jnp.float32) * score_scale
    )
    probs = jax.nn.softmax(scores, axis=-1)
    probs_low = probs.astype(jnp.bfloat16)
    mixed = jnp.einsum("pqk,pkd->pqd", probs_low, values, preferred_element_type=jnp.float32)
    slim_own = flips(pack_slim, "crop")
    mixed = after(mixed.astype(jnp.bfloat16), slim_own)
    mixed = heads_back(mixed, crop_batch, 1)
    slim_other = core_swap(slim_own)
    hidden_one = embedded + matmul(mixed, output_full) + vector_rows[4]
    hidden_one = after(hidden_one, slim_other)
    lift_full, first_full, second_full = moves(
        gather_plan(slim_spots),
        slim_own + slim_other,
        [
            lead + (row_count, 8 * DEC),
            lead + (first_chunks, row_count, DEC),
            lead + (second_chunks, row_count, DEC),
        ],
    )
    lift_full = lift_full.reshape(D, 8 * DEC)
    first_full = slab_trim(first_full, first_count, convolve_one.shape[0])
    second_full = slab_trim(second_full, second_count, convolve_two.shape[0])
    normed_two, pull_two = jax.vjp(layer_norm, hidden_one, vector_rows[2], vector_rows[3])
    normed_two = normed_two.astype(jnp.bfloat16)
    normed_all = jnp.concatenate(flips(normed_two, "crop"), 0)
    bias_class = vector_rows[8:].reshape(slab_count, crops, down_count)
    bias_class = lax.dynamic_index_in_dim(bias_class, own_crop, 1, keepdims=False).reshape(-1)
    inner = matmul(normed_all, up_full) + bias_class
    activated = gelu_exact(inner).astype(jnp.bfloat16)
    partial = matmul(activated, down_full).astype(jnp.bfloat16).reshape(crops, rows_in, D)
    product = total_of(flips_of(list(partial), "crop"))
    hidden_two = hidden_one + product + vector_rows[5]
    hidden_low = hidden_two.astype(jnp.bfloat16)
    volume = to_volume(matmul(hidden_low, lift_full), crop_batch)
    joined = jnp.concatenate([volume.astype(jnp.bfloat16), skip_feats], -1)
    joined = with_planes(joined, neighbours(joined))
    volume_rimmed = with_planes(
        volume, (joined[:, :1, ..., :DEC], joined[:, -1:, ..., :DEC])
    )
    target_rimmed = with_planes(cotangent, neighbours(cotangent)).astype(jnp.float32)
    cols_one = columns(joined)
    conv_one = matmul(cols_one, first_full).reshape(volume.shape)
    conv_one_rimmed = with_planes(conv_one, neighbours(conv_one.astype(jnp.bfloat16)))
    average_a, inverse_a = norm_scales(conv_one, voxel_count)
    normed_a = (conv_one_rimmed - average_a) * inverse_a
    first_act = inside(gelu_exact(normed_a).astype(jnp.bfloat16))
    cols_two = columns(first_act)
    conv_two = matmul(cols_two, second_full).reshape(volume.shape)
    conv_two_rimmed = with_planes(conv_two, neighbours(conv_two.astype(jnp.bfloat16)))
    average_b, inverse_b = norm_scales(conv_two, voxel_count)
    normed_b = (conv_two_rimmed - average_b) * inverse_b
    before = normed_b + volume_rimmed
    block_output = gelu_exact(before[:, 1:-1]).astype(jnp.bfloat16)

    grad_before = target_rimmed * gelu_slope(before)
    mean_b, slope_b = norm_slopes(grad_before[:, 1:-1], normed_b[:, 1:-1], voxel_count)
    grad_conv_two = inverse_b * (grad_before - mean_b - normed_b * slope_b)
    grad_conv_two = inside(grad_conv_two.astype(jnp.bfloat16))
    weight_second = matmul_left_t(cols_two, grad_conv_two[:, 1:-1].reshape(-1, DEC))
    grad_first = back_conv(grad_conv_two, second_full, DEC) * gelu_slope(normed_a[:, 1:-1])
    grad_first_rimmed = with_planes(grad_first, neighbours(grad_first.astype(jnp.bfloat16)))
    mean_a, slope_a = norm_slopes(grad_first, normed_a[:, 1:-1], voxel_count)
    grad_conv_one = inverse_a * (grad_first_rimmed - mean_a - normed_a * slope_a)
    grad_conv_one = inside(grad_conv_one.astype(jnp.bfloat16))
    weight_first = matmul_left_t(cols_one, grad_conv_one[:, 1:-1].reshape(-1, DEC))
    grad_joined = back_conv(grad_conv_one, first_full, 2 * DEC)
    skip_grad = grad_joined[..., DEC:].astype(jnp.bfloat16)
    grad_lifted = to_tokens(grad_before[:, 1:-1] + grad_joined[..., :DEC]).astype(jnp.bfloat16)
    weight_lift = matmul_left_t(hidden_low, grad_lifted)
    grad_hidden = matmul_right_t(grad_lifted, lift_full)
    bias_down = jnp.sum(grad_hidden, 0)
    grad_branch = grad_hidden.astype(jnp.bfloat16)
    grad_all = jnp.concatenate(flips(grad_branch, "crop"), 0)
    grad_inner = matmul_right_t(grad_all, down_full) * gelu_slope(inner)
    bias_up = jnp.sum(grad_inner, 0)
    grad_inner_low = grad_inner.astype(jnp.bfloat16)
    partial = matmul_right_t(grad_inner_low, up_full).astype(jnp.bfloat16)
    partial = partial.reshape(crops, rows_in, D)
    weight_down = matmul_left_t(activated, grad_all).astype(jnp.bfloat16)
    weight_up = matmul_left_t(normed_all, grad_inner_low).astype(jnp.bfloat16)
    ff_grads = jnp.concatenate(
        [weight_up.reshape(slab_count, -1, D), weight_down.reshape(slab_count, -1, D)], 1
    )

    slim_move = scatter_cores(
        [
            weight_lift.astype(jnp.bfloat16).reshape(lead + (row_count, 8 * DEC)),
            slab_fill(weight_first.astype(jnp.bfloat16), first_count, first_chunks, row_count),
            slab_fill(weight_second.astype(jnp.bfloat16), second_count, second_chunks, row_count),
        ],
        slim_spots,
        slim_chunks,
    )
    slim_parts = core_sum(*slim_move)
    partial = after(partial, slim_move[1])
    back_two = pull_two(total_of(flips_of(list(partial), "crop")))
    grad_hidden = grad_hidden + back_two[0]
    bias_out = jnp.sum(grad_hidden, 0)
    grad_branch = grad_hidden.astype(jnp.bfloat16)
    weight_out = matmul_left_t(mixed, grad_branch)
    grad_mixed = matmul_right_t(grad_branch, output_full).astype(jnp.bfloat16)
    grad_mixed = after(grad_mixed, slim_parts)
    slim_got = flips_of(slim_parts, "crop")
    grad_mixed = heads_out(grad_mixed.reshape(crop_batch, local_tokens, D), 1)
    grad_probs = jnp.einsum(
        "pqd,pkd->pqk", grad_mixed, values, preferred_element_type=jnp.float32
    )
    centre = jnp.sum(probs * grad_probs, -1, keepdims=True)
    grad_scores = (probs * (grad_probs - centre)).astype(jnp.bfloat16)
    grad_query = (
        jnp.einsum("pqk,pkd->pqd", grad_scores, keys, preferred_element_type=jnp.float32)
        * score_scale
    )
    grad_keys = (
        jnp.einsum("pqk,pqd->pkd", grad_scores, query, preferred_element_type=jnp.float32)
        * score_scale
    )
    grad_values = jnp.einsum(
        "pqk,pqd->pkd", probs_low, grad_mixed, preferred_element_type=jnp.float32
    )
    grad_triple = jnp.concatenate([grad_query, grad_keys, grad_values], -1).astype(jnp.bfloat16)
    grad_triple = heads_back(grad_triple, crop_batch, 3)
    grad_triple = after(grad_triple, slim_got)
    ff_grads = after(ff_grads, grad_triple)
    ff_sum = lax.psum_scatter(ff_grads, SLAB, scatter_dimension=0, tiled=False)
    weight_triple = matmul_left_t(normed_one, grad_triple)
    back_one = pull_one(matmul_right_t(grad_triple, triple_full))
    grad_hidden = grad_hidden + back_one[0]
    grad_low = grad_hidden.astype(jnp.bfloat16)

    grad_rows = jnp.concatenate(flips(grad_low, "crop"), 0)
    weight_embed = matmul_left_t(pixel_rows, grad_rows).astype(jnp.bfloat16)
    slim_sum = total_of(after(slim_got, weight_embed)).astype(jnp.bfloat16)
    embed_sum = lax.psum_scatter(weight_embed, SLAB, scatter_dimension=0, tiled=True)
    pixel_grad = matmul_right_t(after(grad_rows, weight_embed), embed_full)
    ct_grad = jnp.pad(pixel_grad[:, :ct_size], ((0, 0), (0, (CHANS - 1) * ct_size)))
    pixel_grad = jnp.where(is_mri, pixel_grad[:, ct_size:], ct_grad).astype(jnp.bfloat16)
    pixel_got = flips_of(list(pixel_grad.reshape(crops, rows_in, pieces * block)), "crop")
    pixel_got = jnp.stack(pixel_got)
    patch_grad = jnp.stack(
        [
            lax.dynamic_index_in_dim(pixel_got, own_crop ^ part, 0, keepdims=False)
            for part in range(crops)
        ]
    )
    patch_grad = patch_grad.reshape(crops, rows_in, pieces, block).transpose(1, 2, 0, 3)
    patch_grad = patch_grad.reshape(patches.shape)

    bias_ct = jnp.sum(jnp.where(own_mri, 0.0, grad_hidden), 0)
    bias_mri = jnp.sum(jnp.where(own_mri, grad_hidden, 0.0), 0)
    position_grad = jnp.sum(grad_hidden.reshape(crop_batch, local_tokens, D), 0)
    at_class = lax.broadcasted_iota(jnp.int32, (slab_count, crops, down_count), 1) == own_crop
    bias_full = jnp.where(at_class, bias_up.reshape(slab_count, 1, down_count), 0.0)
    vector_grad = jnp.concatenate(
        [
            jnp.stack(
                [
                    back_one[1],
                    back_one[2],
                    back_two[1],
                    back_two[2],
                    bias_out,
                    bias_down,
                    bias_ct,
                    bias_mri,
                ]
            ),
            bias_full.reshape(4, D),
        ],
        0,
    ).astype(jnp.bfloat16)
    vector_pack = vector_grad.reshape(crops, layers, 2, 1, vector_size).transpose(1, 2, 0, 3, 4)
    vector_pack = jnp.pad(
        vector_pack, ((0, 0),) * 3 + ((0, row_count - 1), (0, D - vector_size))
    )
    weight_triple = after(weight_triple.astype(jnp.bfloat16), weight_embed)
    one_parts = core_sum(*scatter_cores(
        [
            weight_triple.reshape(lead + (row_count, 3 * D)),
            weight_out.astype(jnp.bfloat16).reshape(lead + (row_count, D)),
            vector_pack,
        ],
        one_spots,
        5,
    ))
    one_sum = total_of(flips_of(one_parts, "crop")).astype(jnp.bfloat16)
    sums = jnp.concatenate([slim_sum, one_sum], 1)
    sums = z_scatter(after(sums, (embed_sum, pixel_grad)))
    sums = sums.reshape(-1, D)
    one_row = slim_chunks * row_count

    def by_units(rows, chunks):
        shaped = rows.reshape(chunks, -1, crops, unit).transpose(0, 2, 1, 3)
        return shaped.reshape(crops, -1, unit)

    def join_units(got, chunks):
        return (
            got.reshape(crops, chunks, -1, unit).transpose(0, 2, 1, 3).reshape(-1, chunks * unit)
        )

    embed_got = crop_swap(by_units(embed_sum, 1)).astype(jnp.float32)
    embed_grad = (
        embed_got.reshape(crops, groups, block, unit).transpose(1, 0, 2, 3).reshape(-1, unit)
    )
    sum_one = sums[one_row:]
    slim_all = sums[:one_row].reshape(slim_chunks, row_count, 6, DEC)
    slim_all = slim_all.transpose(0, 2, 1, 3).reshape(-1, DEC)
    first_start = 8 * row_count
    second_start = first_start + first_chunks * row_count
    lift_sum = slim_all[:first_start].reshape(8, row_count, DEC).transpose(1, 0, 2)
    lift_sum = lift_sum.reshape(row_count, crops, -1).transpose(1, 0, 2)
    narrow_sum = jnp.concatenate(
        [
            slim_all[first_start : first_start + first_count],
            slim_all[second_start : second_start + second_count],
        ],
        0,
    )
    narrow_sum = narrow_sum.reshape(-1, crops, DEC // crops).transpose(1, 0, 2)
    lift_units, narrow_units = to_units(lift_sum, unit), to_units(narrow_sum, unit)
    up_units = ff_sum[:up_size].reshape(up_rows, crops, per_class).transpose(1, 0, 2)
    up_units = to_units(up_units, unit)
    wide = jnp.concatenate(
        [
            up_units,
            by_units(ff_sum[up_size:], 1),
            by_units(sum_one[: 3 * row_count], 3),
            by_units(sum_one[3 * row_count : 4 * row_count], 1),
            by_units(position_grad.astype(jnp.bfloat16), 1),
            lift_units,
            narrow_units,
        ],
        1,
    )
    wide = crop_swap(wide).astype(jnp.float32)
    marks = []
    edge = 0
    for size in (up_units.shape[1], down_count, 3 * row_count, row_count, position_grad.shape[0],
                 lift_units.shape[1], narrow_units.shape[1]):
        marks.append(wide[:, edge : edge + size])
        edge += size
    up_grad = from_units(marks[0], up_rows, per_class)
    up_grad = up_grad.reshape(crops, up_rows, -1, down_count).transpose(1, 2, 0, 3)
    up_grad = up_grad.reshape(expand_up.shape)
    down_grad = join_units(marks[1], 1)
    triple_grad = join_units(marks[2], 3)
    output_grad = join_units(marks[3], 1)
    position_grad = jnp.sum(marks[4], 0)
    lift_grad = from_units(marks[5], row_count, 8 * DEC // crops).reshape(upsample.shape)
    narrow_got = from_units(marks[6], first_count + second_count, DEC // crops)
    first_grad = narrow_got[:, :first_count].reshape(-1, DEC // crops)[: convolve_one.shape[0]]
    second_grad = narrow_got[:, first_count:].reshape(-1, DEC // crops)[: convolve_two.shape[0]]
    vector_final = sum_one[4 * row_count, :vector_size].astype(jnp.float32)
    gradients = (
        embed_grad,
        triple_grad,
        output_grad,
        up_grad,
        down_grad,
        lift_grad,
        first_grad,
        second_grad,
        position_grad,
        vector_final,
    )
    local_sum = jnp.float32(0.0)
    for gradient in (embed_sum, ff_sum, lift_sum, narrow_sum, sum_one, position_grad):
        wide_grad = gradient.astype(jnp.float32)
        local_sum = local_sum + jnp.sum(wide_grad * wide_grad)
    grad_norm = jnp.sqrt(slab_sum(total_of(flips(local_sum.reshape(1, 1), "crop"))))[0, 0]
    factor = jnp.minimum(1.0, CLIP / grad_norm)
    news, means, squares = ([], [], [])
    for weight, gradient, mean_old, square_old, step_rate, step_decay in zip(
        shards, gradients, means_in, squares_in, step_rates, step_decays
    ):
        weight_new, mean_new, square_new = adam_update(
            weight, gradient, mean_old, square_old, factor, step_rate, step_decay
        )
        news.append(weight_new)
        means.append(mean_new)
        squares.append(square_new)
    return (
        block_output,
        patch_grad,
        skip_grad,
        grad_norm,
        news[0],
        news[1],
        news[2],
        news[3],
        news[4],
        news[5],
        news[6],
        news[7],
        news[8],
        news[9],
        means[0],
        means[1],
        means[2],
        means[3],
        means[4],
        means[5],
        means[6],
        means[7],
        means[8],
        means[9],
        squares[0],
        squares[1],
        squares[2],
        squares[3],
        squares[4],
        squares[5],
        squares[6],
        squares[7],
        squares[8],
        squares[9],
    )


def solution(mesh):
    crops, slabs = mesh.devices.shape
    mesh = Mesh(mesh.devices.reshape(crops, slabs // 2, 2), ("crop", "z", "core"))
    return jax.shard_map(
        local,
        mesh=mesh,
        in_specs=(
            P("crop", ("z", "core"), None, None),
            P("crop"),
            P("crop", ("z", "core"), None, None, None),
            P("crop", ("z", "core"), None, None, None),
            P(("z", "core"), "crop"),
            P(("z", "core"), "crop"),
            P(("z", "core"), "crop"),
            P(("z", "core"), "crop"),
            P(("z", "core"), "crop"),
            P(("z", "core"), "crop"),
            P(("z", "core"), "crop"),
            P(("z", "core"), "crop"),
            P(("z", "core"), "crop"),
            P(("crop", "z", "core")),
            P(("z", "core"), "crop"),
            P(("z", "core"), "crop"),
            P(("z", "core"), "crop"),
            P(("z", "core"), "crop"),
            P(("z", "core"), "crop"),
            P(("z", "core"), "crop"),
            P(("z", "core"), "crop"),
            P(("z", "core"), "crop"),
            P(("z", "core"), "crop"),
            P(("crop", "z", "core")),
            P(("z", "core"), "crop"),
            P(("z", "core"), "crop"),
            P(("z", "core"), "crop"),
            P(("z", "core"), "crop"),
            P(("z", "core"), "crop"),
            P(("z", "core"), "crop"),
            P(("z", "core"), "crop"),
            P(("z", "core"), "crop"),
            P(("z", "core"), "crop"),
            P(("crop", "z", "core")),
        ),
        out_specs=(
            P("crop", ("z", "core"), None, None, None),
            P("crop", ("z", "core"), None, None),
            P("crop", ("z", "core"), None, None, None),
            P(),
            P(("z", "core"), "crop"),
            P(("z", "core"), "crop"),
            P(("z", "core"), "crop"),
            P(("z", "core"), "crop"),
            P(("z", "core"), "crop"),
            P(("z", "core"), "crop"),
            P(("z", "core"), "crop"),
            P(("z", "core"), "crop"),
            P(("z", "core"), "crop"),
            P(("crop", "z", "core")),
            P(("z", "core"), "crop"),
            P(("z", "core"), "crop"),
            P(("z", "core"), "crop"),
            P(("z", "core"), "crop"),
            P(("z", "core"), "crop"),
            P(("z", "core"), "crop"),
            P(("z", "core"), "crop"),
            P(("z", "core"), "crop"),
            P(("z", "core"), "crop"),
            P(("crop", "z", "core")),
            P(("z", "core"), "crop"),
            P(("z", "core"), "crop"),
            P(("z", "core"), "crop"),
            P(("z", "core"), "crop"),
            P(("z", "core"), "crop"),
            P(("z", "core"), "crop"),
            P(("z", "core"), "crop"),
            P(("z", "core"), "crop"),
            P(("z", "core"), "crop"),
            P(("crop", "z", "core")),
        ),
        check_vma=False,
    )
```

```python
import math

import jax
import jax.numpy as jnp
from jax import lax
from jax.experimental import pallas as pl
from jax.experimental.pallas import tpu as pltpu
from jax.sharding import Mesh
from jax.sharding import PartitionSpec as P

D = 768
HEADS = 12
HDIM = 64
FF = 3072
PATCH = 4096
CHANS = 4
DEC = 128
SIDE = 8
STEP = 10


BETA_ONE = 0.9
BETA_TWO = 0.95
RATE = 0.07
DECAY = 0.05
VECTOR_RATE = 0.4
VECTOR_DECAY = 0.0
EPSILON = 1e-08
CLIP = 1.0
CONTRACT_ROWS = (((0,), (0,)), ((), ()))
CONTRACT_COLS = (((1,), (1,)), ((), ()))


def layer_norm(values, gain, shift):
    center = values - jnp.mean(values, -1, keepdims=True)
    spread = jnp.mean(center * center, -1, keepdims=True)
    return center * lax.rsqrt(spread + 1e-06) * gain + shift


def gelu_exact(values):
    return jax.nn.gelu(values, approximate=False)


def gelu_slope(values):
    return (
        0.5 * (1.0 + lax.erf(values * 0.7071067811865476))
        + values * jnp.exp(-0.5 * values * values) * 0.3989422804014327
    )


def matmul(left, right):
    return jnp.dot(left, right, preferred_element_type=jnp.float32)


def matmul_left_t(left, right):
    return lax.dot_general(left, right, CONTRACT_ROWS, preferred_element_type=jnp.float32)


def matmul_right_t(left, right):
    return lax.dot_general(left, right, CONTRACT_COLS, preferred_element_type=jnp.float32)


SLAB = ("z", "core")
SWAP = [(0, 1), (1, 0)]


def flip_pairs(count, step):
    return [(i, i ^ step) for i in range(count)]


def slab_sum(values):
    values = values + lax.ppermute(values, "core", SWAP)
    count, step = lax.axis_size("z"), 1
    while step < count:
        values = values + lax.ppermute(values, "z", flip_pairs(count, step))
        step *= 2
    return values


def crop_swap(pieces):
    return lax.all_to_all(pieces, "crop", 0, 0, tiled=True)


def flips(value, axis):
    count = lax.axis_size(axis)
    return [value] + [
        lax.ppermute(value, axis, flip_pairs(count, shift)) for shift in range(1, count)
    ]


def flips_of(pieces, axis):
    count = lax.axis_size(axis)
    return [pieces[0]] + [
        lax.ppermute(pieces[shift], axis, flip_pairs(count, shift)) for shift in range(1, count)
    ]


def total_of(pieces):
    total = pieces[0].astype(jnp.float32)
    for piece in pieces[1:]:
        total = total + piece.astype(jnp.float32)
    return total


def moves(plan, inputs, outputs):
    place = jnp.stack([lax.axis_index("crop"), lax.axis_index("core")]).astype(jnp.int32)

    def kernel(place_ref, *refs):
        crop, core = place_ref[0], place_ref[1]
        sources, targets = refs[: len(inputs)], refs[len(inputs) : -1]
        copies = [
            pltpu.make_async_copy(
                sources[source].at[from_index(crop, core)],
                targets[target].at[to_index(crop, core)],
                refs[-1].at[number],
            )
            for number, (source, from_index, target, to_index) in enumerate(plan)
        ]
        for copy in copies:
            copy.start()
        for copy in copies:
            copy.wait()

    size = sum(math.prod(shape) for shape in outputs)
    return pl.pallas_call(
        kernel,
        in_specs=[pl.BlockSpec(memory_space=pltpu.SMEM)]
        + [pl.BlockSpec(memory_space=pl.ANY)] * len(inputs),
        out_specs=[pl.BlockSpec(memory_space=pltpu.VMEM)] * len(outputs),
        out_shape=[jax.ShapeDtypeStruct(shape, jnp.bfloat16) for shape in outputs],
        scratch_shapes=[pltpu.SemaphoreType.DMA((len(plan),))],
        compiler_params=pltpu.CompilerParams(vmem_limit_bytes=4 * size + 2**22),
        cost_estimate=pl.CostEstimate(flops=0, transcendentals=0, bytes_accessed=4 * size),
    )(place, *inputs)


def column_plan(pieces, block, apart):
    crops = lax.axis_size("crop")
    plan = []
    for shift in range(crops):
        for piece in range(pieces):

            def whole(crop, core, shift=shift, piece=piece):
                start = (piece * crops + (crop ^ shift)) * block
                return (slice(None), pl.ds(pl.multiple_of(start, block), block))

            def part(crop, core, piece=piece):
                return (slice(None), pl.ds(piece * block, block))

            plan.append((0, whole, shift, part) if apart else (shift, part, 0, whole))
    return plan


def chunk_at(spot, crop, core):
    kind, number, width = spot
    if kind == "row":
        return (slice(None), core, crop, number)
    return (slice(None), core, crop, slice(None), pl.ds(number * width, width))


def pack_at(number, lanes):
    if lanes is None:
        return (slice(None), number)
    return (slice(None), number, slice(None), pl.ds(lanes, DEC))


def gather_plan(spots):
    plan = []
    crops = lax.axis_size("crop")
    for side in range(2):
        for shift in range(crops):
            for number, lanes, target, spot in spots:
                plan.append(
                    (
                        side * crops + shift,
                        lambda crop, core, number=number, lanes=lanes: pack_at(number, lanes),
                        target,
                        lambda crop, core, side=side, shift=shift, spot=spot: chunk_at(
                            spot, crop ^ shift, core ^ side
                        ),
                    )
                )
    return plan


def core_swap(pieces):
    return [lax.ppermute(piece, "core", SWAP) for piece in pieces]


def scatter_plan(spots):
    plan = []
    for side in range(2):
        for shift in range(lax.axis_size("crop")):
            for number, lanes, source, spot in spots:
                plan.append(
                    (
                        source,
                        lambda crop, core, side=side, shift=shift, spot=spot: chunk_at(
                            spot, crop ^ shift, core ^ side
                        ),
                        side,
                        lambda crop, core, shift=shift, number=number, lanes=lanes: (shift,)
                        + pack_at(number, lanes),
                    )
                )
    return plan


def scatter_cores(weights, spots, chunks):
    crops, layers = lax.axis_size("crop"), lax.axis_size("z")
    shape = (crops, layers, chunks, weights[0].shape[3], D)
    return moves(scatter_plan(spots), weights, [shape, shape])


def core_sum(keep, send):
    got = lax.ppermute(send, "core", SWAP)
    return [
        (keep[shift].astype(jnp.float32) + got[shift].astype(jnp.float32)).astype(jnp.bfloat16)
        for shift in range(keep.shape[0])
    ]


def row_pad(rows, count):
    return jnp.pad(rows, ((0, count - rows.shape[0]), (0, 0)))


def slab_trim(full, piece, size):
    layers, cores, crops = full.shape[:3]
    rows = full.reshape(layers * cores, crops, -1, DEC)[:, :, :piece]
    return rows.reshape(layers * cores, -1, DEC)[:, :size].reshape(-1, DEC)


def slab_fill(full, piece, chunks, rows):
    layers, crops = lax.axis_size("z"), lax.axis_size("crop")
    shaped = full.reshape(2 * layers, -1, DEC)
    shaped = jnp.pad(shaped, ((0, 0), (0, crops * piece - shaped.shape[1]), (0, 0)))
    shaped = shaped.reshape(2 * layers, crops, piece, DEC)
    shaped = jnp.pad(shaped, ((0, 0), (0, 0), (0, chunks * rows - piece), (0, 0)))
    return shaped.reshape(layers, 2, crops, chunks, rows, DEC)


def to_units(rows, unit):
    crops, size = rows.shape[0], rows.shape[1] * rows.shape[2]
    flat = jnp.pad(rows.reshape(crops, size), ((0, 0), (0, -size % unit)))
    return flat.reshape(crops, -1, unit)


def from_units(units, rows, width):
    return units.reshape(units.shape[0], -1)[:, : rows * width].reshape(-1, rows, width)


def after(value, earlier):
    return lax.optimization_barrier((value, earlier))[0]


def z_sum(pack):
    own = lax.axis_index("z")
    pieces = [
        lax.dynamic_index_in_dim(pack, own ^ shift, 0, keepdims=False)
        for shift in range(pack.shape[0])
    ]
    return total_of(flips_of(pieces, "z")).astype(jnp.bfloat16)


def neighbours(volume):
    count = lax.axis_size(SLAB)
    forward = [(i, i + 1) for i in range(count - 1)]
    backward = [(target, source) for source, target in forward]
    low = lax.ppermute(volume[:, -1:], SLAB, forward)
    high = lax.ppermute(volume[:, :1], SLAB, backward)
    return low, high


def with_planes(volume, rims):
    low, high = rims
    return jnp.concatenate([low.astype(volume.dtype), volume, high.astype(volume.dtype)], axis=1)


def inside(rimmed):
    place, last = lax.axis_index(SLAB), lax.axis_size(SLAB) - 1
    plane = lax.broadcasted_iota(jnp.int32, rimmed.shape, 1)
    outside = ((plane == 0) & (place == 0)) | (
        (plane == rimmed.shape[1] - 1) & (place == last)
    )
    return jnp.where(outside, jnp.zeros((), rimmed.dtype), rimmed)


def columns(rimmed):
    padded = jnp.pad(rimmed, ((0, 0), (0, 0), (1, 1), (1, 1), (0, 0)))
    crop_count, layers, breadth = (rimmed.shape[0], rimmed.shape[1] - 2, rimmed.shape[2])
    pieces = [
        padded[
            :,
            shift_z : shift_z + layers,
            shift_y : shift_y + breadth,
            shift_x : shift_x + breadth,
            :,
        ]
        for shift_z in range(3)
        for shift_y in range(3)
        for shift_x in range(3)
    ]
    return jnp.concatenate(pieces, -1).reshape(crop_count * layers * breadth * breadth, -1)


def back_conv(grad_rimmed, kernel, inputs):
    outputs = kernel.shape[1]
    flipped = (
        kernel.reshape(27, inputs, outputs)[::-1].transpose(0, 2, 1).reshape(27 * outputs, inputs)
    )
    crop_count, planes, breadth = grad_rimmed.shape[:3]
    return matmul(columns(grad_rimmed), flipped).reshape(
        crop_count, planes - 2, breadth, breadth, inputs
    )


def slab_totals(first, second):
    both = jnp.stack([jnp.sum(first, (1, 2, 3)), jnp.sum(second, (1, 2, 3))])
    return slab_sum(both)


def over_voxels(values):
    return values[:, None, None, None, :]


def norm_scales(values, voxel_count):
    totals = slab_totals(values, values * values)
    average = totals[0] / voxel_count
    inverse = lax.rsqrt(totals[1] / voxel_count - average * average + 1e-05)
    return over_voxels(average), over_voxels(inverse)


def norm_slopes(grad, normed, voxel_count):
    totals = slab_totals(grad, grad * normed)
    return over_voxels(totals[0] / voxel_count), over_voxels(totals[1] / voxel_count)


def heads_out(block, parts):
    crop_count, tokens = block.shape[0], block.shape[1]
    slab_count = lax.axis_size(SLAB)
    shaped = block.reshape(crop_count, tokens, parts, HEADS, HDIM).transpose(0, 3, 1, 2, 4)
    shaped = shaped.reshape(crop_count * HEADS, tokens, parts * HDIM)
    spare = -shaped.shape[0] % slab_count
    shaped = jnp.pad(shaped, ((0, spare), (0, 0), (0, 0)))
    return lax.all_to_all(shaped, SLAB, 0, 1, tiled=True)


def heads_back(block, crop_count, parts):
    shaped = lax.all_to_all(block, SLAB, 1, 0, tiled=True)[: crop_count * HEADS]
    tokens = shaped.shape[1]
    shaped = shaped.reshape(crop_count, HEADS, tokens, parts, HDIM).transpose(0, 2, 3, 1, 4)
    return shaped.reshape(crop_count * tokens, parts * D)


def to_volume(lifted, crop_count):
    layers = lifted.shape[0] // (crop_count * SIDE * SIDE)
    shaped = lifted.reshape(crop_count, layers, SIDE, SIDE, 2, 2, 2, DEC)
    return shaped.transpose(0, 1, 4, 2, 5, 3, 6, 7).reshape(
        crop_count, 2 * layers, 2 * SIDE, 2 * SIDE, DEC
    )


def to_tokens(volume):
    crop_count, layers = (volume.shape[0], volume.shape[1] // 2)
    shaped = volume.reshape(crop_count, layers, 2, SIDE, 2, SIDE, 2, DEC)
    return shaped.transpose(0, 1, 3, 5, 2, 4, 6, 7).reshape(
        crop_count * layers * SIDE * SIDE, 8 * DEC
    )


def adam_update(weight, gradient, mean_old, square_old, factor, step_rate, step_decay):
    clipped = gradient * factor
    mean_new = BETA_ONE * mean_old + (1.0 - BETA_ONE) * clipped
    square_new = BETA_TWO * square_old + (1.0 - BETA_TWO) * clipped * clipped
    direction = (
        mean_new
        / (1.0 - BETA_ONE**STEP)
        / (jnp.sqrt(square_new / (1.0 - BETA_TWO**STEP)) + EPSILON)
    )
    return (weight - step_rate * (direction + step_decay * weight), mean_new, square_new)


def local(
    patches,
    modality,
    skip_feats,
    cotangent,
    embedding,
    attention_in,
    attention_out,
    expand_up,
    expand_down,
    upsample,
    convolve_one,
    convolve_two,
    positions,
    vectors,
    embedding_mean,
    attention_in_mean,
    attention_out_mean,
    expand_up_mean,
    expand_down_mean,
    upsample_mean,
    convolve_one_mean,
    convolve_two_mean,
    positions_mean,
    vectors_mean,
    embedding_square,
    attention_in_square,
    attention_out_square,
    expand_up_square,
    expand_down_square,
    upsample_square,
    convolve_one_square,
    convolve_two_square,
    positions_square,
    vectors_square,
):
    shards = (
        embedding,
        attention_in,
        attention_out,
        expand_up,
        expand_down,
        upsample,
        convolve_one,
        convolve_two,
        positions,
        vectors,
    )
    means_in = (
        embedding_mean,
        attention_in_mean,
        attention_out_mean,
        expand_up_mean,
        expand_down_mean,
        upsample_mean,
        convolve_one_mean,
        convolve_two_mean,
        positions_mean,
        vectors_mean,
    )
    squares_in = (
        embedding_square,
        attention_in_square,
        attention_out_square,
        expand_up_square,
        expand_down_square,
        upsample_square,
        convolve_one_square,
        convolve_two_square,
        positions_square,
        vectors_square,
    )
    step_rates = (RATE,) * 9 + (VECTOR_RATE,)
    step_decays = (DECAY,) * 9 + (VECTOR_DECAY,)
    crops = lax.axis_size("crop")
    layers = lax.axis_size("z")
    slab_count = 2 * layers
    crop_batch = patches.shape[0]
    local_tokens = patches.shape[1] * patches.shape[2]
    rows_in = crop_batch * local_tokens
    voxel_count = skip_feats.shape[1] * skip_feats.shape[2] * skip_feats.shape[3] * slab_count
    score_scale = HDIM ** (-0.5)
    unit = D // crops

    lows = [entry.astype(jnp.bfloat16) for entry in shards]
    embed_rows = embedding.shape[0]
    share = embed_rows // crops
    block = math.gcd(share, PATCH)
    groups = share // block
    row_count = attention_in.shape[0] // crops
    down_count = expand_down.shape[0] // crops
    embed_wide = (
        lows[0].reshape(groups, crops, block, unit).transpose(1, 0, 2, 3).reshape(crops, share, unit)
    )
    first_count = -(-convolve_one.shape[0] // crops)
    second_count = -(-convolve_two.shape[0] // crops)
    narrow = jnp.concatenate(
        [
            jnp.pad(lows[6], ((0, crops * first_count - lows[6].shape[0]), (0, 0))).reshape(
                crops, first_count, -1
            ),
            jnp.pad(lows[7], ((0, crops * second_count - lows[7].shape[0]), (0, 0))).reshape(
                crops, second_count, -1
            ),
        ],
        1,
    )
    up_rows = expand_up.shape[0]
    class_size = FF // crops
    per_class = class_size // crops
    up_units = lows[3].reshape(up_rows, -1, crops, down_count).transpose(2, 0, 1, 3)
    up_units = to_units(up_units.reshape(crops, up_rows, per_class), unit)
    lift_units = to_units(lows[5].reshape(crops, row_count, -1), unit)
    narrow_units = to_units(narrow, unit)
    wide = jnp.concatenate(
        [
            lows[1].reshape(crops, row_count, 3, unit).transpose(0, 2, 1, 3).reshape(crops, -1, unit),
            lows[2].reshape(crops, row_count, unit),
            up_units,
            lows[4].reshape(crops, down_count, unit),
            jnp.broadcast_to(lows[8][None], (crops,) + lows[8].shape),
            lift_units,
            narrow_units,
        ],
        1,
    )
    pieces = (CHANS * PATCH) // (block * crops)
    ct_size = PATCH // crops
    own_crop = lax.axis_index("crop")
    own_mri = jnp.broadcast_to(
        (modality == 1)[:, None, None], (crop_batch, local_tokens, 1)
    ).reshape(-1, 1)
    marks = jnp.broadcast_to(own_mri.astype(jnp.float32), (rows_in, 128))
    is_mri = jnp.concatenate(flips(marks, "crop"), 0)[:, :1] > 0.5
    lanes = pieces * block
    if block % 128 == 0:
        pixels = moves(
            column_plan(pieces, block, True),
            [patches.reshape(rows_in, crops * lanes)],
            [(rows_in, lanes)] * crops,
        )
    else:
        pixels = patches.reshape(rows_in, pieces, crops, block).transpose(2, 0, 1, 3)
        pixels = pixels.reshape(crops, rows_in, lanes)
        pixels = [
            lax.dynamic_index_in_dim(pixels, own_crop ^ shift, 0, keepdims=False)
            for shift in range(crops)
        ]
    pixel_parts = flips_of(list(pixels), "crop")
    wide = crop_swap(wide)
    embed_part = crop_swap(after(embed_wide, (wide, is_mri)))
    embed_part = embed_part.transpose(1, 0, 2).reshape(share, D)
    marks = []
    edge = 0
    for size in (3 * row_count, row_count, up_units.shape[1], down_count, lows[8].shape[0],
                 lift_units.shape[1], narrow_units.shape[1]):
        marks.append(wide[:, edge : edge + size])
        edge += size
    lift_rows = from_units(marks[5], row_count, 8 * DEC // crops)
    narrow = from_units(marks[6], first_count + second_count, DEC // crops)
    triple_part = marks[0].reshape(3, crops, row_count, unit).transpose(0, 2, 1, 3).reshape(-1, D)
    output_part = marks[1].transpose(1, 0, 2).reshape(row_count, D)
    up_part = from_units(marks[2], up_rows, per_class).transpose(1, 0, 2).reshape(-1, D)
    down_part = marks[3].transpose(1, 0, 2).reshape(down_count, D)
    position_rows = marks[4].transpose(1, 0, 2).reshape(-1, D).astype(jnp.float32)
    lift_part = (
        lift_rows.transpose(1, 0, 2).reshape(row_count, 8, DEC).transpose(1, 0, 2).reshape(-1, DEC)
    )
    narrow_part = narrow.transpose(1, 0, 2).reshape(-1, DEC)
    first_chunks, second_chunks = -(-first_count // row_count), -(-second_count // row_count)
    slim = jnp.concatenate(
        [
            lift_part,
            row_pad(narrow_part[:first_count], first_chunks * row_count),
            row_pad(narrow_part[first_count:], second_chunks * row_count),
        ],
        0,
    )
    slim_chunks = -(-(8 + first_chunks + second_chunks) // 6)
    slim = row_pad(slim, 6 * slim_chunks * row_count)
    slim = slim.reshape(slim_chunks, 6, row_count, DEC).transpose(0, 2, 1, 3).reshape(-1, D)
    vector_size = vectors.shape[0]
    vector_part = jnp.pad(lows[9][None], ((0, row_count - 1), (0, D - vector_size)))

    quarter = 6
    packs = jnp.concatenate([triple_part, output_part, vector_part, slim], 0)
    packs = lax.all_gather(packs.reshape(-1, row_count, D), "z", axis=0)
    packs = after(packs, pixel_parts)
    pack_one, pack_slim = packs[:, :5], packs[:, 5:]
    embed_full = lax.all_gather(embed_part, SLAB, axis=0, tiled=True)
    up_size = up_part.shape[0]
    ff_part = after(jnp.concatenate([up_part, down_part], 0), embed_part)
    ff_full = lax.all_gather(ff_part, SLAB, axis=0)
    up_full = ff_full[:, :up_size].reshape(D, class_size)
    down_full = ff_full[:, up_size:].reshape(class_size, D)
    one_spots = [
        (0, None, 0, ("lane", 0, D)),
        (1, None, 0, ("lane", 1, D)),
        (2, None, 0, ("lane", 2, D)),
        (3, None, 1, ("lane", 0, D)),
        (4, None, 2, ("lane", 0, D)),
    ]
    slim_list = [(0, ("lane", k, DEC)) for k in range(8)]
    slim_list += [(1, ("row", k, DEC)) for k in range(first_chunks)]
    slim_list += [(2, ("row", k, DEC)) for k in range(second_chunks)]
    slim_spots = [
        (number // quarter, number % quarter * DEC, target, spot)
        for number, (target, spot) in enumerate(slim_list)
    ]
    lead = (layers, 2, crops)
    none = jnp.zeros((), jnp.bfloat16)
    one_own = flips(pack_one, "crop")
    pixels = jnp.concatenate(pixel_parts, 0)
    pixel_rows = jnp.concatenate(
        [jnp.where(is_mri, none, pixels[:, :ct_size]), jnp.where(is_mri, pixels, none)], 1
    )
    partial = matmul(pixel_rows, embed_full).astype(jnp.bfloat16)
    product = total_of(flips_of(list(partial.reshape(crops, rows_in, D)), "crop"))
    one_other = core_swap(after(one_own, partial))
    triple_full, output_full, vector_full = moves(
        gather_plan(one_spots),
        one_own + one_other,
        [lead + (row_count, 3 * D), lead + (row_count, D), lead + (row_count, D)],
    )
    triple_full = triple_full.reshape(D, 3 * D)
    output_full = output_full.reshape(D, D)
    vector_full = vector_full[:, :, :, 0, :vector_size].transpose(2, 0, 1, 3).reshape(12 * D)
    vector_rows = vector_full.astype(jnp.float32).reshape(12, D)
    embedded = (
        product
        + jnp.where(own_mri, vector_rows[7], vector_rows[6])
        + jnp.concatenate([position_rows] * crop_batch, 0)
    )
    normed_one, pull_one = jax.vjp(layer_norm, embedded, vector_rows[0], vector_rows[1])
    normed_one = normed_one.astype(jnp.bfloat16)
    triple = matmul(normed_one, triple_full).astype(jnp.bfloat16)
    triple = heads_out(triple.reshape(crop_batch, local_tokens, 3 * D), 3)
    query, keys, values = triple[..., :HDIM], triple[..., HDIM : 2 * HDIM], triple[..., 2 * HDIM :]
    scores = (
        jnp.einsum("pqd,pkd->pqk", query, keys, preferred_element_type=jnp.float32) * score_scale
    )
    probs = jax.nn.softmax(scores, axis=-1)
    probs_low = probs.astype(jnp.bfloat16)
    mixed = jnp.einsum("pqk,pkd->pqd", probs_low, values, preferred_element_type=jnp.float32)
    slim_own = flips(pack_slim, "crop")
    mixed = after(mixed.astype(jnp.bfloat16), slim_own)
    mixed = heads_back(mixed, crop_batch, 1)
    slim_other = core_swap(slim_own)
    hidden_one = embedded + matmul(mixed, output_full) + vector_rows[4]
    hidden_one = after(hidden_one, slim_other)
    lift_full, first_full, second_full = moves(
        gather_plan(slim_spots),
        slim_own + slim_other,
        [
            lead + (row_count, 8 * DEC),
            lead + (first_chunks, row_count, DEC),
            lead + (second_chunks, row_count, DEC),
        ],
    )
    lift_full = lift_full.reshape(D, 8 * DEC)
    first_full = slab_trim(first_full, first_count, convolve_one.shape[0])
    second_full = slab_trim(second_full, second_count, convolve_two.shape[0])
    normed_two, pull_two = jax.vjp(layer_norm, hidden_one, vector_rows[2], vector_rows[3])
    normed_two = normed_two.astype(jnp.bfloat16)
    normed_all = jnp.concatenate(flips(normed_two, "crop"), 0)
    bias_class = vector_rows[8:].reshape(slab_count, crops, down_count)
    bias_class = lax.dynamic_index_in_dim(bias_class, own_crop, 1, keepdims=False).reshape(-1)
    inner = matmul(normed_all, up_full) + bias_class
    activated = gelu_exact(inner).astype(jnp.bfloat16)
    partial = matmul(activated, down_full).astype(jnp.bfloat16).reshape(crops, rows_in, D)
    product = total_of(flips_of(list(partial), "crop"))
    hidden_two = hidden_one + product + vector_rows[5]
    hidden_low = hidden_two.astype(jnp.bfloat16)
    volume = to_volume(matmul(hidden_low, lift_full), crop_batch)
    joined = jnp.concatenate([volume.astype(jnp.bfloat16), skip_feats], -1)
    joined = with_planes(joined, neighbours(joined))
    volume_rimmed = with_planes(
        volume, (joined[:, :1, ..., :DEC], joined[:, -1:, ..., :DEC])
    )
    target_rimmed = with_planes(cotangent, neighbours(cotangent)).astype(jnp.float32)
    cols_one = columns(joined)
    conv_one = matmul(cols_one, first_full).reshape(volume.shape)
    conv_one_rimmed = with_planes(conv_one, neighbours(conv_one.astype(jnp.bfloat16)))
    average_a, inverse_a = norm_scales(conv_one, voxel_count)
    normed_a = (conv_one_rimmed - average_a) * inverse_a
    first_act = inside(gelu_exact(normed_a).astype(jnp.bfloat16))
    cols_two = columns(first_act)
    conv_two = matmul(cols_two, second_full).reshape(volume.shape)
    conv_two_rimmed = with_planes(conv_two, neighbours(conv_two.astype(jnp.bfloat16)))
    average_b, inverse_b = norm_scales(conv_two, voxel_count)
    normed_b = (conv_two_rimmed - average_b) * inverse_b
    before = normed_b + volume_rimmed
    block_output = gelu_exact(before[:, 1:-1]).astype(jnp.bfloat16)

    grad_before = target_rimmed * gelu_slope(before)
    mean_b, slope_b = norm_slopes(grad_before[:, 1:-1], normed_b[:, 1:-1], voxel_count)
    grad_conv_two = inverse_b * (grad_before - mean_b - normed_b * slope_b)
    grad_conv_two = inside(grad_conv_two.astype(jnp.bfloat16))
    weight_second = matmul_left_t(cols_two, grad_conv_two[:, 1:-1].reshape(-1, DEC))
    grad_first = back_conv(grad_conv_two, second_full, DEC) * gelu_slope(normed_a[:, 1:-1])
    grad_first_rimmed = with_planes(grad_first, neighbours(grad_first.astype(jnp.bfloat16)))
    mean_a, slope_a = norm_slopes(grad_first, normed_a[:, 1:-1], voxel_count)
    grad_conv_one = inverse_a * (grad_first_rimmed - mean_a - normed_a * slope_a)
    grad_conv_one = inside(grad_conv_one.astype(jnp.bfloat16))
    weight_first = matmul_left_t(cols_one, grad_conv_one[:, 1:-1].reshape(-1, DEC))
    grad_joined = back_conv(grad_conv_one, first_full, 2 * DEC)
    skip_grad = grad_joined[..., DEC:].astype(jnp.bfloat16)
    grad_lifted = to_tokens(grad_before[:, 1:-1] + grad_joined[..., :DEC]).astype(jnp.bfloat16)
    weight_lift = matmul_left_t(hidden_low, grad_lifted)
    grad_hidden = matmul_right_t(grad_lifted, lift_full)
    bias_down = jnp.sum(grad_hidden, 0)
    grad_branch = grad_hidden.astype(jnp.bfloat16)
    grad_all = jnp.concatenate(flips(grad_branch, "crop"), 0)
    grad_inner = matmul_right_t(grad_all, down_full) * gelu_slope(inner)
    bias_up = jnp.sum(grad_inner, 0)
    grad_inner_low = grad_inner.astype(jnp.bfloat16)
    partial = matmul_right_t(grad_inner_low, up_full).astype(jnp.bfloat16)
    partial = partial.reshape(crops, rows_in, D)
    weight_down = matmul_left_t(activated, grad_all).astype(jnp.bfloat16)
    weight_up = matmul_left_t(normed_all, grad_inner_low).astype(jnp.bfloat16)
    ff_grads = jnp.concatenate(
        [weight_up.reshape(slab_count, -1, D), weight_down.reshape(slab_count, -1, D)], 1
    ).reshape(-1, D)

    slim_move = scatter_cores(
        [
            weight_lift.astype(jnp.bfloat16).reshape(lead + (row_count, 8 * DEC)),
            slab_fill(weight_first.astype(jnp.bfloat16), first_count, first_chunks, row_count),
            slab_fill(weight_second.astype(jnp.bfloat16), second_count, second_chunks, row_count),
        ],
        slim_spots,
        slim_chunks,
    )
    slim_parts = core_sum(*slim_move)
    partial = after(partial, slim_move[1])
    back_two = pull_two(total_of(flips_of(list(partial), "crop")))
    grad_hidden = grad_hidden + back_two[0]
    bias_out = jnp.sum(grad_hidden, 0)
    grad_branch = grad_hidden.astype(jnp.bfloat16)
    weight_out = matmul_left_t(mixed, grad_branch)
    grad_mixed = matmul_right_t(grad_branch, output_full).astype(jnp.bfloat16)
    grad_mixed = after(grad_mixed, slim_parts)
    slim_got = flips_of(slim_parts, "crop")
    grad_mixed = heads_out(grad_mixed.reshape(crop_batch, local_tokens, D), 1)
    grad_probs = jnp.einsum(
        "pqd,pkd->pqk", grad_mixed, values, preferred_element_type=jnp.float32
    )
    centre = jnp.sum(probs * grad_probs, -1, keepdims=True)
    grad_scores = (probs * (grad_probs - centre)).astype(jnp.bfloat16)
    grad_query = (
        jnp.einsum("pqk,pkd->pqd", grad_scores, keys, preferred_element_type=jnp.float32)
        * score_scale
    )
    grad_keys = (
        jnp.einsum("pqk,pqd->pkd", grad_scores, query, preferred_element_type=jnp.float32)
        * score_scale
    )
    grad_values = jnp.einsum(
        "pqk,pqd->pkd", probs_low, grad_mixed, preferred_element_type=jnp.float32
    )
    grad_triple = jnp.concatenate([grad_query, grad_keys, grad_values], -1).astype(jnp.bfloat16)
    grad_triple = heads_back(grad_triple, crop_batch, 3)
    grad_triple = after(grad_triple, slim_got)
    ff_grads = after(ff_grads, grad_triple)
    ff_sum = lax.psum_scatter(ff_grads, SLAB, scatter_dimension=0, tiled=True)
    weight_triple = matmul_left_t(normed_one, grad_triple)
    back_one = pull_one(matmul_right_t(grad_triple, triple_full))
    grad_hidden = grad_hidden + back_one[0]
    grad_low = grad_hidden.astype(jnp.bfloat16)

    grad_rows = jnp.concatenate(flips(grad_low, "crop"), 0)
    weight_embed = matmul_left_t(pixel_rows, grad_rows).astype(jnp.bfloat16)
    slim_sum = total_of(after(slim_got, weight_embed)).astype(jnp.bfloat16)
    embed_sum = lax.psum_scatter(after(weight_embed, ff_sum), SLAB, scatter_dimension=0, tiled=True)
    pixel_grad = matmul_right_t(after(grad_rows, weight_embed), embed_full)
    ct_grad = jnp.pad(pixel_grad[:, :ct_size], ((0, 0), (0, (CHANS - 1) * ct_size)))
    pixel_grad = jnp.where(is_mri, pixel_grad[:, ct_size:], ct_grad).astype(jnp.bfloat16)
    bias_ct = jnp.sum(jnp.where(own_mri, 0.0, grad_hidden), 0)
    bias_mri = jnp.sum(jnp.where(own_mri, grad_hidden, 0.0), 0)
    position_grad = jnp.sum(grad_hidden.reshape(crop_batch, local_tokens, D), 0)
    position_grad = position_grad.astype(jnp.bfloat16).reshape(-1, crops, unit).swapaxes(0, 1)
    position_grad = [
        lax.dynamic_index_in_dim(position_grad, own_crop ^ shift, 0, keepdims=False)
        for shift in range(crops)
    ]
    position_grad = total_of(flips_of(position_grad, "crop"))
    at_class = lax.broadcasted_iota(jnp.int32, (slab_count, crops, down_count), 1) == own_crop
    bias_full = jnp.where(at_class, bias_up.reshape(slab_count, 1, down_count), 0.0)
    vector_grad = jnp.concatenate(
        [
            jnp.stack(
                [
                    back_one[1],
                    back_one[2],
                    back_two[1],
                    back_two[2],
                    bias_out,
                    bias_down,
                    bias_ct,
                    bias_mri,
                ]
            ),
            bias_full.reshape(4, D),
        ],
        0,
    ).astype(jnp.bfloat16)
    vector_pack = vector_grad.reshape(crops, layers, 2, 1, vector_size).transpose(1, 2, 0, 3, 4)
    vector_pack = jnp.pad(
        vector_pack, ((0, 0),) * 3 + ((0, row_count - 1), (0, D - vector_size))
    )
    weight_triple = after(weight_triple.astype(jnp.bfloat16), weight_embed)
    one_parts = core_sum(*scatter_cores(
        [
            weight_triple.reshape(lead + (row_count, 3 * D)),
            weight_out.astype(jnp.bfloat16).reshape(lead + (row_count, D)),
            vector_pack,
        ],
        one_spots,
        5,
    ))
    one_got = flips_of(one_parts, "crop")
    one_sum = total_of(one_got).astype(jnp.bfloat16)
    pixel_got = flips_of(
        after(list(pixel_grad.reshape(crops, rows_in, pieces * block)), one_got), "crop"
    )
    if block % 128 == 0:
        (patch_grad,) = moves(
            column_plan(pieces, block, False), pixel_got, [(rows_in, crops * lanes)]
        )
    else:
        pixel_got = jnp.stack(pixel_got)
        patch_grad = jnp.stack(
            [
                lax.dynamic_index_in_dim(pixel_got, own_crop ^ part, 0, keepdims=False)
                for part in range(crops)
            ]
        )
        patch_grad = patch_grad.reshape(crops, rows_in, pieces, block).transpose(1, 2, 0, 3)
    patch_grad = patch_grad.reshape(patches.shape)

    def by_units(rows, chunks):
        shaped = rows.reshape(chunks, -1, crops, unit).transpose(0, 2, 1, 3)
        return shaped.reshape(crops, -1, unit)

    def join_units(got, chunks):
        return (
            got.reshape(crops, chunks, -1, unit).transpose(0, 2, 1, 3).reshape(-1, chunks * unit)
        )

    slim_all = z_sum(slim_sum).reshape(slim_chunks, row_count, 6, DEC)
    sum_one = z_sum(one_sum).reshape(-1, D)

    slim_all = slim_all.transpose(0, 2, 1, 3).reshape(-1, DEC)
    first_start = 8 * row_count
    second_start = first_start + first_chunks * row_count
    lift_sum = slim_all[:first_start].reshape(8, row_count, DEC).transpose(1, 0, 2)
    lift_sum = lift_sum.reshape(row_count, crops, -1).transpose(1, 0, 2)
    narrow_sum = jnp.concatenate(
        [
            slim_all[first_start : first_start + first_count],
            slim_all[second_start : second_start + second_count],
        ],
        0,
    )
    narrow_sum = narrow_sum.reshape(-1, crops, DEC // crops).transpose(1, 0, 2)
    lift_units, narrow_units = to_units(lift_sum, unit), to_units(narrow_sum, unit)
    up_units = ff_sum[:up_size].reshape(up_rows, crops, per_class).transpose(1, 0, 2)
    up_units = to_units(up_units, unit)
    wide = jnp.concatenate(
        [
            up_units,
            by_units(ff_sum[up_size:], 1),
            by_units(sum_one[: 3 * row_count], 3),
            by_units(sum_one[3 * row_count : 4 * row_count], 1),
            lift_units,
            narrow_units,
            by_units(embed_sum, 1),
        ],
        1,
    )
    local_sum = jnp.float32(0.0)
    for gradient in (embed_sum, ff_sum, lift_sum, narrow_sum, sum_one, position_grad):
        wide_grad = gradient.astype(jnp.float32)
        local_sum = local_sum + jnp.sum(wide_grad * wide_grad)
    wide = crop_swap(after(wide, local_sum)).astype(jnp.float32)
    embed_got = wide[:, -share:]
    embed_grad = (
        embed_got.astype(jnp.float32).reshape(crops, groups, block, unit).transpose(1, 0, 2, 3).reshape(-1, unit)
    )
    marks = []
    edge = 0
    for size in (up_units.shape[1], down_count, 3 * row_count, row_count,
                 lift_units.shape[1], narrow_units.shape[1]):
        marks.append(wide[:, edge : edge + size])
        edge += size
    up_grad = from_units(marks[0], up_rows, per_class)
    up_grad = up_grad.reshape(crops, up_rows, -1, down_count).transpose(1, 2, 0, 3)
    up_grad = up_grad.reshape(expand_up.shape)
    down_grad = join_units(marks[1], 1)
    triple_grad = join_units(marks[2], 3)
    output_grad = join_units(marks[3], 1)
    lift_grad = from_units(marks[4], row_count, 8 * DEC // crops).reshape(upsample.shape)
    narrow_got = from_units(marks[5], first_count + second_count, DEC // crops)
    first_grad = narrow_got[:, :first_count].reshape(-1, DEC // crops)[: convolve_one.shape[0]]
    second_grad = narrow_got[:, first_count:].reshape(-1, DEC // crops)[: convolve_two.shape[0]]
    vector_final = sum_one[4 * row_count, :vector_size].astype(jnp.float32)
    gradients = (
        embed_grad,
        triple_grad,
        output_grad,
        up_grad,
        down_grad,
        lift_grad,
        first_grad,
        second_grad,
        position_grad,
        vector_final,
    )
    grad_norm = jnp.sqrt(slab_sum(total_of(flips(local_sum.reshape(1, 1), "crop"))))[0, 0]
    factor = jnp.minimum(1.0, CLIP / grad_norm)
    news, means, squares = ([], [], [])
    for weight, gradient, mean_old, square_old, step_rate, step_decay in zip(
        shards, gradients, means_in, squares_in, step_rates, step_decays
    ):
        weight_new, mean_new, square_new = adam_update(
            weight, gradient, mean_old, square_old, factor, step_rate, step_decay
        )
        news.append(weight_new)
        means.append(mean_new)
        squares.append(square_new)
    return (
        block_output,
        patch_grad,
        skip_grad,
        grad_norm,
        news[0],
        news[1],
        news[2],
        news[3],
        news[4],
        news[5],
        news[6],
        news[7],
        news[8],
        news[9],
        means[0],
        means[1],
        means[2],
        means[3],
        means[4],
        means[5],
        means[6],
        means[7],
        means[8],
        means[9],
        squares[0],
        squares[1],
        squares[2],
        squares[3],
        squares[4],
        squares[5],
        squares[6],
        squares[7],
        squares[8],
        squares[9],
    )


def solution(mesh):
    crops, slabs = mesh.devices.shape
    mesh = Mesh(mesh.devices.reshape(crops, slabs // 2, 2), ("crop", "z", "core"))
    return jax.shard_map(
        local,
        mesh=mesh,
        in_specs=(
            P("crop", ("z", "core"), None, None),
            P("crop"),
            P("crop", ("z", "core"), None, None, None),
            P("crop", ("z", "core"), None, None, None),
            P(("z", "core"), "crop"),
            P(("z", "core"), "crop"),
            P(("z", "core"), "crop"),
            P(("z", "core"), "crop"),
            P(("z", "core"), "crop"),
            P(("z", "core"), "crop"),
            P(("z", "core"), "crop"),
            P(("z", "core"), "crop"),
            P(("z", "core"), "crop"),
            P(("crop", "z", "core")),
            P(("z", "core"), "crop"),
            P(("z", "core"), "crop"),
            P(("z", "core"), "crop"),
            P(("z", "core"), "crop"),
            P(("z", "core"), "crop"),
            P(("z", "core"), "crop"),
            P(("z", "core"), "crop"),
            P(("z", "core"), "crop"),
            P(("z", "core"), "crop"),
            P(("crop", "z", "core")),
            P(("z", "core"), "crop"),
            P(("z", "core"), "crop"),
            P(("z", "core"), "crop"),
            P(("z", "core"), "crop"),
            P(("z", "core"), "crop"),
            P(("z", "core"), "crop"),
            P(("z", "core"), "crop"),
            P(("z", "core"), "crop"),
            P(("z", "core"), "crop"),
            P(("crop", "z", "core")),
        ),
        out_specs=(
            P("crop", ("z", "core"), None, None, None),
            P("crop", ("z", "core"), None, None),
            P("crop", ("z", "core"), None, None, None),
            P(),
            P(("z", "core"), "crop"),
            P(("z", "core"), "crop"),
            P(("z", "core"), "crop"),
            P(("z", "core"), "crop"),
            P(("z", "core"), "crop"),
            P(("z", "core"), "crop"),
            P(("z", "core"), "crop"),
            P(("z", "core"), "crop"),
            P(("z", "core"), "crop"),
            P(("crop", "z", "core")),
            P(("z", "core"), "crop"),
            P(("z", "core"), "crop"),
            P(("z", "core"), "crop"),
            P(("z", "core"), "crop"),
            P(("z", "core"), "crop"),
            P(("z", "core"), "crop"),
            P(("z", "core"), "crop"),
            P(("z", "core"), "crop"),
            P(("z", "core"), "crop"),
            P(("crop", "z", "core")),
            P(("z", "core"), "crop"),
            P(("z", "core"), "crop"),
            P(("z", "core"), "crop"),
            P(("z", "core"), "crop"),
            P(("z", "core"), "crop"),
            P(("z", "core"), "crop"),
            P(("z", "core"), "crop"),
            P(("z", "core"), "crop"),
            P(("z", "core"), "crop"),
            P(("crop", "z", "core")),
        ),
        check_vma=False,
    )
```

```python
import math

import jax
import jax.numpy as jnp
from jax import lax
from jax.experimental import pallas as pl
from jax.experimental.pallas import tpu as pltpu
from jax.sharding import Mesh
from jax.sharding import PartitionSpec as P

D = 768
HEADS = 12
HDIM = 64
FF = 3072
PATCH = 4096
CHANS = 4
DEC = 128
SIDE = 8
STEP = 10


BETA_ONE = 0.9
BETA_TWO = 0.95
RATE = 0.07
DECAY = 0.05
VECTOR_RATE = 0.4
VECTOR_DECAY = 0.0
EPSILON = 1e-08
CLIP = 1.0
CONTRACT_ROWS = (((0,), (0,)), ((), ()))
CONTRACT_COLS = (((1,), (1,)), ((), ()))


def layer_norm(values, gain, shift):
    center = values - jnp.mean(values, -1, keepdims=True)
    spread = jnp.mean(center * center, -1, keepdims=True)
    return center * lax.rsqrt(spread + 1e-06) * gain + shift


def gelu_exact(values):
    return jax.nn.gelu(values, approximate=False)


def gelu_slope(values):
    return (
        0.5 * (1.0 + lax.erf(values * 0.7071067811865476))
        + values * jnp.exp(-0.5 * values * values) * 0.3989422804014327
    )


def matmul(left, right):
    return jnp.dot(left, right, preferred_element_type=jnp.float32)


def matmul_left_t(left, right):
    return lax.dot_general(left, right, CONTRACT_ROWS, preferred_element_type=jnp.float32)


def matmul_right_t(left, right):
    return lax.dot_general(left, right, CONTRACT_COLS, preferred_element_type=jnp.float32)


SLAB = ("z", "core")
SWAP = [(0, 1), (1, 0)]


def flip_pairs(count, step):
    return [(i, i ^ step) for i in range(count)]


def slab_sum(values):
    values = values + lax.ppermute(values, "core", SWAP)
    count, step = lax.axis_size("z"), 1
    while step < count:
        values = values + lax.ppermute(values, "z", flip_pairs(count, step))
        step *= 2
    return values


def crop_swap(pieces):
    return lax.all_to_all(pieces, "crop", 0, 0, tiled=True)


def flips(value, axis):
    count = lax.axis_size(axis)
    return [value] + [
        lax.ppermute(value, axis, flip_pairs(count, shift)) for shift in range(1, count)
    ]


def flips_of(pieces, axis):
    count = lax.axis_size(axis)
    return [pieces[0]] + [
        lax.ppermute(pieces[shift], axis, flip_pairs(count, shift)) for shift in range(1, count)
    ]


def total_of(pieces):
    total = pieces[0].astype(jnp.float32)
    for piece in pieces[1:]:
        total = total + piece.astype(jnp.float32)
    return total


def moves(plan, inputs, outputs):
    place = jnp.stack([lax.axis_index("crop"), lax.axis_index("core")]).astype(jnp.int32)

    def kernel(place_ref, *refs):
        crop, core = place_ref[0], place_ref[1]
        sources, targets = refs[: len(inputs)], refs[len(inputs) : -1]
        copies = [
            pltpu.make_async_copy(
                sources[source].at[from_index(crop, core)],
                targets[target].at[to_index(crop, core)],
                refs[-1].at[number],
            )
            for number, (source, from_index, target, to_index) in enumerate(plan)
        ]
        for copy in copies:
            copy.start()
        for copy in copies:
            copy.wait()

    size = sum(math.prod(shape) for shape in outputs)
    return pl.pallas_call(
        kernel,
        in_specs=[pl.BlockSpec(memory_space=pltpu.SMEM)]
        + [pl.BlockSpec(memory_space=pl.ANY)] * len(inputs),
        out_specs=[pl.BlockSpec(memory_space=pltpu.VMEM)] * len(outputs),
        out_shape=[jax.ShapeDtypeStruct(shape, jnp.bfloat16) for shape in outputs],
        scratch_shapes=[pltpu.SemaphoreType.DMA((len(plan),))],
        compiler_params=pltpu.CompilerParams(vmem_limit_bytes=4 * size + 2**22),
        cost_estimate=pl.CostEstimate(flops=0, transcendentals=0, bytes_accessed=4 * size),
    )(place, *inputs)


def column_plan(pieces, block, apart):
    crops = lax.axis_size("crop")
    plan = []
    for shift in range(crops):
        for piece in range(pieces):

            def whole(crop, core, shift=shift, piece=piece):
                start = (piece * crops + (crop ^ shift)) * block
                return (slice(None), pl.ds(pl.multiple_of(start, block), block))

            def part(crop, core, piece=piece):
                return (slice(None), pl.ds(piece * block, block))

            plan.append((0, whole, shift, part) if apart else (shift, part, 0, whole))
    return plan


def chunk_at(spot, crop, core):
    kind, number, width = spot
    if kind == "row":
        return (slice(None), core, crop, number)
    return (slice(None), core, crop, slice(None), pl.ds(number * width, width))


def pack_at(number, lanes):
    if lanes is None:
        return (slice(None), number)
    return (slice(None), number, slice(None), pl.ds(lanes, DEC))


def gather_plan(spots):
    plan = []
    crops = lax.axis_size("crop")
    for side in range(2):
        for shift in range(crops):
            for number, lanes, target, spot in spots:
                plan.append(
                    (
                        side * crops + shift,
                        lambda crop, core, number=number, lanes=lanes: pack_at(number, lanes),
                        target,
                        lambda crop, core, side=side, shift=shift, spot=spot: chunk_at(
                            spot, crop ^ shift, core ^ side
                        ),
                    )
                )
    return plan


def core_swap(pieces):
    return [lax.ppermute(piece, "core", SWAP) for piece in pieces]


def scatter_plan(spots):
    plan = []
    for side in range(2):
        for shift in range(lax.axis_size("crop")):
            for number, lanes, source, spot in spots:
                plan.append(
                    (
                        source,
                        lambda crop, core, side=side, shift=shift, spot=spot: chunk_at(
                            spot, crop ^ shift, core ^ side
                        ),
                        side,
                        lambda crop, core, shift=shift, number=number, lanes=lanes: (shift,)
                        + pack_at(number, lanes),
                    )
                )
    return plan


def scatter_cores(weights, spots, chunks):
    crops, layers = lax.axis_size("crop"), lax.axis_size("z")
    shape = (crops, layers, chunks, weights[0].shape[3], D)
    return moves(scatter_plan(spots), weights, [shape, shape])


def core_sum(keep, send):
    got = lax.ppermute(send, "core", SWAP)
    return [
        (keep[shift].astype(jnp.float32) + got[shift].astype(jnp.float32)).astype(jnp.bfloat16)
        for shift in range(keep.shape[0])
    ]


def row_pad(rows, count):
    return jnp.pad(rows, ((0, count - rows.shape[0]), (0, 0)))


def slab_trim(full, piece, size):
    layers, cores, crops = full.shape[:3]
    rows = full.reshape(layers * cores, crops, -1, DEC)[:, :, :piece]
    return rows.reshape(layers * cores, -1, DEC)[:, :size].reshape(-1, DEC)


def slab_fill(full, piece, chunks, rows):
    layers, crops = lax.axis_size("z"), lax.axis_size("crop")
    shaped = full.reshape(2 * layers, -1, DEC)
    shaped = jnp.pad(shaped, ((0, 0), (0, crops * piece - shaped.shape[1]), (0, 0)))
    shaped = shaped.reshape(2 * layers, crops, piece, DEC)
    shaped = jnp.pad(shaped, ((0, 0), (0, 0), (0, chunks * rows - piece), (0, 0)))
    return shaped.reshape(layers, 2, crops, chunks, rows, DEC)


def to_units(rows, unit):
    crops, size = rows.shape[0], rows.shape[1] * rows.shape[2]
    flat = jnp.pad(rows.reshape(crops, size), ((0, 0), (0, -size % unit)))
    return flat.reshape(crops, -1, unit)


def from_units(units, rows, width):
    return units.reshape(units.shape[0], -1)[:, : rows * width].reshape(-1, rows, width)


def after(value, earlier):
    return lax.optimization_barrier((value, earlier))[0]


def z_sum(pack, late=None):
    own = lax.axis_index("z")
    pieces = [
        lax.dynamic_index_in_dim(pack, own ^ shift, 0, keepdims=False)
        for shift in range(pack.shape[0])
    ]
    got = flips_of(pieces, "z")
    if late is not None:
        got = after(got, late)
    return total_of(got).astype(jnp.bfloat16)


def neighbours(volume):
    count = lax.axis_size(SLAB)
    forward = [(i, i + 1) for i in range(count - 1)]
    backward = [(target, source) for source, target in forward]
    low = lax.ppermute(volume[:, -1:], SLAB, forward)
    high = lax.ppermute(volume[:, :1], SLAB, backward)
    return low, high


def with_planes(volume, rims):
    low, high = rims
    return jnp.concatenate([low.astype(volume.dtype), volume, high.astype(volume.dtype)], axis=1)


def inside(rimmed):
    place, last = lax.axis_index(SLAB), lax.axis_size(SLAB) - 1
    plane = lax.broadcasted_iota(jnp.int32, rimmed.shape, 1)
    outside = ((plane == 0) & (place == 0)) | (
        (plane == rimmed.shape[1] - 1) & (place == last)
    )
    return jnp.where(outside, jnp.zeros((), rimmed.dtype), rimmed)


def columns(rimmed):
    padded = jnp.pad(rimmed, ((0, 0), (0, 0), (1, 1), (1, 1), (0, 0)))
    crop_count, layers, breadth = (rimmed.shape[0], rimmed.shape[1] - 2, rimmed.shape[2])
    pieces = [
        padded[
            :,
            shift_z : shift_z + layers,
            shift_y : shift_y + breadth,
            shift_x : shift_x + breadth,
            :,
        ]
        for shift_z in range(3)
        for shift_y in range(3)
        for shift_x in range(3)
    ]
    return jnp.concatenate(pieces, -1).reshape(crop_count * layers * breadth * breadth, -1)


def back_conv(grad_rimmed, kernel, inputs):
    outputs = kernel.shape[1]
    flipped = (
        kernel.reshape(27, inputs, outputs)[::-1].transpose(0, 2, 1).reshape(27 * outputs, inputs)
    )
    crop_count, planes, breadth = grad_rimmed.shape[:3]
    return matmul(columns(grad_rimmed), flipped).reshape(
        crop_count, planes - 2, breadth, breadth, inputs
    )


def slab_totals(first, second):
    both = jnp.stack([jnp.sum(first, (1, 2, 3)), jnp.sum(second, (1, 2, 3))])
    return slab_sum(both)


def over_voxels(values):
    return values[:, None, None, None, :]


def norm_scales(values, voxel_count):
    totals = slab_totals(values, values * values)
    average = totals[0] / voxel_count
    inverse = lax.rsqrt(totals[1] / voxel_count - average * average + 1e-05)
    return over_voxels(average), over_voxels(inverse)


def norm_slopes(grad, normed, voxel_count):
    totals = slab_totals(grad, grad * normed)
    return over_voxels(totals[0] / voxel_count), over_voxels(totals[1] / voxel_count)


def heads_out(block, parts):
    crop_count, tokens = block.shape[0], block.shape[1]
    slab_count = lax.axis_size(SLAB)
    shaped = block.reshape(crop_count, tokens, parts, HEADS, HDIM).transpose(0, 3, 1, 2, 4)
    shaped = shaped.reshape(crop_count * HEADS, tokens, parts * HDIM)
    spare = -shaped.shape[0] % slab_count
    shaped = jnp.pad(shaped, ((0, spare), (0, 0), (0, 0)))
    return lax.all_to_all(shaped, SLAB, 0, 1, tiled=True)


def heads_back(block, crop_count, parts):
    shaped = lax.all_to_all(block, SLAB, 1, 0, tiled=True)[: crop_count * HEADS]
    tokens = shaped.shape[1]
    shaped = shaped.reshape(crop_count, HEADS, tokens, parts, HDIM).transpose(0, 2, 3, 1, 4)
    return shaped.reshape(crop_count * tokens, parts * D)


def to_volume(lifted, crop_count):
    layers = lifted.shape[0] // (crop_count * SIDE * SIDE)
    shaped = lifted.reshape(crop_count, layers, SIDE, SIDE, 2, 2, 2, DEC)
    return shaped.transpose(0, 1, 4, 2, 5, 3, 6, 7).reshape(
        crop_count, 2 * layers, 2 * SIDE, 2 * SIDE, DEC
    )


def to_tokens(volume):
    crop_count, layers = (volume.shape[0], volume.shape[1] // 2)
    shaped = volume.reshape(crop_count, layers, 2, SIDE, 2, SIDE, 2, DEC)
    return shaped.transpose(0, 1, 3, 5, 2, 4, 6, 7).reshape(
        crop_count * layers * SIDE * SIDE, 8 * DEC
    )


def adam_update(weight, gradient, mean_old, square_old, factor, step_rate, step_decay):
    clipped = gradient * factor
    mean_new = BETA_ONE * mean_old + (1.0 - BETA_ONE) * clipped
    square_new = BETA_TWO * square_old + (1.0 - BETA_TWO) * clipped * clipped
    direction = (
        mean_new
        / (1.0 - BETA_ONE**STEP)
        / (jnp.sqrt(square_new / (1.0 - BETA_TWO**STEP)) + EPSILON)
    )
    return (weight - step_rate * (direction + step_decay * weight), mean_new, square_new)


def local(
    patches,
    modality,
    skip_feats,
    cotangent,
    embedding,
    attention_in,
    attention_out,
    expand_up,
    expand_down,
    upsample,
    convolve_one,
    convolve_two,
    positions,
    vectors,
    embedding_mean,
    attention_in_mean,
    attention_out_mean,
    expand_up_mean,
    expand_down_mean,
    upsample_mean,
    convolve_one_mean,
    convolve_two_mean,
    positions_mean,
    vectors_mean,
    embedding_square,
    attention_in_square,
    attention_out_square,
    expand_up_square,
    expand_down_square,
    upsample_square,
    convolve_one_square,
    convolve_two_square,
    positions_square,
    vectors_square,
):
    shards = (
        embedding,
        attention_in,
        attention_out,
        expand_up,
        expand_down,
        upsample,
        convolve_one,
        convolve_two,
        positions,
        vectors,
    )
    means_in = (
        embedding_mean,
        attention_in_mean,
        attention_out_mean,
        expand_up_mean,
        expand_down_mean,
        upsample_mean,
        convolve_one_mean,
        convolve_two_mean,
        positions_mean,
        vectors_mean,
    )
    squares_in = (
        embedding_square,
        attention_in_square,
        attention_out_square,
        expand_up_square,
        expand_down_square,
        upsample_square,
        convolve_one_square,
        convolve_two_square,
        positions_square,
        vectors_square,
    )
    step_rates = (RATE,) * 9 + (VECTOR_RATE,)
    step_decays = (DECAY,) * 9 + (VECTOR_DECAY,)
    crops = lax.axis_size("crop")
    layers = lax.axis_size("z")
    slab_count = 2 * layers
    crop_batch = patches.shape[0]
    local_tokens = patches.shape[1] * patches.shape[2]
    rows_in = crop_batch * local_tokens
    voxel_count = skip_feats.shape[1] * skip_feats.shape[2] * skip_feats.shape[3] * slab_count
    score_scale = HDIM ** (-0.5)
    unit = D // crops

    lows = [entry.astype(jnp.bfloat16) for entry in shards]
    embed_rows = embedding.shape[0]
    share = embed_rows // crops
    block = math.gcd(share, PATCH)
    groups = share // block
    row_count = attention_in.shape[0] // crops
    down_count = expand_down.shape[0] // crops
    embed_wide = (
        lows[0].reshape(groups, crops, block, unit).transpose(1, 0, 2, 3).reshape(crops, share, unit)
    )
    first_count = -(-convolve_one.shape[0] // crops)
    second_count = -(-convolve_two.shape[0] // crops)
    narrow = jnp.concatenate(
        [
            jnp.pad(lows[6], ((0, crops * first_count - lows[6].shape[0]), (0, 0))).reshape(
                crops, first_count, -1
            ),
            jnp.pad(lows[7], ((0, crops * second_count - lows[7].shape[0]), (0, 0))).reshape(
                crops, second_count, -1
            ),
        ],
        1,
    )
    up_rows = expand_up.shape[0]
    class_size = FF // crops
    per_class = class_size // crops
    up_units = lows[3].reshape(up_rows, -1, crops, down_count).transpose(2, 0, 1, 3)
    up_units = to_units(up_units.reshape(crops, up_rows, per_class), unit)
    lift_units = to_units(lows[5].reshape(crops, row_count, -1), unit)
    narrow_units = to_units(narrow, unit)
    wide = jnp.concatenate(
        [
            lows[1].reshape(crops, row_count, 3, unit).transpose(0, 2, 1, 3).reshape(crops, -1, unit),
            lows[2].reshape(crops, row_count, unit),
            up_units,
            lows[4].reshape(crops, down_count, unit),
            jnp.broadcast_to(lows[8][None], (crops,) + lows[8].shape),
            lift_units,
            narrow_units,
        ],
        1,
    )
    pieces = (CHANS * PATCH) // (block * crops)
    ct_size = PATCH // crops
    own_crop = lax.axis_index("crop")
    own_mri = jnp.broadcast_to(
        (modality == 1)[:, None, None], (crop_batch, local_tokens, 1)
    ).reshape(-1, 1)
    marks = jnp.broadcast_to(own_mri.astype(jnp.float32), (rows_in, 128))
    is_mri = jnp.concatenate(flips(marks, "crop"), 0)[:, :1] > 0.5
    lanes = pieces * block
    if block % 128 == 0:
        pixels = moves(
            column_plan(pieces, block, True),
            [patches.reshape(rows_in, crops * lanes)],
            [(rows_in, lanes)] * crops,
        )
    else:
        pixels = patches.reshape(rows_in, pieces, crops, block).transpose(2, 0, 1, 3)
        pixels = pixels.reshape(crops, rows_in, lanes)
        pixels = [
            lax.dynamic_index_in_dim(pixels, own_crop ^ shift, 0, keepdims=False)
            for shift in range(crops)
        ]
    pixel_parts = flips_of(list(pixels), "crop")
    wide = crop_swap(wide)
    embed_part = crop_swap(after(embed_wide, (wide, is_mri)))
    embed_part = embed_part.transpose(1, 0, 2).reshape(share, D)
    marks = []
    edge = 0
    for size in (3 * row_count, row_count, up_units.shape[1], down_count, lows[8].shape[0],
                 lift_units.shape[1], narrow_units.shape[1]):
        marks.append(wide[:, edge : edge + size])
        edge += size
    lift_rows = from_units(marks[5], row_count, 8 * DEC // crops)
    narrow = from_units(marks[6], first_count + second_count, DEC // crops)
    triple_part = marks[0].reshape(3, crops, row_count, unit).transpose(0, 2, 1, 3).reshape(-1, D)
    output_part = marks[1].transpose(1, 0, 2).reshape(row_count, D)
    up_part = from_units(marks[2], up_rows, per_class).transpose(1, 0, 2).reshape(-1, D)
    down_part = marks[3].transpose(1, 0, 2).reshape(down_count, D)
    position_rows = marks[4].transpose(1, 0, 2).reshape(-1, D).astype(jnp.float32)
    lift_part = (
        lift_rows.transpose(1, 0, 2).reshape(row_count, 8, DEC).transpose(1, 0, 2).reshape(-1, DEC)
    )
    narrow_part = narrow.transpose(1, 0, 2).reshape(-1, DEC)
    first_chunks, second_chunks = -(-first_count // row_count), -(-second_count // row_count)
    slim = jnp.concatenate(
        [
            lift_part,
            row_pad(narrow_part[:first_count], first_chunks * row_count),
            row_pad(narrow_part[first_count:], second_chunks * row_count),
        ],
        0,
    )
    slim_chunks = -(-(8 + first_chunks + second_chunks) // 6)
    slim = row_pad(slim, 6 * slim_chunks * row_count)
    slim = slim.reshape(slim_chunks, 6, row_count, DEC).transpose(0, 2, 1, 3).reshape(-1, D)
    vector_size = vectors.shape[0]
    vector_part = jnp.pad(lows[9][None], ((0, row_count - 1), (0, D - vector_size)))

    quarter = 6
    packs = jnp.concatenate([triple_part, output_part, vector_part, slim], 0)
    packs = lax.all_gather(packs.reshape(-1, row_count, D), "z", axis=0)
    packs = after(packs, pixel_parts)
    pack_one, pack_slim = packs[:, :5], packs[:, 5:]
    embed_full = lax.all_gather(embed_part, SLAB, axis=0, tiled=True)
    up_size = up_part.shape[0]
    ff_part = after(jnp.concatenate([up_part, down_part], 0), embed_part)
    ff_full = lax.all_gather(ff_part, SLAB, axis=0)
    up_full = ff_full[:, :up_size].reshape(D, class_size)
    down_full = ff_full[:, up_size:].reshape(class_size, D)
    one_spots = [
        (0, None, 0, ("lane", 0, D)),
        (1, None, 0, ("lane", 1, D)),
        (2, None, 0, ("lane", 2, D)),
        (3, None, 1, ("lane", 0, D)),
        (4, None, 2, ("lane", 0, D)),
    ]
    slim_list = [(0, ("lane", k, DEC)) for k in range(8)]
    slim_list += [(1, ("row", k, DEC)) for k in range(first_chunks)]
    slim_list += [(2, ("row", k, DEC)) for k in range(second_chunks)]
    slim_spots = [
        (number // quarter, number % quarter * DEC, target, spot)
        for number, (target, spot) in enumerate(slim_list)
    ]
    lead = (layers, 2, crops)
    none = jnp.zeros((), jnp.bfloat16)
    one_own = flips(pack_one, "crop")
    pixels = jnp.concatenate(pixel_parts, 0)
    pixel_rows = jnp.concatenate(
        [jnp.where(is_mri, none, pixels[:, :ct_size]), jnp.where(is_mri, pixels, none)], 1
    )
    partial = matmul(pixel_rows, embed_full).astype(jnp.bfloat16)
    product = total_of(flips_of(list(partial.reshape(crops, rows_in, D)), "crop"))
    one_other = core_swap(after(one_own, partial))
    triple_full, output_full, vector_full = moves(
        gather_plan(one_spots),
        one_own + one_other,
        [lead + (row_count, 3 * D), lead + (row_count, D), lead + (row_count, D)],
    )
    triple_full = triple_full.reshape(D, 3 * D)
    output_full = output_full.reshape(D, D)
    vector_full = vector_full[:, :, :, 0, :vector_size].transpose(2, 0, 1, 3).reshape(12 * D)
    vector_rows = vector_full.astype(jnp.float32).reshape(12, D)
    embedded = (
        product
        + jnp.where(own_mri, vector_rows[7], vector_rows[6])
        + jnp.concatenate([position_rows] * crop_batch, 0)
    )
    normed_one, pull_one = jax.vjp(layer_norm, embedded, vector_rows[0], vector_rows[1])
    normed_one = normed_one.astype(jnp.bfloat16)
    triple = matmul(normed_one, triple_full).astype(jnp.bfloat16)
    triple = heads_out(triple.reshape(crop_batch, local_tokens, 3 * D), 3)
    query, keys, values = triple[..., :HDIM], triple[..., HDIM : 2 * HDIM], triple[..., 2 * HDIM :]
    scores = (
        jnp.einsum("pqd,pkd->pqk", query, keys, preferred_element_type=jnp.float32) * score_scale
    )
    probs = jax.nn.softmax(scores, axis=-1)
    probs_low = probs.astype(jnp.bfloat16)
    mixed = jnp.einsum("pqk,pkd->pqd", probs_low, values, preferred_element_type=jnp.float32)
    slim_own = flips(pack_slim, "crop")
    mixed = after(mixed.astype(jnp.bfloat16), slim_own)
    mixed = heads_back(mixed, crop_batch, 1)
    slim_other = core_swap(slim_own)
    hidden_one = embedded + matmul(mixed, output_full) + vector_rows[4]
    hidden_one = after(hidden_one, slim_other)
    lift_full, first_full, second_full = moves(
        gather_plan(slim_spots),
        slim_own + slim_other,
        [
            lead + (row_count, 8 * DEC),
            lead + (first_chunks, row_count, DEC),
            lead + (second_chunks, row_count, DEC),
        ],
    )
    lift_full = lift_full.reshape(D, 8 * DEC)
    first_full = slab_trim(first_full, first_count, convolve_one.shape[0])
    second_full = slab_trim(second_full, second_count, convolve_two.shape[0])
    normed_two, pull_two = jax.vjp(layer_norm, hidden_one, vector_rows[2], vector_rows[3])
    normed_two = normed_two.astype(jnp.bfloat16)
    normed_all = jnp.concatenate(flips(normed_two, "crop"), 0)
    bias_class = vector_rows[8:].reshape(slab_count, crops, down_count)
    bias_class = lax.dynamic_index_in_dim(bias_class, own_crop, 1, keepdims=False).reshape(-1)
    inner = matmul(normed_all, up_full) + bias_class
    activated = gelu_exact(inner).astype(jnp.bfloat16)
    partial = matmul(activated, down_full).astype(jnp.bfloat16).reshape(crops, rows_in, D)
    product = total_of(flips_of(list(partial), "crop"))
    hidden_two = hidden_one + product + vector_rows[5]
    hidden_low = hidden_two.astype(jnp.bfloat16)
    volume = to_volume(matmul(hidden_low, lift_full), crop_batch)
    joined = jnp.concatenate([volume.astype(jnp.bfloat16), skip_feats], -1)
    joined = with_planes(joined, neighbours(joined))
    volume_rimmed = with_planes(
        volume, (joined[:, :1, ..., :DEC], joined[:, -1:, ..., :DEC])
    )
    target_rimmed = with_planes(cotangent, neighbours(cotangent)).astype(jnp.float32)
    cols_one = columns(joined)
    conv_one = matmul(cols_one, first_full).reshape(volume.shape)
    conv_one_rimmed = with_planes(conv_one, neighbours(conv_one.astype(jnp.bfloat16)))
    average_a, inverse_a = norm_scales(conv_one, voxel_count)
    normed_a = (conv_one_rimmed - average_a) * inverse_a
    first_act = inside(gelu_exact(normed_a).astype(jnp.bfloat16))
    cols_two = columns(first_act)
    conv_two = matmul(cols_two, second_full).reshape(volume.shape)
    conv_two_rimmed = with_planes(conv_two, neighbours(conv_two.astype(jnp.bfloat16)))
    average_b, inverse_b = norm_scales(conv_two, voxel_count)
    normed_b = (conv_two_rimmed - average_b) * inverse_b
    before = normed_b + volume_rimmed
    block_output = gelu_exact(before[:, 1:-1]).astype(jnp.bfloat16)

    grad_before = target_rimmed * gelu_slope(before)
    mean_b, slope_b = norm_slopes(grad_before[:, 1:-1], normed_b[:, 1:-1], voxel_count)
    grad_conv_two = inverse_b * (grad_before - mean_b - normed_b * slope_b)
    grad_conv_two = inside(grad_conv_two.astype(jnp.bfloat16))
    weight_second = matmul_left_t(cols_two, grad_conv_two[:, 1:-1].reshape(-1, DEC))
    grad_first = back_conv(grad_conv_two, second_full, DEC) * gelu_slope(normed_a[:, 1:-1])
    grad_first_rimmed = with_planes(grad_first, neighbours(grad_first.astype(jnp.bfloat16)))
    mean_a, slope_a = norm_slopes(grad_first, normed_a[:, 1:-1], voxel_count)
    grad_conv_one = inverse_a * (grad_first_rimmed - mean_a - normed_a * slope_a)
    grad_conv_one = inside(grad_conv_one.astype(jnp.bfloat16))
    weight_first = matmul_left_t(cols_one, grad_conv_one[:, 1:-1].reshape(-1, DEC))
    grad_joined = back_conv(grad_conv_one, first_full, 2 * DEC)
    skip_grad = grad_joined[..., DEC:].astype(jnp.bfloat16)
    grad_lifted = to_tokens(grad_before[:, 1:-1] + grad_joined[..., :DEC]).astype(jnp.bfloat16)
    weight_lift = matmul_left_t(hidden_low, grad_lifted)
    grad_hidden = matmul_right_t(grad_lifted, lift_full)
    bias_down = jnp.sum(grad_hidden, 0)
    grad_branch = grad_hidden.astype(jnp.bfloat16)
    grad_all = jnp.concatenate(flips(grad_branch, "crop"), 0)
    grad_inner = matmul_right_t(grad_all, down_full) * gelu_slope(inner)
    bias_up = jnp.sum(grad_inner, 0)
    grad_inner_low = grad_inner.astype(jnp.bfloat16)
    partial = matmul_right_t(grad_inner_low, up_full).astype(jnp.bfloat16)
    partial = partial.reshape(crops, rows_in, D)
    weight_down = matmul_left_t(activated, grad_all).astype(jnp.bfloat16)
    weight_up = matmul_left_t(normed_all, grad_inner_low).astype(jnp.bfloat16)
    ff_grads = jnp.concatenate(
        [weight_up.reshape(slab_count, -1, D), weight_down.reshape(slab_count, -1, D)], 1
    ).reshape(-1, D)

    slim_move = scatter_cores(
        [
            weight_lift.astype(jnp.bfloat16).reshape(lead + (row_count, 8 * DEC)),
            slab_fill(weight_first.astype(jnp.bfloat16), first_count, first_chunks, row_count),
            slab_fill(weight_second.astype(jnp.bfloat16), second_count, second_chunks, row_count),
        ],
        slim_spots,
        slim_chunks,
    )
    slim_parts = core_sum(*slim_move)
    partial = after(partial, slim_move[1])
    back_two = pull_two(total_of(flips_of(list(partial), "crop")))
    grad_hidden = grad_hidden + back_two[0]
    bias_out = jnp.sum(grad_hidden, 0)
    grad_branch = grad_hidden.astype(jnp.bfloat16)
    weight_out = matmul_left_t(mixed, grad_branch)
    grad_mixed = matmul_right_t(grad_branch, output_full).astype(jnp.bfloat16)
    grad_mixed = after(grad_mixed, slim_parts)
    slim_got = flips_of(slim_parts, "crop")
    grad_mixed = heads_out(grad_mixed.reshape(crop_batch, local_tokens, D), 1)
    grad_probs = jnp.einsum(
        "pqd,pkd->pqk", grad_mixed, values, preferred_element_type=jnp.float32
    )
    centre = jnp.sum(probs * grad_probs, -1, keepdims=True)
    grad_scores = (probs * (grad_probs - centre)).astype(jnp.bfloat16)
    grad_query = (
        jnp.einsum("pqk,pkd->pqd", grad_scores, keys, preferred_element_type=jnp.float32)
        * score_scale
    )
    grad_keys = (
        jnp.einsum("pqk,pqd->pkd", grad_scores, query, preferred_element_type=jnp.float32)
        * score_scale
    )
    grad_values = jnp.einsum(
        "pqk,pqd->pkd", probs_low, grad_mixed, preferred_element_type=jnp.float32
    )
    grad_triple = jnp.concatenate([grad_query, grad_keys, grad_values], -1).astype(jnp.bfloat16)
    grad_triple = heads_back(grad_triple, crop_batch, 3)
    grad_triple = after(grad_triple, slim_got)
    ff_grads = after(ff_grads, grad_triple)
    ff_sum = lax.psum_scatter(ff_grads, SLAB, scatter_dimension=0, tiled=True)
    weight_triple = matmul_left_t(normed_one, grad_triple)
    back_one = pull_one(matmul_right_t(grad_triple, triple_full))
    grad_hidden = grad_hidden + back_one[0]
    grad_low = grad_hidden.astype(jnp.bfloat16)

    grad_rows = jnp.concatenate(flips(grad_low, "crop"), 0)
    weight_embed = matmul_left_t(pixel_rows, grad_rows).astype(jnp.bfloat16)
    slim_sum = total_of(after(slim_got, weight_embed)).astype(jnp.bfloat16)
    embed_sum = lax.psum_scatter(after(weight_embed, ff_sum), SLAB, scatter_dimension=0, tiled=True)
    bias_ct = jnp.sum(jnp.where(own_mri, 0.0, grad_hidden), 0)
    bias_mri = jnp.sum(jnp.where(own_mri, grad_hidden, 0.0), 0)
    position_grad = jnp.sum(grad_hidden.reshape(crop_batch, local_tokens, D), 0)
    position_grad = position_grad.astype(jnp.bfloat16).reshape(-1, crops, unit).swapaxes(0, 1)
    position_grad = [
        lax.dynamic_index_in_dim(position_grad, own_crop ^ shift, 0, keepdims=False)
        for shift in range(crops)
    ]
    position_grad = total_of(flips_of(position_grad, "crop"))
    at_class = lax.broadcasted_iota(jnp.int32, (slab_count, crops, down_count), 1) == own_crop
    bias_full = jnp.where(at_class, bias_up.reshape(slab_count, 1, down_count), 0.0)
    vector_grad = jnp.concatenate(
        [
            jnp.stack(
                [
                    back_one[1],
                    back_one[2],
                    back_two[1],
                    back_two[2],
                    bias_out,
                    bias_down,
                    bias_ct,
                    bias_mri,
                ]
            ),
            bias_full.reshape(4, D),
        ],
        0,
    ).astype(jnp.bfloat16)
    vector_pack = vector_grad.reshape(crops, layers, 2, 1, vector_size).transpose(1, 2, 0, 3, 4)
    vector_pack = jnp.pad(
        vector_pack, ((0, 0),) * 3 + ((0, row_count - 1), (0, D - vector_size))
    )
    weight_triple = after(weight_triple.astype(jnp.bfloat16), weight_embed)
    one_parts = core_sum(*scatter_cores(
        [
            weight_triple.reshape(lead + (row_count, 3 * D)),
            weight_out.astype(jnp.bfloat16).reshape(lead + (row_count, D)),
            vector_pack,
        ],
        one_spots,
        5,
    ))
    pixel_grad = matmul_right_t(after(grad_rows, one_parts), embed_full)
    ct_grad = jnp.pad(pixel_grad[:, :ct_size], ((0, 0), (0, (CHANS - 1) * ct_size)))
    pixel_grad = jnp.where(is_mri, pixel_grad[:, ct_size:], ct_grad).astype(jnp.bfloat16)
    slim_all = z_sum(slim_sum, one_parts).reshape(slim_chunks, row_count, 6, DEC)
    slim_all = slim_all.transpose(0, 2, 1, 3).reshape(-1, DEC)
    first_start = 8 * row_count
    second_start = first_start + first_chunks * row_count
    lift_sum = slim_all[:first_start].reshape(8, row_count, DEC).transpose(1, 0, 2)
    lift_sum = lift_sum.reshape(row_count, crops, -1).transpose(1, 0, 2)
    narrow_sum = jnp.concatenate(
        [
            slim_all[first_start : first_start + first_count],
            slim_all[second_start : second_start + second_count],
        ],
        0,
    )
    narrow_sum = narrow_sum.reshape(-1, crops, DEC // crops).transpose(1, 0, 2)
    lift_units, narrow_units = to_units(lift_sum, unit), to_units(narrow_sum, unit)
    up_units = ff_sum[:up_size].reshape(up_rows, crops, per_class).transpose(1, 0, 2)
    up_units = to_units(up_units, unit)
    one_got = flips_of(one_parts, "crop")
    one_got, lift_units, narrow_units, up_units, _ = lax.optimization_barrier(
        (one_got, lift_units, narrow_units, up_units, position_grad)
    )
    one_sum = total_of(one_got).astype(jnp.bfloat16)
    pixel_got = flips_of(
        after(list(pixel_grad.reshape(crops, rows_in, pieces * block)), one_got), "crop"
    )

    def by_units(rows, chunks):
        shaped = rows.reshape(chunks, -1, crops, unit).transpose(0, 2, 1, 3)
        return shaped.reshape(crops, -1, unit)

    def join_units(got, chunks):
        return (
            got.reshape(crops, chunks, -1, unit).transpose(0, 2, 1, 3).reshape(-1, chunks * unit)
        )

    sum_one = z_sum(one_sum).reshape(-1, D)

    wide = jnp.concatenate(
        [
            up_units,
            by_units(ff_sum[up_size:], 1),
            by_units(sum_one[: 3 * row_count], 3),
            by_units(sum_one[3 * row_count : 4 * row_count], 1),
            lift_units,
            narrow_units,
            by_units(embed_sum, 1),
        ],
        1,
    )
    local_sum = jnp.float32(0.0)
    for gradient in (embed_sum, ff_sum, lift_sum, narrow_sum, sum_one, position_grad):
        wide_grad = gradient.astype(jnp.float32)
        local_sum = local_sum + jnp.sum(wide_grad * wide_grad)
    wide = crop_swap(after(wide, local_sum)).astype(jnp.float32)
    norm_crop = total_of(flips(local_sum.reshape(1, 1), "crop"))
    if block % 128 == 0:
        (patch_grad,) = moves(
            column_plan(pieces, block, False), pixel_got, [(rows_in, crops * lanes)]
        )
    else:
        pixel_got = jnp.stack(pixel_got)
        patch_grad = jnp.stack(
            [
                lax.dynamic_index_in_dim(pixel_got, own_crop ^ part, 0, keepdims=False)
                for part in range(crops)
            ]
        )
        patch_grad = patch_grad.reshape(crops, rows_in, pieces, block).transpose(1, 2, 0, 3)
    patch_grad = patch_grad.reshape(patches.shape)
    embed_got = wide[:, -share:]
    embed_grad = (
        embed_got.astype(jnp.float32).reshape(crops, groups, block, unit).transpose(1, 0, 2, 3).reshape(-1, unit)
    )
    marks = []
    edge = 0
    for size in (up_units.shape[1], down_count, 3 * row_count, row_count,
                 lift_units.shape[1], narrow_units.shape[1]):
        marks.append(wide[:, edge : edge + size])
        edge += size
    up_grad = from_units(marks[0], up_rows, per_class)
    up_grad = up_grad.reshape(crops, up_rows, -1, down_count).transpose(1, 2, 0, 3)
    up_grad = up_grad.reshape(expand_up.shape)
    down_grad = join_units(marks[1], 1)
    triple_grad = join_units(marks[2], 3)
    output_grad = join_units(marks[3], 1)
    lift_grad = from_units(marks[4], row_count, 8 * DEC // crops).reshape(upsample.shape)
    narrow_got = from_units(marks[5], first_count + second_count, DEC // crops)
    first_grad = narrow_got[:, :first_count].reshape(-1, DEC // crops)[: convolve_one.shape[0]]
    second_grad = narrow_got[:, first_count:].reshape(-1, DEC // crops)[: convolve_two.shape[0]]
    vector_final = sum_one[4 * row_count, :vector_size].astype(jnp.float32)
    gradients = (
        embed_grad,
        triple_grad,
        output_grad,
        up_grad,
        down_grad,
        lift_grad,
        first_grad,
        second_grad,
        position_grad,
        vector_final,
    )
    grad_norm = jnp.sqrt(slab_sum(norm_crop))[0, 0]
    factor = jnp.minimum(1.0, CLIP / grad_norm)
    news, means, squares = ([], [], [])
    for weight, gradient, mean_old, square_old, step_rate, step_decay in zip(
        shards, gradients, means_in, squares_in, step_rates, step_decays
    ):
        weight_new, mean_new, square_new = adam_update(
            weight, gradient, mean_old, square_old, factor, step_rate, step_decay
        )
        news.append(weight_new)
        means.append(mean_new)
        squares.append(square_new)
    return (
        block_output,
        patch_grad,
        skip_grad,
        grad_norm,
        news[0],
        news[1],
        news[2],
        news[3],
        news[4],
        news[5],
        news[6],
        news[7],
        news[8],
        news[9],
        means[0],
        means[1],
        means[2],
        means[3],
        means[4],
        means[5],
        means[6],
        means[7],
        means[8],
        means[9],
        squares[0],
        squares[1],
        squares[2],
        squares[3],
        squares[4],
        squares[5],
        squares[6],
        squares[7],
        squares[8],
        squares[9],
    )


def solution(mesh):
    crops, slabs = mesh.devices.shape
    mesh = Mesh(mesh.devices.reshape(crops, slabs // 2, 2), ("crop", "z", "core"))
    return jax.shard_map(
        local,
        mesh=mesh,
        in_specs=(
            P("crop", ("z", "core"), None, None),
            P("crop"),
            P("crop", ("z", "core"), None, None, None),
            P("crop", ("z", "core"), None, None, None),
            P(("z", "core"), "crop"),
            P(("z", "core"), "crop"),
            P(("z", "core"), "crop"),
            P(("z", "core"), "crop"),
            P(("z", "core"), "crop"),
            P(("z", "core"), "crop"),
            P(("z", "core"), "crop"),
            P(("z", "core"), "crop"),
            P(("z", "core"), "crop"),
            P(("crop", "z", "core")),
            P(("z", "core"), "crop"),
            P(("z", "core"), "crop"),
            P(("z", "core"), "crop"),
            P(("z", "core"), "crop"),
            P(("z", "core"), "crop"),
            P(("z", "core"), "crop"),
            P(("z", "core"), "crop"),
            P(("z", "core"), "crop"),
            P(("z", "core"), "crop"),
            P(("crop", "z", "core")),
            P(("z", "core"), "crop"),
            P(("z", "core"), "crop"),
            P(("z", "core"), "crop"),
            P(("z", "core"), "crop"),
            P(("z", "core"), "crop"),
            P(("z", "core"), "crop"),
            P(("z", "core"), "crop"),
            P(("z", "core"), "crop"),
            P(("z", "core"), "crop"),
            P(("crop", "z", "core")),
        ),
        out_specs=(
            P("crop", ("z", "core"), None, None, None),
            P("crop", ("z", "core"), None, None),
            P("crop", ("z", "core"), None, None, None),
            P(),
            P(("z", "core"), "crop"),
            P(("z", "core"), "crop"),
            P(("z", "core"), "crop"),
            P(("z", "core"), "crop"),
            P(("z", "core"), "crop"),
            P(("z", "core"), "crop"),
            P(("z", "core"), "crop"),
            P(("z", "core"), "crop"),
            P(("z", "core"), "crop"),
            P(("crop", "z", "core")),
            P(("z", "core"), "crop"),
            P(("z", "core"), "crop"),
            P(("z", "core"), "crop"),
            P(("z", "core"), "crop"),
            P(("z", "core"), "crop"),
            P(("z", "core"), "crop"),
            P(("z", "core"), "crop"),
            P(("z", "core"), "crop"),
            P(("z", "core"), "crop"),
            P(("crop", "z", "core")),
            P(("z", "core"), "crop"),
            P(("z", "core"), "crop"),
            P(("z", "core"), "crop"),
            P(("z", "core"), "crop"),
            P(("z", "core"), "crop"),
            P(("z", "core"), "crop"),
            P(("z", "core"), "crop"),
            P(("z", "core"), "crop"),
            P(("z", "core"), "crop"),
            P(("crop", "z", "core")),
        ),
        check_vma=False,
    )
```

```python
import math

import jax
import jax.numpy as jnp
from jax import lax
from jax.experimental import pallas as pl
from jax.experimental.pallas import tpu as pltpu
from jax.sharding import Mesh
from jax.sharding import PartitionSpec as P

D = 768
HEADS = 12
HDIM = 64
FF = 3072
PATCH = 4096
CHANS = 4
DEC = 128
SIDE = 8
STEP = 10


BETA_ONE = 0.9
BETA_TWO = 0.95
RATE = 0.07
DECAY = 0.05
VECTOR_RATE = 0.4
VECTOR_DECAY = 0.0
EPSILON = 1e-08
CLIP = 1.0
CONTRACT_ROWS = (((0,), (0,)), ((), ()))
CONTRACT_COLS = (((1,), (1,)), ((), ()))


def layer_norm(values, gain, shift):
    center = values - jnp.mean(values, -1, keepdims=True)
    spread = jnp.mean(center * center, -1, keepdims=True)
    return center * lax.rsqrt(spread + 1e-06) * gain + shift


def gelu_exact(values):
    return jax.nn.gelu(values, approximate=False)


def gelu_slope(values):
    return (
        0.5 * (1.0 + lax.erf(values * 0.7071067811865476))
        + values * jnp.exp(-0.5 * values * values) * 0.3989422804014327
    )


def matmul(left, right):
    return jnp.dot(left, right, preferred_element_type=jnp.float32)


def matmul_left_t(left, right):
    return lax.dot_general(left, right, CONTRACT_ROWS, preferred_element_type=jnp.float32)


def matmul_right_t(left, right):
    return lax.dot_general(left, right, CONTRACT_COLS, preferred_element_type=jnp.float32)


SLAB = ("z", "core")
SWAP = [(0, 1), (1, 0)]


def flip_pairs(count, step):
    return [(i, i ^ step) for i in range(count)]


def slab_sum(values):
    values = values + lax.ppermute(values, "core", SWAP)
    count, step = lax.axis_size("z"), 1
    while step < count:
        values = values + lax.ppermute(values, "z", flip_pairs(count, step))
        step *= 2
    return values


def crop_swap(pieces):
    return lax.all_to_all(pieces, "crop", 0, 0, tiled=True)


def flips(value, axis):
    count = lax.axis_size(axis)
    return [value] + [
        lax.ppermute(value, axis, flip_pairs(count, shift)) for shift in range(1, count)
    ]


def flips_of(pieces, axis):
    count = lax.axis_size(axis)
    return [pieces[0]] + [
        lax.ppermute(pieces[shift], axis, flip_pairs(count, shift)) for shift in range(1, count)
    ]


def total_of(pieces):
    total = pieces[0].astype(jnp.float32)
    for piece in pieces[1:]:
        total = total + piece.astype(jnp.float32)
    return total


def moves(plan, inputs, outputs):
    place = jnp.stack([lax.axis_index("crop"), lax.axis_index("core")]).astype(jnp.int32)

    def kernel(place_ref, *refs):
        crop, core = place_ref[0], place_ref[1]
        sources, targets = refs[: len(inputs)], refs[len(inputs) : -1]
        copies = [
            pltpu.make_async_copy(
                sources[source].at[from_index(crop, core)],
                targets[target].at[to_index(crop, core)],
                refs[-1].at[number],
            )
            for number, (source, from_index, target, to_index) in enumerate(plan)
        ]
        for copy in copies:
            copy.start()
        for copy in copies:
            copy.wait()

    size = sum(math.prod(shape) for shape in outputs)
    return pl.pallas_call(
        kernel,
        in_specs=[pl.BlockSpec(memory_space=pltpu.SMEM)]
        + [pl.BlockSpec(memory_space=pl.ANY)] * len(inputs),
        out_specs=[pl.BlockSpec(memory_space=pltpu.VMEM)] * len(outputs),
        out_shape=[jax.ShapeDtypeStruct(shape, jnp.bfloat16) for shape in outputs],
        scratch_shapes=[pltpu.SemaphoreType.DMA((len(plan),))],
        compiler_params=pltpu.CompilerParams(vmem_limit_bytes=4 * size + 2**22),
        cost_estimate=pl.CostEstimate(flops=0, transcendentals=0, bytes_accessed=4 * size),
    )(place, *inputs)


def column_plan(pieces, block, apart):
    crops = lax.axis_size("crop")
    plan = []
    for shift in range(crops):
        for piece in range(pieces):

            def whole(crop, core, shift=shift, piece=piece):
                start = (piece * crops + (crop ^ shift)) * block
                return (slice(None), pl.ds(pl.multiple_of(start, block), block))

            def part(crop, core, piece=piece):
                return (slice(None), pl.ds(piece * block, block))

            plan.append((0, whole, shift, part) if apart else (shift, part, 0, whole))
    return plan


def chunk_at(spot, crop, core):
    kind, number, width = spot
    if kind == "row":
        return (slice(None), core, crop, number)
    return (slice(None), core, crop, slice(None), pl.ds(number * width, width))


def pack_at(number, lanes):
    if lanes is None:
        return (slice(None), number)
    return (slice(None), number, slice(None), pl.ds(lanes, DEC))


def gather_plan(spots):
    plan = []
    crops = lax.axis_size("crop")
    for side in range(2):
        for shift in range(crops):
            for number, lanes, target, spot in spots:
                plan.append(
                    (
                        side * crops + shift,
                        lambda crop, core, number=number, lanes=lanes: pack_at(number, lanes),
                        target,
                        lambda crop, core, side=side, shift=shift, spot=spot: chunk_at(
                            spot, crop ^ shift, core ^ side
                        ),
                    )
                )
    return plan


def core_swap(pieces):
    return [lax.ppermute(piece, "core", SWAP) for piece in pieces]


def scatter_plan(spots):
    plan = []
    for side in range(2):
        for shift in range(lax.axis_size("crop")):
            for number, lanes, source, spot in spots:
                plan.append(
                    (
                        source,
                        lambda crop, core, side=side, shift=shift, spot=spot: chunk_at(
                            spot, crop ^ shift, core ^ side
                        ),
                        side,
                        lambda crop, core, shift=shift, number=number, lanes=lanes: (shift,)
                        + pack_at(number, lanes),
                    )
                )
    return plan


def scatter_cores(weights, spots, chunks):
    crops, layers = lax.axis_size("crop"), lax.axis_size("z")
    shape = (crops, layers, chunks, weights[0].shape[3], D)
    return moves(scatter_plan(spots), weights, [shape, shape])


def core_sum(keep, send):
    got = lax.ppermute(send, "core", SWAP)
    return [
        (keep[shift].astype(jnp.float32) + got[shift].astype(jnp.float32)).astype(jnp.bfloat16)
        for shift in range(keep.shape[0])
    ]


def row_pad(rows, count):
    return jnp.pad(rows, ((0, count - rows.shape[0]), (0, 0)))


def slab_trim(full, piece, size):
    layers, cores, crops = full.shape[:3]
    rows = full.reshape(layers * cores, crops, -1, DEC)[:, :, :piece]
    return rows.reshape(layers * cores, -1, DEC)[:, :size].reshape(-1, DEC)


def slab_fill(full, piece, chunks, rows):
    layers, crops = lax.axis_size("z"), lax.axis_size("crop")
    shaped = full.reshape(2 * layers, -1, DEC)
    shaped = jnp.pad(shaped, ((0, 0), (0, crops * piece - shaped.shape[1]), (0, 0)))
    shaped = shaped.reshape(2 * layers, crops, piece, DEC)
    shaped = jnp.pad(shaped, ((0, 0), (0, 0), (0, chunks * rows - piece), (0, 0)))
    return shaped.reshape(layers, 2, crops, chunks, rows, DEC)


def to_units(rows, unit):
    crops, size = rows.shape[0], rows.shape[1] * rows.shape[2]
    flat = jnp.pad(rows.reshape(crops, size), ((0, 0), (0, -size % unit)))
    return flat.reshape(crops, -1, unit)


def from_units(units, rows, width):
    return units.reshape(units.shape[0], -1)[:, : rows * width].reshape(-1, rows, width)


def after(value, earlier):
    return lax.optimization_barrier((value, earlier))[0]


def z_sum(pack, late=None):
    own = lax.axis_index("z")
    pieces = [
        lax.dynamic_index_in_dim(pack, own ^ shift, 0, keepdims=False)
        for shift in range(pack.shape[0])
    ]
    got = flips_of(pieces, "z")
    if late is not None:
        got = after(got, late)
    return total_of(got).astype(jnp.bfloat16)


def neighbours(volume):
    count = lax.axis_size(SLAB)
    forward = [(i, i + 1) for i in range(count - 1)]
    backward = [(target, source) for source, target in forward]
    low = lax.ppermute(volume[:, -1:], SLAB, forward)
    high = lax.ppermute(volume[:, :1], SLAB, backward)
    return low, high


def with_planes(volume, rims):
    low, high = rims
    return jnp.concatenate([low.astype(volume.dtype), volume, high.astype(volume.dtype)], axis=1)


def inside(rimmed):
    place, last = lax.axis_index(SLAB), lax.axis_size(SLAB) - 1
    plane = lax.broadcasted_iota(jnp.int32, rimmed.shape, 1)
    outside = ((plane == 0) & (place == 0)) | (
        (plane == rimmed.shape[1] - 1) & (place == last)
    )
    return jnp.where(outside, jnp.zeros((), rimmed.dtype), rimmed)


def columns(rimmed):
    padded = jnp.pad(rimmed, ((0, 0), (0, 0), (1, 1), (1, 1), (0, 0)))
    crop_count, layers, breadth = (rimmed.shape[0], rimmed.shape[1] - 2, rimmed.shape[2])
    pieces = [
        padded[
            :,
            shift_z : shift_z + layers,
            shift_y : shift_y + breadth,
            shift_x : shift_x + breadth,
            :,
        ]
        for shift_z in range(3)
        for shift_y in range(3)
        for shift_x in range(3)
    ]
    return jnp.concatenate(pieces, -1).reshape(crop_count * layers * breadth * breadth, -1)


def back_conv(grad_rimmed, kernel, inputs):
    outputs = kernel.shape[1]
    flipped = (
        kernel.reshape(27, inputs, outputs)[::-1].transpose(0, 2, 1).reshape(27 * outputs, inputs)
    )
    crop_count, planes, breadth = grad_rimmed.shape[:3]
    return matmul(columns(grad_rimmed), flipped).reshape(
        crop_count, planes - 2, breadth, breadth, inputs
    )


def slab_totals(first, second):
    both = jnp.stack([jnp.sum(first, (1, 2, 3)), jnp.sum(second, (1, 2, 3))])
    return slab_sum(both)


def over_voxels(values):
    return values[:, None, None, None, :]


def norm_scales(values, voxel_count):
    totals = slab_totals(values, values * values)
    average = totals[0] / voxel_count
    inverse = lax.rsqrt(totals[1] / voxel_count - average * average + 1e-05)
    return over_voxels(average), over_voxels(inverse)


def norm_slopes(grad, normed, voxel_count):
    totals = slab_totals(grad, grad * normed)
    return over_voxels(totals[0] / voxel_count), over_voxels(totals[1] / voxel_count)


def heads_out(block, parts):
    crop_count, tokens = block.shape[0], block.shape[1]
    slab_count = lax.axis_size(SLAB)
    shaped = block.reshape(crop_count, tokens, parts, HEADS, HDIM).transpose(0, 3, 1, 2, 4)
    shaped = shaped.reshape(crop_count * HEADS, tokens, parts * HDIM)
    spare = -shaped.shape[0] % slab_count
    shaped = jnp.pad(shaped, ((0, spare), (0, 0), (0, 0)))
    return lax.all_to_all(shaped, SLAB, 0, 1, tiled=True)


def heads_back(block, crop_count, parts):
    shaped = lax.all_to_all(block, SLAB, 1, 0, tiled=True)[: crop_count * HEADS]
    tokens = shaped.shape[1]
    shaped = shaped.reshape(crop_count, HEADS, tokens, parts, HDIM).transpose(0, 2, 3, 1, 4)
    return shaped.reshape(crop_count * tokens, parts * D)


def to_volume(lifted, crop_count):
    layers = lifted.shape[0] // (crop_count * SIDE * SIDE)
    shaped = lifted.reshape(crop_count, layers, SIDE, SIDE, 2, 2, 2, DEC)
    return shaped.transpose(0, 1, 4, 2, 5, 3, 6, 7).reshape(
        crop_count, 2 * layers, 2 * SIDE, 2 * SIDE, DEC
    )


def to_tokens(volume):
    crop_count, layers = (volume.shape[0], volume.shape[1] // 2)
    shaped = volume.reshape(crop_count, layers, 2, SIDE, 2, SIDE, 2, DEC)
    return shaped.transpose(0, 1, 3, 5, 2, 4, 6, 7).reshape(
        crop_count * layers * SIDE * SIDE, 8 * DEC
    )


def adam_update(weight, gradient, mean_old, square_old, factor, step_rate, step_decay):
    clipped = gradient * factor
    mean_new = BETA_ONE * mean_old + (1.0 - BETA_ONE) * clipped
    square_new = BETA_TWO * square_old + (1.0 - BETA_TWO) * clipped * clipped
    direction = (
        mean_new
        / (1.0 - BETA_ONE**STEP)
        / (jnp.sqrt(square_new / (1.0 - BETA_TWO**STEP)) + EPSILON)
    )
    return (weight - step_rate * (direction + step_decay * weight), mean_new, square_new)


def local(
    patches,
    modality,
    skip_feats,
    cotangent,
    embedding,
    attention_in,
    attention_out,
    expand_up,
    expand_down,
    upsample,
    convolve_one,
    convolve_two,
    positions,
    vectors,
    embedding_mean,
    attention_in_mean,
    attention_out_mean,
    expand_up_mean,
    expand_down_mean,
    upsample_mean,
    convolve_one_mean,
    convolve_two_mean,
    positions_mean,
    vectors_mean,
    embedding_square,
    attention_in_square,
    attention_out_square,
    expand_up_square,
    expand_down_square,
    upsample_square,
    convolve_one_square,
    convolve_two_square,
    positions_square,
    vectors_square,
):
    shards = (
        embedding,
        attention_in,
        attention_out,
        expand_up,
        expand_down,
        upsample,
        convolve_one,
        convolve_two,
        positions,
        vectors,
    )
    means_in = (
        embedding_mean,
        attention_in_mean,
        attention_out_mean,
        expand_up_mean,
        expand_down_mean,
        upsample_mean,
        convolve_one_mean,
        convolve_two_mean,
        positions_mean,
        vectors_mean,
    )
    squares_in = (
        embedding_square,
        attention_in_square,
        attention_out_square,
        expand_up_square,
        expand_down_square,
        upsample_square,
        convolve_one_square,
        convolve_two_square,
        positions_square,
        vectors_square,
    )
    step_rates = (RATE,) * 9 + (VECTOR_RATE,)
    step_decays = (DECAY,) * 9 + (VECTOR_DECAY,)
    crops = lax.axis_size("crop")
    layers = lax.axis_size("z")
    slab_count = 2 * layers
    crop_batch = patches.shape[0]
    local_tokens = patches.shape[1] * patches.shape[2]
    rows_in = crop_batch * local_tokens
    voxel_count = skip_feats.shape[1] * skip_feats.shape[2] * skip_feats.shape[3] * slab_count
    score_scale = HDIM ** (-0.5)
    unit = D // crops

    lows = [entry.astype(jnp.bfloat16) for entry in shards]
    embed_rows = embedding.shape[0]
    share = embed_rows // crops
    block = math.gcd(share, PATCH)
    groups = share // block
    row_count = attention_in.shape[0] // crops
    down_count = expand_down.shape[0] // crops
    embed_wide = (
        lows[0].reshape(groups, crops, block, unit).transpose(1, 0, 2, 3).reshape(crops, share, unit)
    )
    first_count = -(-convolve_one.shape[0] // crops)
    second_count = -(-convolve_two.shape[0] // crops)
    narrow = jnp.concatenate(
        [
            jnp.pad(lows[6], ((0, crops * first_count - lows[6].shape[0]), (0, 0))).reshape(
                crops, first_count, -1
            ),
            jnp.pad(lows[7], ((0, crops * second_count - lows[7].shape[0]), (0, 0))).reshape(
                crops, second_count, -1
            ),
        ],
        1,
    )
    up_rows = expand_up.shape[0]
    class_size = FF // crops
    per_class = class_size // crops
    up_units = lows[3].reshape(up_rows, -1, crops, down_count).transpose(2, 0, 1, 3)
    up_units = to_units(up_units.reshape(crops, up_rows, per_class), unit)
    lift_units = to_units(lows[5].reshape(crops, row_count, -1), unit)
    narrow_units = to_units(narrow, unit)
    wide = jnp.concatenate(
        [
            lows[1].reshape(crops, row_count, 3, unit).transpose(0, 2, 1, 3).reshape(crops, -1, unit),
            lows[2].reshape(crops, row_count, unit),
            up_units,
            lows[4].reshape(crops, down_count, unit),
            jnp.broadcast_to(lows[8][None], (crops,) + lows[8].shape),
            lift_units,
            narrow_units,
        ],
        1,
    )
    pieces = (CHANS * PATCH) // (block * crops)
    ct_size = PATCH // crops
    own_crop = lax.axis_index("crop")
    own_mri = jnp.broadcast_to(
        (modality == 1)[:, None, None], (crop_batch, local_tokens, 1)
    ).reshape(-1, 1)
    marks = jnp.broadcast_to(own_mri.astype(jnp.float32), (rows_in, 128))
    is_mri = jnp.concatenate(flips(marks, "crop"), 0)[:, :1] > 0.5
    lanes = pieces * block
    if block % 128 == 0:
        pixels = moves(
            column_plan(pieces, block, True),
            [patches.reshape(rows_in, crops * lanes)],
            [(rows_in, lanes)] * crops,
        )
    else:
        pixels = patches.reshape(rows_in, pieces, crops, block).transpose(2, 0, 1, 3)
        pixels = pixels.reshape(crops, rows_in, lanes)
        pixels = [
            lax.dynamic_index_in_dim(pixels, own_crop ^ shift, 0, keepdims=False)
            for shift in range(crops)
        ]
    pixel_parts = flips_of(list(pixels), "crop")
    wide = crop_swap(wide)
    embed_part = crop_swap(after(embed_wide, (wide, is_mri)))
    embed_part = embed_part.transpose(1, 0, 2).reshape(share, D)
    marks = []
    edge = 0
    for size in (3 * row_count, row_count, up_units.shape[1], down_count, lows[8].shape[0],
                 lift_units.shape[1], narrow_units.shape[1]):
        marks.append(wide[:, edge : edge + size])
        edge += size
    lift_rows = from_units(marks[5], row_count, 8 * DEC // crops)
    narrow = from_units(marks[6], first_count + second_count, DEC // crops)
    triple_part = marks[0].reshape(3, crops, row_count, unit).transpose(0, 2, 1, 3).reshape(-1, D)
    output_part = marks[1].transpose(1, 0, 2).reshape(row_count, D)
    up_part = from_units(marks[2], up_rows, per_class).transpose(1, 0, 2).reshape(-1, D)
    down_part = marks[3].transpose(1, 0, 2).reshape(down_count, D)
    position_rows = marks[4].transpose(1, 0, 2).reshape(-1, D).astype(jnp.float32)
    lift_part = (
        lift_rows.transpose(1, 0, 2).reshape(row_count, 8, DEC).transpose(1, 0, 2).reshape(-1, DEC)
    )
    narrow_part = narrow.transpose(1, 0, 2).reshape(-1, DEC)
    first_chunks, second_chunks = -(-first_count // row_count), -(-second_count // row_count)
    slim = jnp.concatenate(
        [
            lift_part,
            row_pad(narrow_part[:first_count], first_chunks * row_count),
            row_pad(narrow_part[first_count:], second_chunks * row_count),
        ],
        0,
    )
    slim_chunks = -(-(8 + first_chunks + second_chunks) // 6)
    slim = row_pad(slim, 6 * slim_chunks * row_count)
    slim = slim.reshape(slim_chunks, 6, row_count, DEC).transpose(0, 2, 1, 3).reshape(-1, D)
    vector_size = vectors.shape[0]
    vector_part = jnp.pad(lows[9][None], ((0, row_count - 1), (0, D - vector_size)))

    quarter = 6
    packs = jnp.concatenate([triple_part, output_part, vector_part, slim], 0)
    packs = lax.all_gather(packs.reshape(-1, row_count, D), "z", axis=0)
    packs = after(packs, pixel_parts)
    pack_one, pack_slim = packs[:, :5], packs[:, 5:]
    embed_full = lax.all_gather(embed_part, SLAB, axis=0, tiled=True)
    up_size = up_part.shape[0]
    ff_part = after(jnp.concatenate([up_part, down_part], 0), embed_part)
    ff_full = lax.all_gather(ff_part, SLAB, axis=0)
    up_full = ff_full[:, :up_size].reshape(D, class_size)
    down_full = ff_full[:, up_size:].reshape(class_size, D)
    one_spots = [
        (0, None, 0, ("lane", 0, D)),
        (1, None, 0, ("lane", 1, D)),
        (2, None, 0, ("lane", 2, D)),
        (3, None, 1, ("lane", 0, D)),
        (4, None, 2, ("lane", 0, D)),
    ]
    slim_list = [(0, ("lane", k, DEC)) for k in range(8)]
    slim_list += [(1, ("row", k, DEC)) for k in range(first_chunks)]
    slim_list += [(2, ("row", k, DEC)) for k in range(second_chunks)]
    slim_spots = [
        (number // quarter, number % quarter * DEC, target, spot)
        for number, (target, spot) in enumerate(slim_list)
    ]
    lead = (layers, 2, crops)
    none = jnp.zeros((), jnp.bfloat16)
    one_own = flips(pack_one, "crop")
    pixels = jnp.concatenate(pixel_parts, 0)
    pixel_rows = jnp.concatenate(
        [jnp.where(is_mri, none, pixels[:, :ct_size]), jnp.where(is_mri, pixels, none)], 1
    )
    partial = matmul(pixel_rows, embed_full).astype(jnp.bfloat16)
    product = total_of(flips_of(list(partial.reshape(crops, rows_in, D)), "crop"))
    one_other = core_swap(after(one_own, partial))
    triple_full, output_full, vector_full = moves(
        gather_plan(one_spots),
        one_own + one_other,
        [lead + (row_count, 3 * D), lead + (row_count, D), lead + (row_count, D)],
    )
    triple_full = triple_full.reshape(D, 3 * D)
    output_full = output_full.reshape(D, D)
    vector_full = vector_full[:, :, :, 0, :vector_size].transpose(2, 0, 1, 3).reshape(12 * D)
    vector_rows = vector_full.astype(jnp.float32).reshape(12, D)
    embedded = (
        product
        + jnp.where(own_mri, vector_rows[7], vector_rows[6])
        + jnp.concatenate([position_rows] * crop_batch, 0)
    )
    normed_one, pull_one = jax.vjp(layer_norm, embedded, vector_rows[0], vector_rows[1])
    normed_one = normed_one.astype(jnp.bfloat16)
    triple = matmul(normed_one, triple_full).astype(jnp.bfloat16)
    triple = heads_out(triple.reshape(crop_batch, local_tokens, 3 * D), 3)
    query, keys, values = triple[..., :HDIM], triple[..., HDIM : 2 * HDIM], triple[..., 2 * HDIM :]
    scores = (
        jnp.einsum("pqd,pkd->pqk", query, keys, preferred_element_type=jnp.float32) * score_scale
    )
    probs = jax.nn.softmax(scores, axis=-1)
    probs_low = probs.astype(jnp.bfloat16)
    mixed = jnp.einsum("pqk,pkd->pqd", probs_low, values, preferred_element_type=jnp.float32)
    slim_own = flips(pack_slim, "crop")
    mixed = after(mixed.astype(jnp.bfloat16), slim_own)
    mixed = heads_back(mixed, crop_batch, 1)
    slim_other = core_swap(slim_own)
    hidden_one = embedded + matmul(mixed, output_full) + vector_rows[4]
    hidden_one = after(hidden_one, slim_other)
    lift_full, first_full, second_full = moves(
        gather_plan(slim_spots),
        slim_own + slim_other,
        [
            lead + (row_count, 8 * DEC),
            lead + (first_chunks, row_count, DEC),
            lead + (second_chunks, row_count, DEC),
        ],
    )
    lift_full = lift_full.reshape(D, 8 * DEC)
    first_full = slab_trim(first_full, first_count, convolve_one.shape[0])
    second_full = slab_trim(second_full, second_count, convolve_two.shape[0])
    normed_two, pull_two = jax.vjp(layer_norm, hidden_one, vector_rows[2], vector_rows[3])
    normed_two = normed_two.astype(jnp.bfloat16)
    normed_all = jnp.concatenate(flips(normed_two, "crop"), 0)
    bias_class = vector_rows[8:].reshape(slab_count, crops, down_count)
    bias_class = lax.dynamic_index_in_dim(bias_class, own_crop, 1, keepdims=False).reshape(-1)
    inner = matmul(normed_all, up_full) + bias_class
    activated = gelu_exact(inner).astype(jnp.bfloat16)
    partial = matmul(activated, down_full).astype(jnp.bfloat16).reshape(crops, rows_in, D)
    product = total_of(flips_of(list(partial), "crop"))
    hidden_two = hidden_one + product + vector_rows[5]
    hidden_low = hidden_two.astype(jnp.bfloat16)
    volume = to_volume(matmul(hidden_low, lift_full), crop_batch)
    joined = jnp.concatenate([volume.astype(jnp.bfloat16), skip_feats], -1)
    joined = with_planes(joined, neighbours(joined))
    volume_rimmed = with_planes(
        volume, (joined[:, :1, ..., :DEC], joined[:, -1:, ..., :DEC])
    )
    target_rimmed = with_planes(cotangent, neighbours(cotangent)).astype(jnp.float32)
    cols_one = columns(joined)
    conv_one = matmul(cols_one, first_full).reshape(volume.shape)
    conv_one_rimmed = with_planes(conv_one, neighbours(conv_one.astype(jnp.bfloat16)))
    average_a, inverse_a = norm_scales(conv_one, voxel_count)
    normed_a = (conv_one_rimmed - average_a) * inverse_a
    first_act = inside(gelu_exact(normed_a).astype(jnp.bfloat16))
    cols_two = columns(first_act)
    conv_two = matmul(cols_two, second_full).reshape(volume.shape)
    conv_two_rimmed = with_planes(conv_two, neighbours(conv_two.astype(jnp.bfloat16)))
    average_b, inverse_b = norm_scales(conv_two, voxel_count)
    normed_b = (conv_two_rimmed - average_b) * inverse_b
    before = normed_b + volume_rimmed
    block_output = gelu_exact(before[:, 1:-1]).astype(jnp.bfloat16)

    grad_before = target_rimmed * gelu_slope(before)
    mean_b, slope_b = norm_slopes(grad_before[:, 1:-1], normed_b[:, 1:-1], voxel_count)
    grad_conv_two = inverse_b * (grad_before - mean_b - normed_b * slope_b)
    grad_conv_two = inside(grad_conv_two.astype(jnp.bfloat16))
    weight_second = matmul_left_t(cols_two, grad_conv_two[:, 1:-1].reshape(-1, DEC))
    grad_first = back_conv(grad_conv_two, second_full, DEC) * gelu_slope(normed_a[:, 1:-1])
    grad_first_rimmed = with_planes(grad_first, neighbours(grad_first.astype(jnp.bfloat16)))
    mean_a, slope_a = norm_slopes(grad_first, normed_a[:, 1:-1], voxel_count)
    grad_conv_one = inverse_a * (grad_first_rimmed - mean_a - normed_a * slope_a)
    grad_conv_one = inside(grad_conv_one.astype(jnp.bfloat16))
    weight_first = matmul_left_t(cols_one, grad_conv_one[:, 1:-1].reshape(-1, DEC))
    grad_joined = back_conv(grad_conv_one, first_full, 2 * DEC)
    skip_grad = grad_joined[..., DEC:].astype(jnp.bfloat16)
    grad_lifted = to_tokens(grad_before[:, 1:-1] + grad_joined[..., :DEC]).astype(jnp.bfloat16)
    weight_lift = matmul_left_t(hidden_low, grad_lifted)
    grad_hidden = matmul_right_t(grad_lifted, lift_full)
    bias_down = jnp.sum(grad_hidden, 0)
    grad_branch = grad_hidden.astype(jnp.bfloat16)
    grad_all = jnp.concatenate(flips(grad_branch, "crop"), 0)
    grad_inner = matmul_right_t(grad_all, down_full) * gelu_slope(inner)
    bias_up = jnp.sum(grad_inner, 0)
    grad_inner_low = grad_inner.astype(jnp.bfloat16)
    partial = matmul_right_t(grad_inner_low, up_full).astype(jnp.bfloat16)
    partial = partial.reshape(crops, rows_in, D)
    weight_down = matmul_left_t(activated, grad_all).astype(jnp.bfloat16)
    weight_up = matmul_left_t(normed_all, grad_inner_low).astype(jnp.bfloat16)
    ff_grads = jnp.concatenate(
        [weight_up.reshape(slab_count, -1, D), weight_down.reshape(slab_count, -1, D)], 1
    ).reshape(-1, D)

    slim_move = scatter_cores(
        [
            weight_lift.astype(jnp.bfloat16).reshape(lead + (row_count, 8 * DEC)),
            slab_fill(weight_first.astype(jnp.bfloat16), first_count, first_chunks, row_count),
            slab_fill(weight_second.astype(jnp.bfloat16), second_count, second_chunks, row_count),
        ],
        slim_spots,
        slim_chunks,
    )
    slim_parts = core_sum(*slim_move)
    partial = after(partial, slim_move[1])
    back_two = pull_two(total_of(flips_of(list(partial), "crop")))
    grad_hidden = grad_hidden + back_two[0]
    bias_out = jnp.sum(grad_hidden, 0)
    grad_branch = grad_hidden.astype(jnp.bfloat16)
    weight_out = matmul_left_t(mixed, grad_branch)
    grad_mixed = matmul_right_t(grad_branch, output_full).astype(jnp.bfloat16)
    grad_mixed = after(grad_mixed, slim_parts)
    slim_got = flips_of(slim_parts, "crop")
    grad_mixed = heads_out(grad_mixed.reshape(crop_batch, local_tokens, D), 1)
    grad_probs = jnp.einsum(
        "pqd,pkd->pqk", grad_mixed, values, preferred_element_type=jnp.float32
    )
    centre = jnp.sum(probs * grad_probs, -1, keepdims=True)
    grad_scores = (probs * (grad_probs - centre)).astype(jnp.bfloat16)
    grad_query = (
        jnp.einsum("pqk,pkd->pqd", grad_scores, keys, preferred_element_type=jnp.float32)
        * score_scale
    )
    grad_keys = (
        jnp.einsum("pqk,pqd->pkd", grad_scores, query, preferred_element_type=jnp.float32)
        * score_scale
    )
    grad_values = jnp.einsum(
        "pqk,pqd->pkd", probs_low, grad_mixed, preferred_element_type=jnp.float32
    )
    grad_triple = jnp.concatenate([grad_query, grad_keys, grad_values], -1).astype(jnp.bfloat16)
    grad_triple = heads_back(grad_triple, crop_batch, 3)
    grad_triple = after(grad_triple, slim_got)
    ff_grads = after(ff_grads, grad_triple)
    ff_sum = lax.psum_scatter(ff_grads, SLAB, scatter_dimension=0, tiled=True)
    weight_triple = matmul_left_t(normed_one, grad_triple)
    back_one = pull_one(matmul_right_t(grad_triple, triple_full))
    grad_hidden = grad_hidden + back_one[0]
    grad_low = grad_hidden.astype(jnp.bfloat16)

    grad_rows = jnp.concatenate(flips(grad_low, "crop"), 0)
    slim_sum = total_of(after(slim_got, grad_triple)).astype(jnp.bfloat16)
    grad_rows = after(grad_rows, (ff_grads, slim_sum))
    weight_embed = matmul_left_t(pixel_rows, grad_rows).astype(jnp.bfloat16)
    embed_sum = lax.psum_scatter(weight_embed, SLAB, scatter_dimension=0, tiled=True)
    bias_ct = jnp.sum(jnp.where(own_mri, 0.0, grad_hidden), 0)
    bias_mri = jnp.sum(jnp.where(own_mri, grad_hidden, 0.0), 0)
    position_grad = jnp.sum(grad_hidden.reshape(crop_batch, local_tokens, D), 0)
    position_grad = position_grad.astype(jnp.bfloat16).reshape(-1, crops, unit).swapaxes(0, 1)
    position_grad = [
        lax.dynamic_index_in_dim(position_grad, own_crop ^ shift, 0, keepdims=False)
        for shift in range(crops)
    ]
    position_grad = total_of(flips_of(position_grad, "crop"))
    at_class = lax.broadcasted_iota(jnp.int32, (slab_count, crops, down_count), 1) == own_crop
    bias_full = jnp.where(at_class, bias_up.reshape(slab_count, 1, down_count), 0.0)
    vector_grad = jnp.concatenate(
        [
            jnp.stack(
                [
                    back_one[1],
                    back_one[2],
                    back_two[1],
                    back_two[2],
                    bias_out,
                    bias_down,
                    bias_ct,
                    bias_mri,
                ]
            ),
            bias_full.reshape(4, D),
        ],
        0,
    ).astype(jnp.bfloat16)
    vector_pack = vector_grad.reshape(crops, layers, 2, 1, vector_size).transpose(1, 2, 0, 3, 4)
    vector_pack = jnp.pad(
        vector_pack, ((0, 0),) * 3 + ((0, row_count - 1), (0, D - vector_size))
    )
    weight_triple = after(weight_triple.astype(jnp.bfloat16), weight_embed)
    one_parts = core_sum(*scatter_cores(
        [
            weight_triple.reshape(lead + (row_count, 3 * D)),
            weight_out.astype(jnp.bfloat16).reshape(lead + (row_count, D)),
            vector_pack,
        ],
        one_spots,
        5,
    ))
    pixel_grad = matmul_right_t(after(grad_rows, one_parts), embed_full)
    ct_grad = jnp.pad(pixel_grad[:, :ct_size], ((0, 0), (0, (CHANS - 1) * ct_size)))
    pixel_grad = jnp.where(is_mri, pixel_grad[:, ct_size:], ct_grad).astype(jnp.bfloat16)
    slim_all = z_sum(slim_sum, one_parts).reshape(slim_chunks, row_count, 6, DEC)
    slim_all = slim_all.transpose(0, 2, 1, 3).reshape(-1, DEC)
    first_start = 8 * row_count
    second_start = first_start + first_chunks * row_count
    lift_sum = slim_all[:first_start].reshape(8, row_count, DEC).transpose(1, 0, 2)
    lift_sum = lift_sum.reshape(row_count, crops, -1).transpose(1, 0, 2)
    narrow_sum = jnp.concatenate(
        [
            slim_all[first_start : first_start + first_count],
            slim_all[second_start : second_start + second_count],
        ],
        0,
    )
    narrow_sum = narrow_sum.reshape(-1, crops, DEC // crops).transpose(1, 0, 2)
    lift_units, narrow_units = to_units(lift_sum, unit), to_units(narrow_sum, unit)
    up_units = ff_sum[:up_size].reshape(up_rows, crops, per_class).transpose(1, 0, 2)
    up_units = to_units(up_units, unit)
    one_got = flips_of(one_parts, "crop")
    one_got, lift_units, narrow_units, up_units, _ = lax.optimization_barrier(
        (one_got, lift_units, narrow_units, up_units, position_grad)
    )
    one_sum = total_of(one_got).astype(jnp.bfloat16)
    pixel_got = flips_of(
        after(list(pixel_grad.reshape(crops, rows_in, pieces * block)), one_got), "crop"
    )

    def by_units(rows, chunks):
        shaped = rows.reshape(chunks, -1, crops, unit).transpose(0, 2, 1, 3)
        return shaped.reshape(crops, -1, unit)

    def join_units(got, chunks):
        return (
            got.reshape(crops, chunks, -1, unit).transpose(0, 2, 1, 3).reshape(-1, chunks * unit)
        )

    sum_one = z_sum(one_sum).reshape(-1, D)

    wide = jnp.concatenate(
        [
            up_units,
            by_units(ff_sum[up_size:], 1),
            by_units(sum_one[: 3 * row_count], 3),
            by_units(sum_one[3 * row_count : 4 * row_count], 1),
            lift_units,
            narrow_units,
            by_units(embed_sum, 1),
        ],
        1,
    )
    local_sum = jnp.float32(0.0)
    for gradient in (embed_sum, ff_sum, lift_sum, narrow_sum, sum_one, position_grad):
        wide_grad = gradient.astype(jnp.float32)
        local_sum = local_sum + jnp.sum(wide_grad * wide_grad)
    wide = crop_swap(after(wide, local_sum)).astype(jnp.float32)
    norm_crop = total_of(flips(local_sum.reshape(1, 1), "crop"))
    if block % 128 == 0:
        (patch_grad,) = moves(
            column_plan(pieces, block, False), pixel_got, [(rows_in, crops * lanes)]
        )
    else:
        pixel_got = jnp.stack(pixel_got)
        patch_grad = jnp.stack(
            [
                lax.dynamic_index_in_dim(pixel_got, own_crop ^ part, 0, keepdims=False)
                for part in range(crops)
            ]
        )
        patch_grad = patch_grad.reshape(crops, rows_in, pieces, block).transpose(1, 2, 0, 3)
    patch_grad = patch_grad.reshape(patches.shape)
    embed_got = wide[:, -share:]
    embed_grad = (
        embed_got.astype(jnp.float32).reshape(crops, groups, block, unit).transpose(1, 0, 2, 3).reshape(-1, unit)
    )
    marks = []
    edge = 0
    for size in (up_units.shape[1], down_count, 3 * row_count, row_count,
                 lift_units.shape[1], narrow_units.shape[1]):
        marks.append(wide[:, edge : edge + size])
        edge += size
    up_grad = from_units(marks[0], up_rows, per_class)
    up_grad = up_grad.reshape(crops, up_rows, -1, down_count).transpose(1, 2, 0, 3)
    up_grad = up_grad.reshape(expand_up.shape)
    down_grad = join_units(marks[1], 1)
    triple_grad = join_units(marks[2], 3)
    output_grad = join_units(marks[3], 1)
    lift_grad = from_units(marks[4], row_count, 8 * DEC // crops).reshape(upsample.shape)
    narrow_got = from_units(marks[5], first_count + second_count, DEC // crops)
    first_grad = narrow_got[:, :first_count].reshape(-1, DEC // crops)[: convolve_one.shape[0]]
    second_grad = narrow_got[:, first_count:].reshape(-1, DEC // crops)[: convolve_two.shape[0]]
    vector_final = sum_one[4 * row_count, :vector_size].astype(jnp.float32)
    gradients = (
        embed_grad,
        triple_grad,
        output_grad,
        up_grad,
        down_grad,
        lift_grad,
        first_grad,
        second_grad,
        position_grad,
        vector_final,
    )
    grad_norm = jnp.sqrt(slab_sum(norm_crop))[0, 0]
    factor = jnp.minimum(1.0, CLIP / grad_norm)
    news, means, squares = ([], [], [])
    for weight, gradient, mean_old, square_old, step_rate, step_decay in zip(
        shards, gradients, means_in, squares_in, step_rates, step_decays
    ):
        weight_new, mean_new, square_new = adam_update(
            weight, gradient, mean_old, square_old, factor, step_rate, step_decay
        )
        news.append(weight_new)
        means.append(mean_new)
        squares.append(square_new)
    return (
        block_output,
        patch_grad,
        skip_grad,
        grad_norm,
        news[0],
        news[1],
        news[2],
        news[3],
        news[4],
        news[5],
        news[6],
        news[7],
        news[8],
        news[9],
        means[0],
        means[1],
        means[2],
        means[3],
        means[4],
        means[5],
        means[6],
        means[7],
        means[8],
        means[9],
        squares[0],
        squares[1],
        squares[2],
        squares[3],
        squares[4],
        squares[5],
        squares[6],
        squares[7],
        squares[8],
        squares[9],
    )


def solution(mesh):
    crops, slabs = mesh.devices.shape
    mesh = Mesh(mesh.devices.reshape(crops, slabs // 2, 2), ("crop", "z", "core"))
    return jax.shard_map(
        local,
        mesh=mesh,
        in_specs=(
            P("crop", ("z", "core"), None, None),
            P("crop"),
            P("crop", ("z", "core"), None, None, None),
            P("crop", ("z", "core"), None, None, None),
            P(("z", "core"), "crop"),
            P(("z", "core"), "crop"),
            P(("z", "core"), "crop"),
            P(("z", "core"), "crop"),
            P(("z", "core"), "crop"),
            P(("z", "core"), "crop"),
            P(("z", "core"), "crop"),
            P(("z", "core"), "crop"),
            P(("z", "core"), "crop"),
            P(("crop", "z", "core")),
            P(("z", "core"), "crop"),
            P(("z", "core"), "crop"),
            P(("z", "core"), "crop"),
            P(("z", "core"), "crop"),
            P(("z", "core"), "crop"),
            P(("z", "core"), "crop"),
            P(("z", "core"), "crop"),
            P(("z", "core"), "crop"),
            P(("z", "core"), "crop"),
            P(("crop", "z", "core")),
            P(("z", "core"), "crop"),
            P(("z", "core"), "crop"),
            P(("z", "core"), "crop"),
            P(("z", "core"), "crop"),
            P(("z", "core"), "crop"),
            P(("z", "core"), "crop"),
            P(("z", "core"), "crop"),
            P(("z", "core"), "crop"),
            P(("z", "core"), "crop"),
            P(("crop", "z", "core")),
        ),
        out_specs=(
            P("crop", ("z", "core"), None, None, None),
            P("crop", ("z", "core"), None, None),
            P("crop", ("z", "core"), None, None, None),
            P(),
            P(("z", "core"), "crop"),
            P(("z", "core"), "crop"),
            P(("z", "core"), "crop"),
            P(("z", "core"), "crop"),
            P(("z", "core"), "crop"),
            P(("z", "core"), "crop"),
            P(("z", "core"), "crop"),
            P(("z", "core"), "crop"),
            P(("z", "core"), "crop"),
            P(("crop", "z", "core")),
            P(("z", "core"), "crop"),
            P(("z", "core"), "crop"),
            P(("z", "core"), "crop"),
            P(("z", "core"), "crop"),
            P(("z", "core"), "crop"),
            P(("z", "core"), "crop"),
            P(("z", "core"), "crop"),
            P(("z", "core"), "crop"),
            P(("z", "core"), "crop"),
            P(("crop", "z", "core")),
            P(("z", "core"), "crop"),
            P(("z", "core"), "crop"),
            P(("z", "core"), "crop"),
            P(("z", "core"), "crop"),
            P(("z", "core"), "crop"),
            P(("z", "core"), "crop"),
            P(("z", "core"), "crop"),
            P(("z", "core"), "crop"),
            P(("z", "core"), "crop"),
            P(("crop", "z", "core")),
        ),
        check_vma=False,
    )
```
